32 devices in a mesh: grp: 4 (over y, x), seq: 8 (over z, core).
Axes of the slice: x: 2, y: 2, z: 4, core: 2. Of those that a mesh axis runs over, the one named last changes fastest.
Arguments:
- tokens: bfloat16 [12288, 1024], P(('grp', 'seq')), may hold values from -6 to 6
- cotangent: bfloat16 [12288, 1024], P(('grp', 'seq')), may hold values from -6 to 6
- master: float32 [24, 1024, 1024], P('grp', 'seq')
- first_moment: float32 [24, 1024, 1024], P('grp', 'seq')
- second_moment: float32 [24, 1024, 1024], P('grp', 'seq')
- norm_params: float32 [4, 1024], replicated
- norm_first: float32 [4, 1024], replicated
- norm_second: float32 [4, 1024], replicated
- seg_valid: int32 [4, 6], replicated, may hold values from 0 to 512, as said below
- book_of_group: int32 [4], replicated, may hold values from 0 to 3, each once
- panel_slot: int32 [15], replicated, may hold values from 0 to 23, as said below
Outputs:
- mixed: bfloat16 [12288, 1024], P(('grp', 'seq'))
- input_grad: float32 [12288, 1024], P(('grp', 'seq'))
- slot_grad: float32 [24, 1024, 1024], P('grp', 'seq')
- slot_first: float32 [24, 1024, 1024], P('grp', 'seq')
- slot_second: float32 [24, 1024, 1024], P('grp', 'seq')
- slot_weight: float32 [24, 1024, 1024], P('grp', 'seq')
- norm_grad: float32 [4, 1024], replicated
- norm_first_new: float32 [4, 1024], replicated
- norm_second_new: float32 [2, 1024], replicated
- norm_second_after: float32 [2, 1024], replicated
- norm_weight: float32 [4, 1024], replicated
The draws below stay inside these ranges and needn't reach their ends.
Inputs may be any that keep to these rules, and one draw needn't show every extreme that they name: `seg_valid`: each book has 512 valid positions in every segment but its last, which holds more than 512 - min(512, 384) valid positions; one book fills all 6 segments. `panel_slot`: all values differ; at most 6 panels fall in the slots of one group, and one group holds exactly 6.
All inputs are finite; a program needn't handle non-finite values.
Results may differ from the reference program's by a relative error of at most 0.024.
Values may be sent and summed in bfloat16 or wider, within the bound.
A program may use at most 512 MiB of HBM per device.

```python
import jax
import jax.numpy as jnp
from jax import lax

D = 1024
HEADS = 8
HEAD_DIM = 128
FF = 4096
S = 512
CM = 512
TOK_DEV = 384
SLOTS = 6
STEP = 10
PANELS = 15
SEGS = 6
TOKENS = 12288
N_GRP = 4
N_SEQ = 8


def owner_table(key):
    key = jax.random.fold_in(key, 101)
    slot_total = N_GRP * SLOTS
    chosen_group = jax.random.randint(jax.random.fold_in(key, 1), (), 0, N_GRP)
    scores = jax.random.randint(jax.random.fold_in(key, 2), (slot_total,), 0, 1 << 16)
    slot_ids = jnp.arange(slot_total, dtype=jnp.int32)
    favoured = (slot_ids // SLOTS == chosen_group) | (slot_ids == 0) | (slot_ids == slot_total - 1)
    ranked = (scores + jnp.where(favoured, 1 << 20, 0)) * slot_total + slot_ids
    chosen = lax.top_k(ranked, PANELS)[1].astype(jnp.int32)
    shuffle = jax.random.permutation(jax.random.fold_in(key, 3), PANELS)
    return chosen[shuffle]


def panel_grad_sizes():
    hidden_ratio = FF // D
    inner_dev = D ** (-0.5)
    deviations = [inner_dev] * 3 + [(D // (2 * S)) ** (-0.5)] + [inner_dev] * hidden_ratio
    deviations = deviations + [FF ** (-0.5)] * hidden_ratio + [(3 * D) ** (-0.5)] * 3
    grad_sizes = [1.0] * 3 + [0.03] + [0.25] * hidden_ratio + [0.6] * hidden_ratio + [0.8] * 3
    grad_unit = (1.0 * TOKENS) ** 0.5
    return jnp.array(deviations, jnp.float32) * jnp.array(grad_sizes, jnp.float32) * grad_unit


def empty_size():
    return 0.5 * D ** (-0.5) * (1.0 * TOKENS) ** 0.5


def slot_values(table, slot_table, empty_value):
    return jnp.full((N_GRP * SLOTS,), empty_value, jnp.float32).at[slot_table].set(table)


def draw_panel_slot(key, part):
    slot_table = owner_table(key)
    return slot_table


def draw_master(key, part):
    key = jax.random.fold_in(key, 11)
    return jax.random.truncated_normal(key, -6.0, 6.0, (N_GRP * SLOTS, D, D), jnp.float32)


def draw_first_moment(key, part):
    slot_table = owner_table(key)
    key = jax.random.fold_in(key, 12)
    slot_size = slot_values(panel_grad_sizes(), slot_table, empty_size())
    noise = jax.random.truncated_normal(key, -5.0, 5.0, (N_GRP * SLOTS, D, D), jnp.float32)
    return 0.11 * noise * slot_size[:, None, None]


def draw_second_moment(key, part):
    slot_table = owner_table(key)
    key = jax.random.fold_in(key, 13)
    slot_size = slot_values(panel_grad_sizes(), slot_table, empty_size())
    spread = jax.random.uniform(key, (N_GRP * SLOTS, D, D), jnp.float32, jnp.log(0.5), jnp.log(8.0))
    return 0.001 * jnp.exp(spread) * (slot_size * slot_size)[:, None, None]


def draw_norm_params(key, part):
    key = jax.random.fold_in(key, 21)
    noise = jax.random.truncated_normal(key, -5.0, 5.0, (4, D), jnp.float32)
    gain_rows = (jnp.arange(4) % 2 == 0)[:, None]
    return jnp.where(gain_rows, 1.0 + 0.1 * noise, 0.3 * noise)


def norm_sizes():
    return jnp.array([1.7, 1.7, 0.5, 0.5], jnp.float32) * (1.0 * TOKENS) ** 0.5


def draw_norm_first(key, part):
    key = jax.random.fold_in(key, 22)
    noise = jax.random.truncated_normal(key, -5.0, 5.0, (4, D), jnp.float32)
    return 0.11 * noise * norm_sizes()[:, None]


def draw_norm_second(key, part):
    key = jax.random.fold_in(key, 23)
    spread = jax.random.uniform(key, (4, D), jnp.float32, jnp.log(0.5), jnp.log(8.0))
    sizes = norm_sizes()
    return 0.001 * jnp.exp(spread) * (sizes * sizes)[:, None]


def draw_seg_valid(key, part):
    key = jax.random.fold_in(key, 31)
    group_len = SEGS * S
    full_book = jax.random.randint(jax.random.fold_in(key, 1), (), 0, N_GRP)
    trimmed = jax.random.randint(jax.random.fold_in(key, 3), (N_GRP,), 0, min(S, TOK_DEV))
    book_len = group_len - trimmed
    book_len = jnp.where(jnp.arange(N_GRP) == full_book, group_len, book_len)
    starts = S * jnp.arange(SEGS, dtype=jnp.int32)
    return jnp.clip(book_len[:, None] - starts[None, :], 0, S).astype(jnp.int32)


def levels(stream_key, extent, split, smallest, top_value):
    factor_of = 1.0
    for axis_at, blocks in split:
        steps = jax.random.uniform(jax.random.fold_in(jax.random.fold_in(stream_key, 6), axis_at), (blocks,), jnp.float32, smallest / len(split), top_value / len(split))
        factor_of = factor_of * jnp.repeat(jnp.exp(steps), extent[axis_at] // blocks).reshape((-1,) + (1,) * (len(extent) - 1 - axis_at))
    return factor_of


def scatter_about(own_key, extent, width, limit, split=(), kind=jnp.bfloat16):
    values = jax.random.normal(own_key, extent, jnp.float32) * width
    if len(split) > 0:
        values = levels(own_key, extent, split, -0.22, 0.18) * values
    return jnp.clip(values, min=-limit, max=limit).astype(kind)


def setup_inputs(seed: int = 0) -> dict:
    arg_keys = jax.random.split(jax.random.key(seed), 12)
    tokens = scatter_about(arg_keys[0], (TOKENS, D), 1.0, 6.0, ((0, 32),))
    cotangent = scatter_about(arg_keys[1], (TOKENS, D), 1.0, 6.0, ((0, 32),))
    master = draw_master(jax.random.fold_in(arg_keys[11], 71), 0)
    first_moment = draw_first_moment(jax.random.fold_in(arg_keys[11], 71), 0)
    second_moment = draw_second_moment(jax.random.fold_in(arg_keys[11], 71), 0)
    norm_params = draw_norm_params(jax.random.fold_in(arg_keys[11], 71), 0)
    norm_first = draw_norm_first(jax.random.fold_in(arg_keys[11], 71), 0)
    norm_second = draw_norm_second(jax.random.fold_in(arg_keys[11], 71), 0)
    seg_valid = draw_seg_valid(jax.random.fold_in(arg_keys[11], 71), 0)
    book_of_group = jax.random.permutation(arg_keys[9], N_GRP).astype(jnp.int32)
    panel_slot = draw_panel_slot(jax.random.fold_in(arg_keys[11], 71), 0)
    return dict(tokens=tokens, cotangent=cotangent, master=master, first_moment=first_moment, second_moment=second_moment, norm_params=norm_params, norm_first=norm_first, norm_second=norm_second, seg_valid=seg_valid, book_of_group=book_of_group, panel_slot=panel_slot)


@jax.custom_vjp
def low(v):
    return lax.optimization_barrier(v.astype(jnp.bfloat16)).astype(jnp.float32)

@jax.custom_vjp
def low_back(v):
    return v

def low_keep(v):
    return (low(v), None)

def low_pass(kept, grad):
    return (grad,)

def back_keep(v):
    return (v, None)

def back_low(kept, grad):
    return (low(grad),)
low.defvjp(low_keep, low_pass)
low_back.defvjp(back_keep, back_low)
HIGHEST = lax.Precision.HIGHEST
NEG_SCORE = -1e+30
FAR_INDEX = 1 << 30
NORM_EPS = 1e-05
BETA_ONE = 0.9
BETA_TWO = 0.999
WEIGHT_DECAY = 0.1
ADAM_EPS = 1e-08
NORM_RATE = 1.0
SLOT_RATE = 2.0

def rounded(values):
    return low(low_back(values))

def product(left, right):
    return jnp.dot(left, right, precision=HIGHEST, preferred_element_type=jnp.float32)

def layer_norm(values, gain, shift):
    row_mean = lax.optimization_barrier(jnp.mean(values, axis=-1, keepdims=True))
    centered = values - row_mean
    variance = lax.optimization_barrier(jnp.mean(centered * centered, axis=-1, keepdims=True))
    return centered * lax.rsqrt(variance + NORM_EPS) * gain + shift

def panel_deviations():
    inner_dev = D ** (-0.5)
    hidden_ratio = FF // D
    deviations = [inner_dev] * 3 + [(D // (2 * S)) ** (-0.5)] + [inner_dev] * hidden_ratio
    deviations = deviations + [FF ** (-0.5)] * hidden_ratio + [(3 * D) ** (-0.5)] * 3
    return jnp.array(deviations, jnp.float32)

def adam_update(gradient, first_old, second_old, weight_old, step_rate):
    first_new = BETA_ONE * first_old + (1.0 - BETA_ONE) * gradient
    second_new = BETA_TWO * second_old + (1.0 - BETA_TWO) * gradient * gradient
    fix_one = 1.0 - BETA_ONE ** STEP
    fix_two = 1.0 - BETA_TWO ** STEP
    movement = first_new / fix_one / (jnp.sqrt(second_new / fix_two) + ADAM_EPS)
    return (first_new, second_new, weight_old - step_rate * (movement + WEIGHT_DECAY * weight_old))

def group_forward(group_rows, row_mask, weights, norms):
    query_weight, key_weight, value_weight, out_weight, up_weight, down_weight, conv_weight = weights
    group_len = group_rows.shape[0]
    comp_rows = group_len // 3
    normed = low(layer_norm(group_rows, norms[0], norms[1]))
    queries = rounded(product(normed, query_weight))
    keys_raw = rounded(product(normed, key_weight))
    values_raw = rounded(product(normed, value_weight))
    windows = normed[:3 * comp_rows].reshape(comp_rows, 3, D)
    compressed = rounded(jnp.einsum('jtd,tde->je', windows, conv_weight, precision=HIGHEST))
    keys_all = jnp.concatenate([keys_raw, rounded(product(compressed, key_weight))], 0)
    values_all = jnp.concatenate([values_raw, rounded(product(compressed, value_weight))], 0)
    keys_all = keys_all.reshape(-1, HEADS, HEAD_DIM)
    values_all = values_all.reshape(-1, HEADS, HEAD_DIM)
    raw_mark = jnp.concatenate([jnp.arange(group_len, dtype=jnp.int32), jnp.full((comp_rows,), -FAR_INDEX, jnp.int32)])
    comp_mark = jnp.concatenate([jnp.full((group_len,), -FAR_INDEX, jnp.int32), jnp.arange(comp_rows, dtype=jnp.int32)])
    score_scale = HEAD_DIM ** (-0.5)

    def segment_block(segment):
        seg_first = segment * S
        block_queries = lax.dynamic_slice_in_dim(queries, seg_first, S, 0).reshape(S, HEADS, HEAD_DIM)
        positions = seg_first + jnp.arange(S, dtype=jnp.int32)
        memory_start = seg_first - S
        comp_end = jnp.floor_divide(memory_start, 3)
        comp_start = jnp.maximum(comp_end - CM, 0)
        raw_ok = (raw_mark[None, :] >= memory_start) & (raw_mark[None, :] <= positions[:, None]) & (raw_mark[None, :] >= 0)
        comp_ok = (comp_mark >= comp_start) & (comp_mark < comp_end)
        allowed = raw_ok | comp_ok[None, :]
        scores = low_back(jnp.einsum('qhd,khd->hqk', block_queries, keys_all, precision=HIGHEST) * score_scale)
        scores = jnp.where(allowed[None], scores, NEG_SCORE)
        probs = low(jax.nn.softmax(scores, axis=-1))
        return jnp.einsum('hqk,khd->qhd', probs, values_all, precision=HIGHEST).reshape(S, D)
    attended = lax.map(jax.checkpoint(segment_block), jnp.arange(group_len // S, dtype=jnp.int32))
    attended = rounded(attended.reshape(group_len, D))
    hidden = group_rows + low_back(product(attended, out_weight))
    normed_two = low(layer_norm(hidden, norms[2], norms[3]))
    pre_act = low_back(product(normed_two, up_weight.T))
    active = low(jax.nn.gelu(pre_act))
    output = hidden + low_back(product(active, down_weight))
    return output * row_mask[:, None]

def reference(tokens, cotangent, master, first_moment, second_moment, norm_params, norm_first, norm_second, seg_valid, book_of_group, panel_slot):
    group_len = N_SEQ * TOK_DEV
    hidden_ratio = FF // D
    inputs = tokens.astype(jnp.float32).reshape(N_GRP, group_len, D)
    counts = seg_valid[book_of_group]
    positions = jnp.arange(group_len, dtype=jnp.int32)
    row_masks = ((positions % S)[None, :] < jnp.repeat(counts, S, axis=1)).astype(jnp.float32)
    deviations = panel_deviations()

    def forward(slots_full, norms, rows_all):

        def select_panel(panel_index):
            return low(deviations[panel_index] * slots_full[panel_slot[panel_index]])
        weights = (select_panel(0), select_panel(1), select_panel(2), select_panel(3), jnp.concatenate([select_panel(4 + piece_index) for piece_index in range(hidden_ratio)], 0), jnp.concatenate([select_panel(4 + hidden_ratio + piece_index) for piece_index in range(hidden_ratio)], 0), jnp.stack([select_panel(4 + 2 * hidden_ratio + tap_index) for tap_index in range(3)], 0))

        def one_group(group_pair):
            return group_forward(group_pair[0], group_pair[1], weights, norms)
        return lax.map(jax.checkpoint(one_group), (rows_all, row_masks))
    outputs, pullback = jax.vjp(forward, master, norm_params, inputs)
    slot_grad, norm_grad, input_grad = pullback(cotangent.astype(jnp.float32).reshape(N_GRP, group_len, D))
    slot_first, slot_second, slot_weight = adam_update(slot_grad, first_moment, second_moment, master, SLOT_RATE)
    norm_first_new, norm_second_all, norm_weight = adam_update(norm_grad, norm_first, norm_second, norm_params, NORM_RATE)
    return (outputs.reshape(N_GRP * group_len, D).astype(jnp.bfloat16), input_grad.reshape(N_GRP * group_len, D), slot_grad, slot_first, slot_second, slot_weight, norm_grad, norm_first_new, norm_second_all[:2], norm_second_all[2:], norm_weight)
```

```python
import functools

import jax
import jax.numpy as jnp
from jax import lax
from jax.experimental import pallas as pl
from jax.experimental.pallas import tpu as pltpu
from jax.sharding import PartitionSpec as P

D = 1024
HEADS = 8
HEAD_DIM = 128
FF = 4096
S = 512
CM = 512
STEP = 10
PANELS = 15
RATIO = FF // D
QB = 128
RAW_KEYS = 2 * S
COMP_KEYS = CM + QB
MIB = 1 << 20

NEG_SCORE = -1e30
NORM_EPS = 1e-05
BETA_ONE = 0.9
BETA_TWO = 0.999
WEIGHT_DECAY = 0.1
ADAM_EPS = 1e-08
NORM_RATE = 1.0
SLOT_RATE = 2.0
BF16 = jnp.bfloat16
F32 = jnp.float32
MESH = pl.DeviceIdType.MESH


def layer_norm(values, gain, shift):
    row_mean = jnp.mean(values, axis=-1, keepdims=True)
    centered = values - row_mean
    variance = jnp.mean(centered * centered, axis=-1, keepdims=True)
    return centered * lax.rsqrt(variance + NORM_EPS) * gain + shift


def panel_deviations():
    inner_dev = D ** (-0.5)
    deviations = [inner_dev] * 3 + [(D // (2 * S)) ** (-0.5)] + [inner_dev] * RATIO
    deviations = deviations + [FF ** (-0.5)] * RATIO + [(3 * D) ** (-0.5)] * 3
    return jnp.array(deviations, F32)


def adam_update(gradient, first_old, second_old, weight_old, step_rate):
    first_new = BETA_ONE * first_old + (1.0 - BETA_ONE) * gradient
    second_new = BETA_TWO * second_old + (1.0 - BETA_TWO) * gradient * gradient
    fix_one = 1.0 - BETA_ONE**STEP
    fix_two = 1.0 - BETA_TWO**STEP
    movement = first_new / fix_one / (jnp.sqrt(second_new / fix_two) + ADAM_EPS)
    return (first_new, second_new, weight_old - step_rate * (movement + WEIGHT_DECAY * weight_old))


def matmul(left, right):
    return jnp.dot(left, right, preferred_element_type=F32)


def times_transposed(left, right):
    return lax.dot_general(left, right, (((1,), (1,)), ((), ())), preferred_element_type=F32)


def contract_rows(left, right):
    return lax.dot_general(left, right, (((0,), (0,)), ((), ())), preferred_element_type=F32)


class Place:
    def __init__(self, lines):
        self.lines = lines
        self.grp = lax.axis_index("grp")
        self.seq = lax.axis_index("seq")
        self.line = self.seq // 2
        self.core = self.seq % 2
        self.row = self.grp // 2
        self.col = self.grp % 2
        self.grp_x = self.row * 2 + 1 - self.col
        self.grp_y = (1 - self.row) * 2 + self.col
        self.x_dev = {"grp": self.grp_x, "seq": self.seq}
        self.y_dev = {"grp": self.grp_y, "seq": self.seq}
        self.core_dev = {"grp": self.grp, "seq": self.line * 2 + 1 - self.core}

    def other_line(self, k):
        return lax.rem(self.line + k, self.lines)

    def line_dev(self, k):
        return {"grp": self.grp, "seq": self.other_line(k) * 2 + self.core}

    def enter(self):
        barrier = pltpu.get_barrier_semaphore()
        partners = [self.line_dev(k) for k in range(1, self.lines)]
        partners = partners + [self.x_dev, self.y_dev, self.core_dev]
        for device in partners:
            pl.semaphore_signal(barrier, inc=1, device_id=device, device_id_type=MESH)
        pl.semaphore_wait(barrier, self.lines + 2)


def remote(src, dst, send, recv, device):
    return pltpu.make_async_remote_copy(
        src_ref=src,
        dst_ref=dst,
        send_sem=send,
        recv_sem=recv,
        device_id=device,
        device_id_type=MESH,
    )


def gather_kernel(panels, lines, ahead, block_ref, full_ref, own_sem, zs, zr, s1, r1, s2, r2, cs, cr):
    at = Place(lines)
    wide = block_ref.shape[-1]

    def cols(g):
        return pl.ds(pl.multiple_of(g * wide, wide), wide)

    def line_copy(p, k):
        dst = full_ref.at[p, at.line // 2, at.line % 2, at.core, :, cols(at.grp)]
        return remote(block_ref.at[p], dst, zs.at[p, k], zr.at[p, at.line], at.line_dev(k))

    def line_arrival(p, k):
        z = at.other_line(k)
        dst = full_ref.at[p, z // 2, z % 2, at.core, :, cols(at.grp)]
        return remote(block_ref.at[p], dst, zs.at[p, k], zr.at[p, z], at.line_dev(k))

    def part(p, h, g):
        return full_ref.at[p, :, h, at.core, :, cols(g)]

    def first(p, h, g):
        device = at.x_dev if h == 0 else at.y_dev
        return remote(part(p, h, g), part(p, h, g), s1.at[p, h], r1.at[p, h], device)

    def second(p, h, j, g):
        device = at.y_dev if h == 0 else at.x_dev
        return remote(part(p, h, g), part(p, h, g), s2.at[p, h, j], r2.at[p, h, j], device)

    def cross(p, h, core):
        ref = full_ref.at[p, :, h, core]
        return remote(ref, ref, cs.at[p, h], cr.at[p, h], at.core_dev)

    def start_lines(p):
        for k in range(1, lines):
            line_copy(p, k).start()

    def start_first(p):
        for k in range(1, lines):
            line_arrival(p, k).wait_recv()
        for h in (0, 1):
            first(p, h, at.grp).start()

    def start_second(p):
        for h in (0, 1):
            near = at.grp_x if h == 0 else at.grp_y
            first(p, h, near).wait_recv()
            second(p, h, 0, at.grp).start()
            second(p, h, 1, near).start()

    def start_cross(p):
        for h in (0, 1):
            second(p, h, 0, at.grp_y if h == 0 else at.grp_x).wait_recv()
            second(p, h, 1, 3 - at.grp).wait_recv()
            cross(p, h, at.core).start()

    def finish(p):
        for h in (0, 1):
            cross(p, h, 1 - at.core).wait_recv()
            first(p, h, at.grp).wait_send()
            second(p, h, 0, at.grp).wait_send()
            second(p, h, 1, at.grp_x if h == 0 else at.grp_y).wait_send()
            cross(p, h, at.core).wait_send()
        for k in range(1, lines):
            line_copy(p, k).wait_send()

    at.enter()
    own_place = full_ref.at[:, at.line // 2, at.line % 2, at.core, :, cols(at.grp)]
    own = pltpu.make_async_copy(block_ref, own_place, own_sem)
    own.start()
    for p in range(ahead):
        start_lines(p)
    own.wait()

    def step(t, carry):
        @pl.when(t + ahead < panels)
        def _():
            start_lines(t + ahead)

        @pl.when(t < panels)
        def _():
            start_first(t)

        @pl.when((t >= 1) & (t < panels + 1))
        def _():
            start_second(t - 1)

        @pl.when((t >= 2) & (t < panels + 2))
        def _():
            start_cross(t - 2)

        @pl.when(t >= 3)
        def _():
            finish(t - 3)

        return carry

    lax.fori_loop(0, panels + 3, step, 0)


def gather_panels(block, lines):
    panels, rows, wide = block.shape
    dma = pltpu.SemaphoreType.DMA
    full = pl.pallas_call(
        functools.partial(gather_kernel, panels, lines, 3),
        out_shape=jax.ShapeDtypeStruct((panels, lines // 2, 2, 2, rows, 4 * wide), BF16),
        in_specs=[pl.BlockSpec(memory_space=pl.ANY)],
        out_specs=pl.BlockSpec(memory_space=pl.ANY),
        scratch_shapes=[
            dma(()),
            dma((panels, lines)),
            dma((panels, lines)),
            dma((panels, 2)),
            dma((panels, 2)),
            dma((panels, 2, 2)),
            dma((panels, 2, 2)),
            dma((panels, 2)),
            dma((panels, 2)),
        ],
        compiler_params=pltpu.CompilerParams(collective_id=0, has_side_effects=True),
        name="gather_panels",
    )(block)
    return full.reshape(panels, D, D)


def reduce_kernel(
    panels, lines, grad_ref, out_ref, own, cross_in, first_in, second_in, line_in,
    own_sem, cs, cr, s1, r1, s2, r2, zs, zr,
):
    at = Place(lines)
    wide = out_ref.shape[-1]
    pairs = lines // 2

    def cols(g):
        return pl.ds(g * wide, wide)

    def load(p, g):
        src = grad_ref.at[p, :, :, at.core, :, cols(g)]
        return pltpu.make_async_copy(src, own.at[p, :, :, g // 2, g % 2], own_sem.at[p, g])

    def cross(p, g):
        src = grad_ref.at[p, :, :, 1 - at.core, :, cols(g)]
        dst = cross_in.at[p, :, :, g // 2, g % 2]
        return remote(src, dst, cs.at[p, g], cr.at[p, g], at.core_dev)

    def first(p, h):
        if h == 0:
            src = own.at[p, :, 0, 1 - at.row]
            return remote(src, first_in.at[p, 0], s1.at[p, 0], r1.at[p, 0], at.y_dev)
        src = own.at[p, :, 1, :, 1 - at.col]
        return remote(src, first_in.at[p, 1], s1.at[p, 1], r1.at[p, 1], at.x_dev)

    def second(p, h):
        if h == 0:
            src = own.at[p, :, 0, at.row, 1 - at.col]
            return remote(src, second_in.at[p, 0], s2.at[p, 0], r2.at[p, 0], at.x_dev)
        src = own.at[p, :, 1, 1 - at.row, at.col]
        return remote(src, second_in.at[p, 1], s2.at[p, 1], r2.at[p, 1], at.y_dev)

    def line_copy(p, k):
        z = at.other_line(k)
        src = own.at[p, z // 2, z % 2, at.row, at.col]
        return remote(src, line_in.at[p, at.line], zs.at[p, k], zr.at[p, at.line], at.line_dev(k))

    def line_arrival(p, k):
        z = at.other_line(k)
        src = own.at[p, z // 2, z % 2, at.row, at.col]
        return remote(src, line_in.at[p, z], zs.at[p, k], zr.at[p, z], at.line_dev(k))

    def add(dst, src):
        dst[...] = (dst[...].astype(F32) + src[...].astype(F32)).astype(BF16)

    def start(p):
        for g in range(4):
            cross(p, g).start()
            load(p, g).start()

    def start_first(p):
        for g in range(4):
            cross(p, g).wait_recv()
            load(p, g).wait()
        for h in (0, 1):
            for i in range(pairs):
                for g in range(4):
                    add(own.at[p, i, h, g // 2, g % 2], cross_in.at[p, i, h, g // 2, g % 2])
            first(p, h).start()

    def start_second(p):
        for h in (0, 1):
            first(p, h).wait_recv()
            for i in range(pairs):
                for j in (0, 1):
                    row, col = (at.row, j) if h == 0 else (j, at.col)
                    add(own.at[p, i, h, row, col], first_in.at[p, h, i, j])
            second(p, h).start()

    def start_lines(p):
        for h in (0, 1):
            second(p, h).wait_recv()
            for i in range(pairs):
                add(own.at[p, i, h, at.row, at.col], second_in.at[p, h, i])
        for k in range(1, lines):
            line_copy(p, k).start()

    def finish(p):
        total = own[p, at.line // 2, at.line % 2, at.row, at.col].astype(F32)
        for k in range(1, lines):
            line_arrival(p, k).wait_recv()
            total = total + line_in[p, at.other_line(k)].astype(F32)
        out_ref[p] = total.astype(BF16)
        for h in (0, 1):
            first(p, h).wait_send()
            second(p, h).wait_send()
        for g in range(4):
            cross(p, g).wait_send()
        for k in range(1, lines):
            line_copy(p, k).wait_send()

    at.enter()
    start(0)

    def step(t, carry):
        @pl.when(t + 1 < panels)
        def _():
            start(t + 1)

        @pl.when(t < panels)
        def _():
            start_first(t)

        @pl.when((t >= 1) & (t < panels + 1))
        def _():
            start_second(t - 1)

        @pl.when((t >= 2) & (t < panels + 2))
        def _():
            start_lines(t - 2)

        @pl.when(t >= 3)
        def _():
            finish(t - 3)

        return carry

    lax.fori_loop(0, panels + 3, step, 0)


def reduce_panels(grads, lines):
    panels = grads.shape[0]
    rows, wide, pairs = D // (2 * lines), D // 4, lines // 2
    dma = pltpu.SemaphoreType.DMA
    return pl.pallas_call(
        functools.partial(reduce_kernel, panels, lines),
        out_shape=jax.ShapeDtypeStruct((panels, rows, wide), BF16),
        in_specs=[pl.BlockSpec(memory_space=pl.ANY)],
        out_specs=pl.BlockSpec(memory_space=pltpu.VMEM),
        scratch_shapes=[
            pltpu.VMEM((panels, pairs, 2, 2, 2, rows, wide), BF16),
            pltpu.VMEM((panels, pairs, 2, 2, 2, rows, wide), BF16),
            pltpu.VMEM((panels, 2, pairs, 2, rows, wide), BF16),
            pltpu.VMEM((panels, 2, pairs, rows, wide), BF16),
            pltpu.VMEM((panels, lines, rows, wide), BF16),
            dma((panels, 4)),
            dma((panels, 4)),
            dma((panels, 4)),
            dma((panels, 2)),
            dma((panels, 2)),
            dma((panels, 2)),
            dma((panels, 2)),
            dma((panels, lines)),
            dma((panels, lines)),
        ],
        compiler_params=pltpu.CompilerParams(
            collective_id=1, has_side_effects=True, vmem_limit_bytes=56 * MIB
        ),
        name="reduce_panels",
    )(grads.reshape(panels, pairs, 2, 2, rows, D))


def key_window(seq, tok_dev):
    first_pos = seq * tok_dev
    memory = (first_pos // S - 1) * S
    raw_first = seq - (RAW_KEYS - QB + tok_dev - 1) // tok_dev
    comp_first = jnp.maximum(jnp.floor_divide(memory - 3 * CM, tok_dev), 0)
    return raw_first, comp_first


def block_window(seq, i, tok_dev, raw_rows, comp_rows):
    position = seq * tok_dev + i * QB
    memory = (position // S - 1) * S
    raw_first, comp_first = key_window(seq, tok_dev)
    raw_base = raw_first * tok_dev
    raw_at = jnp.minimum(memory - raw_base, raw_rows - RAW_KEYS)
    comp_end = jnp.floor_divide(memory, 3)
    comp_low = jnp.maximum(comp_end - CM, 0)
    comp_base = comp_first * (tok_dev // 3)
    comp_at = jnp.clip((comp_low - comp_base) // QB * QB, 0, comp_rows - COMP_KEYS)
    return (
        position,
        pl.multiple_of(raw_at, QB),
        pl.multiple_of(comp_at, QB),
        raw_base + raw_at,
        comp_base + comp_at,
        memory,
        comp_low,
        comp_end,
    )


def attend_kernel(tok_dev, q_ref, kr_ref, vr_ref, kc_ref, vc_ref, o_ref, lse_ref):
    seq = lax.axis_index("seq")
    scale = HEAD_DIM ** (-0.5)
    for i in range(tok_dev // QB):
        pos, raw_at, comp_at, raw_pos, comp_pos, memory, comp_low, comp_end = block_window(
            seq, i, tok_dev, kr_ref.shape[0], kc_ref.shape[0]
        )
        q = q_ref[pl.ds(i * QB, QB), :]
        raw = times_transposed(q, kr_ref[pl.ds(raw_at, RAW_KEYS), :]) * scale
        key_pos = raw_pos + lax.broadcasted_iota(jnp.int32, (QB, RAW_KEYS), 1)
        query_pos = pos + lax.broadcasted_iota(jnp.int32, (QB, RAW_KEYS), 0)
        seen = (key_pos >= jnp.maximum(memory, 0)) & (key_pos <= query_pos)
        raw = jnp.where(seen, raw, NEG_SCORE)
        comp = times_transposed(q, kc_ref[pl.ds(comp_at, COMP_KEYS), :]) * scale
        comp_idx = comp_pos + lax.broadcasted_iota(jnp.int32, (QB, COMP_KEYS), 1)
        comp = jnp.where((comp_idx >= comp_low) & (comp_idx < comp_end), comp, NEG_SCORE)
        top = jnp.maximum(
            jnp.max(raw, axis=1, keepdims=True), jnp.max(comp, axis=1, keepdims=True)
        )
        raw = jnp.exp(raw - top)
        comp = jnp.exp(comp - top)
        total = jnp.sum(raw, axis=1, keepdims=True) + jnp.sum(comp, axis=1, keepdims=True)
        out = matmul(raw.astype(BF16), vr_ref[pl.ds(raw_at, RAW_KEYS), :])
        out = out + matmul(comp.astype(BF16), vc_ref[pl.ds(comp_at, COMP_KEYS), :])
        o_ref[pl.ds(i * QB, QB), :] = out / total
        lse = jnp.broadcast_to(top + jnp.log(total), (QB, QB))
        lse_ref[0, :, pl.ds(i * QB, QB)] = lse.T[:8]


def attend(q, kr, vr, kc, vc):
    tok_dev = q.shape[0]

    def head(rows):
        return pl.BlockSpec((rows, HEAD_DIM), lambda h: (0, h))

    return pl.pallas_call(
        functools.partial(attend_kernel, tok_dev),
        grid=(HEADS,),
        in_specs=[head(x.shape[0]) for x in (q, kr, vr, kc, vc)],
        out_specs=[head(tok_dev), pl.BlockSpec((1, 8, tok_dev), lambda h: (h, 0, 0))],
        out_shape=[
            jax.ShapeDtypeStruct((tok_dev, D), F32),
            jax.ShapeDtypeStruct((HEADS, 8, tok_dev), F32),
        ],
        compiler_params=pltpu.CompilerParams(vmem_limit_bytes=32 * MIB),
        name="attend",
    )(q, kr, vr, kc, vc)


def attend_back_kernel(
    tok_dev, q_ref, kr_ref, vr_ref, kc_ref, vc_ref, do_ref, lse_ref, delta_ref,
    dq_ref, dkr_ref, dvr_ref, dkc_ref, dvc_ref, acc_kr, acc_vr, acc_kc, acc_vc,
):
    seq = lax.axis_index("seq")
    scale = HEAD_DIM ** (-0.5)
    for acc in (acc_kr, acc_vr, acc_kc, acc_vc):
        acc[...] = jnp.zeros_like(acc)
    for i in range(tok_dev // QB):
        pos, raw_at, comp_at, raw_pos, comp_pos, memory, comp_low, comp_end = block_window(
            seq, i, tok_dev, kr_ref.shape[0], kc_ref.shape[0]
        )
        rows = pl.ds(i * QB, QB)
        q = q_ref[rows, :]
        do = do_ref[rows, :]
        lse = lse_ref[0, 0:1, rows]
        delta = delta_ref[0, 0:1, rows]

        def part(k_ref, v_ref, acc_k, acc_v, keys, seen):
            k = k_ref[keys, :]
            s = times_transposed(k, q) * scale
            p = jnp.where(seen, jnp.exp(jnp.where(seen, s, NEG_SCORE) - lse), 0.0)
            dp = times_transposed(v_ref[keys, :], do)
            ds = (p * (dp - delta)).astype(BF16)
            acc_v[keys, :] += matmul(p.astype(BF16), do)
            acc_k[keys, :] += matmul(ds, q)
            return contract_rows(ds, k)

        key_pos = raw_pos + lax.broadcasted_iota(jnp.int32, (RAW_KEYS, QB), 0)
        query_pos = pos + lax.broadcasted_iota(jnp.int32, (RAW_KEYS, QB), 1)
        seen = (key_pos >= jnp.maximum(memory, 0)) & (key_pos <= query_pos)
        dq = part(kr_ref, vr_ref, acc_kr, acc_vr, pl.ds(raw_at, RAW_KEYS), seen)
        comp_idx = comp_pos + lax.broadcasted_iota(jnp.int32, (COMP_KEYS, QB), 0)
        seen = (comp_idx >= comp_low) & (comp_idx < comp_end)
        dq = dq + part(kc_ref, vc_ref, acc_kc, acc_vc, pl.ds(comp_at, COMP_KEYS), seen)
        dq_ref[rows, :] = (dq * scale).astype(BF16)
    dkr_ref[...] = (acc_kr[...] * scale).astype(BF16)
    dkc_ref[...] = (acc_kc[...] * scale).astype(BF16)
    dvr_ref[...] = acc_vr[...].astype(BF16)
    dvc_ref[...] = acc_vc[...].astype(BF16)


def attend_back(q, kr, vr, kc, vc, do, lse, delta):
    tok_dev, raw_rows, comp_rows = q.shape[0], kr.shape[0], kc.shape[0]

    def head(rows):
        return pl.BlockSpec((rows, HEAD_DIM), lambda h: (0, h))

    stat = pl.BlockSpec((1, 8, tok_dev), lambda h: (h, 0, 0))
    outs = [tok_dev, raw_rows, raw_rows, comp_rows, comp_rows]
    return pl.pallas_call(
        functools.partial(attend_back_kernel, tok_dev),
        grid=(HEADS,),
        in_specs=[head(x.shape[0]) for x in (q, kr, vr, kc, vc, do)] + [stat, stat],
        out_specs=[head(rows) for rows in outs],
        out_shape=[jax.ShapeDtypeStruct((rows, D), BF16) for rows in outs],
        scratch_shapes=[
            pltpu.VMEM((raw_rows, HEAD_DIM), F32),
            pltpu.VMEM((raw_rows, HEAD_DIM), F32),
            pltpu.VMEM((comp_rows, HEAD_DIM), F32),
            pltpu.VMEM((comp_rows, HEAD_DIM), F32),
        ],
        compiler_params=pltpu.CompilerParams(vmem_limit_bytes=40 * MIB),
        name="attend_back",
    )(q, kr, vr, kc, vc, do, lse, delta)


def local(
    tokens, cotangent, master, first_moment, second_moment, norm_params, norm_first, norm_second,
    seg_valid, book_of_group, panel_slot,
):
    seq_count = lax.axis_size("seq")
    group_count = lax.axis_size("grp")
    seq_index = lax.axis_index("seq")
    group_index = lax.axis_index("grp")
    lines = seq_count // 2
    tok_dev = tokens.shape[0]
    slot_count, slot_rows = master.shape[0], master.shape[1]
    all_slots = slot_count * group_count
    comp_dev = tok_dev // 3
    wide = D // group_count

    slot_ids = jnp.arange(all_slots, dtype=jnp.int32)
    is_panel = panel_slot[None, :] == slot_ids[:, None]
    slot_used = jnp.any(is_panel, 1)
    slot_panel = jnp.argmax(is_panel, 1).astype(jnp.int32)
    scale_all = jnp.sum(jnp.where(is_panel, panel_deviations()[None, :], 0.0), 1)
    slot_scale = lax.dynamic_slice_in_dim(scale_all, group_index * slot_count, slot_count, 0)
    scaled = (master * slot_scale[:, None, None]).astype(BF16)
    scaled = scaled.reshape(slot_count, slot_rows, group_count, wide).transpose(2, 0, 1, 3)
    slots_in = lax.all_to_all(scaled, "grp", 0, 0, tiled=True)
    block = slots_in.reshape(all_slots, slot_rows, wide)[panel_slot]
    weights = gather_panels(block, lines)
    query_weight, key_weight, value_weight, out_weight = [weights[i] for i in range(4)]
    up_weight = weights[4 : 4 + RATIO].reshape(FF, D)
    down_weight = weights[4 + RATIO : 4 + 2 * RATIO].reshape(FF, D)
    conv_weight = weights[4 + 2 * RATIO :]

    positions = seq_index * tok_dev + jnp.arange(tok_dev, dtype=jnp.int32)
    book_id = jnp.sum(jnp.where(jnp.arange(group_count) == group_index, book_of_group, 0))
    book_counts = jnp.sum(jnp.where((jnp.arange(group_count) == book_id)[:, None], seg_valid, 0), 0)
    segments = seg_valid.shape[1]
    row_counts = jnp.sum(
        jnp.where((positions // S)[:, None] == jnp.arange(segments)[None, :], book_counts[None, :], 0), 1
    )
    row_valid = (positions % S < row_counts).astype(F32)

    raw_first, comp_first = key_window(seq_index, tok_dev)
    raw_devs = (RAW_KEYS - QB + tok_dev - 1) // tok_dev + 1
    comp_devs = min((3 * CM + S) // tok_dev + 1, seq_count)
    all_tokens = lax.all_gather(tokens, "seq", axis=0, tiled=True)
    padded = jnp.concatenate([jnp.zeros(((raw_devs - 1) * tok_dev, D), BF16), all_tokens], 0)
    raw_tokens = lax.dynamic_slice_in_dim(padded, seq_index * tok_dev, raw_devs * tok_dev, 0)
    comp_tokens = lax.dynamic_slice_in_dim(all_tokens, comp_first * tok_dev, comp_devs * tok_dev, 0)

    def first_norm(rows):
        return layer_norm(rows.astype(F32), norm_params[0], norm_params[1]).astype(BF16)

    inputs = tokens.astype(F32)
    normed = first_norm(tokens)
    normed_raw = first_norm(raw_tokens)
    normed_comp = first_norm(comp_tokens).reshape(comp_devs * comp_dev, 3 * D)
    compressed = matmul(normed_comp, conv_weight.reshape(3 * D, D)).astype(BF16)
    queries = matmul(normed, query_weight).astype(BF16)
    keys_raw = matmul(normed_raw, key_weight).astype(BF16)
    values_raw = matmul(normed_raw, value_weight).astype(BF16)
    keys_comp = matmul(compressed, key_weight).astype(BF16)
    values_comp = matmul(compressed, value_weight).astype(BF16)
    attended_sum, log_total = attend(queries, keys_raw, values_raw, keys_comp, values_comp)
    attended = attended_sum.astype(BF16)

    hidden = inputs + matmul(attended, out_weight)
    normed_two = layer_norm(hidden, norm_params[2], norm_params[3]).astype(BF16)
    pre_act = times_transposed(normed_two, up_weight)
    active = jax.nn.gelu(pre_act).astype(BF16)
    output = hidden + matmul(active, down_weight)
    mixed = (output * row_valid[:, None]).astype(BF16)
    grad_out = cotangent.astype(F32) * row_valid[:, None]
    grad_out_low = grad_out.astype(BF16)
    grad_active = times_transposed(grad_out_low, down_weight)
    gelu_value, gelu_back = jax.vjp(jax.nn.gelu, pre_act)
    grad_pre = gelu_back(grad_active)[0].astype(BF16)
    grad_normed_two = matmul(grad_pre, up_weight)
    norm_value, norm_two_back = jax.vjp(layer_norm, hidden, norm_params[2], norm_params[3])
    grad_hidden_norm, grad_gain_two, grad_shift_two = norm_two_back(grad_normed_two)
    grad_hidden = grad_out + grad_hidden_norm
    grad_branch = grad_hidden.astype(BF16)
    grad_attended = times_transposed(grad_branch, out_weight).astype(BF16)
    delta = jnp.sum(
        (grad_attended.astype(F32) * attended_sum).reshape(tok_dev, HEADS, HEAD_DIM), -1
    ).T
    delta = jnp.broadcast_to(delta[:, None, :], (HEADS, 8, tok_dev))
    grad_queries, dkr, dvr, dkc, dvc = attend_back(
        queries, keys_raw, values_raw, keys_comp, values_comp, grad_attended, log_total, delta
    )

    grad_comp = (times_transposed(dkc, key_weight) + times_transposed(dvc, value_weight)).astype(BF16)
    placed = lax.dynamic_update_slice_in_dim(
        jnp.zeros((seq_count * comp_dev, D), BF16), grad_comp, comp_first * comp_dev, 0
    )
    grad_compressed = lax.psum_scatter(placed, "seq", scatter_dimension=0, tiled=True)
    grad_raw = times_transposed(dkr, key_weight) + times_transposed(dvr, value_weight)
    grad_normed = grad_raw[(raw_devs - 1) * tok_dev :]
    for back in range(1, raw_devs):
        rows = grad_raw[(raw_devs - 1 - back) * tok_dev : (raw_devs - back) * tok_dev].astype(BF16)
        pairs = [(s, s - back) for s in range(back, seq_count)]
        grad_normed = grad_normed + lax.ppermute(rows, "seq", pairs).astype(F32)
    grad_normed = grad_normed + times_transposed(grad_queries, query_weight)
    grad_windows = times_transposed(grad_compressed, conv_weight.reshape(3 * D, D))
    grad_normed = grad_normed + grad_windows.reshape(tok_dev, D)
    norm_value_one, norm_one_back = jax.vjp(layer_norm, inputs, norm_params[0], norm_params[1])
    grad_inputs_norm, grad_gain_one, grad_shift_one = norm_one_back(grad_normed)
    input_grad = grad_hidden + grad_inputs_norm
    norm_local = jnp.stack([grad_gain_one, grad_shift_one, grad_gain_two, grad_shift_two], 0)
    norm_grad = lax.psum(norm_local, ("grp", "seq"))

    windows = normed.reshape(comp_dev, 3, D)
    grads = [
        contract_rows(normed, grad_queries),
        contract_rows(normed_raw, dkr) + contract_rows(compressed, dkc),
        contract_rows(normed_raw, dvr) + contract_rows(compressed, dvc),
        contract_rows(attended, grad_branch),
    ]
    grads = grads + [contract_rows(grad_pre[:, i * D : (i + 1) * D], normed_two) for i in range(RATIO)]
    grads = grads + [contract_rows(active[:, i * D : (i + 1) * D], grad_out_low) for i in range(RATIO)]
    grads = grads + [contract_rows(windows[:, i], grad_compressed) for i in range(3)]
    row_grads = reduce_panels(jnp.stack([g.astype(BF16) for g in grads], 0), lines)

    slotted = row_grads[slot_panel].astype(F32) * scale_all[:, None, None]
    slotted = jnp.where(slot_used[:, None, None], slotted, 0.0).astype(BF16)
    slotted = slotted.reshape(group_count, slot_count, slot_rows, wide)
    slot_parts = lax.all_to_all(slotted, "grp", 0, 0, tiled=True)
    slot_grad = slot_parts.transpose(1, 2, 0, 3).reshape(slot_count, slot_rows, D).astype(F32)
    slot_first, slot_second, slot_weight = adam_update(
        slot_grad, first_moment, second_moment, master, SLOT_RATE
    )
    norm_first_new, norm_second_all, norm_weight = adam_update(
        norm_grad, norm_first, norm_second, norm_params, NORM_RATE
    )
    return (
        mixed, input_grad, slot_grad, slot_first, slot_second, slot_weight, norm_grad,
        norm_first_new, norm_second_all[:2], norm_second_all[2:], norm_weight,
    )


def solution(mesh):
    rows, slots, whole = P(("grp", "seq"), None), P("grp", "seq", None), P()
    return jax.shard_map(
        local,
        mesh=mesh,
        in_specs=(rows, rows, slots, slots, slots) + (whole,) * 6,
        out_specs=(rows, rows, slots, slots, slots, slots) + (whole,) * 5,
        check_vma=False,
    )
```

```python
import functools

import jax
import jax.numpy as jnp
from jax import lax
from jax.experimental import pallas as pl
from jax.experimental.pallas import tpu as pltpu
from jax.sharding import PartitionSpec as P

D = 1024
HEADS = 8
HEAD_DIM = 128
FF = 4096
S = 512
CM = 512
STEP = 10
PANELS = 15
RATIO = FF // D
QB = 128
RAW_KEYS = 2 * S
COMP_KEYS = CM + QB
MIB = 1 << 20

NEG_SCORE = -1e30
NORM_EPS = 1e-05
BETA_ONE = 0.9
BETA_TWO = 0.999
WEIGHT_DECAY = 0.1
ADAM_EPS = 1e-08
NORM_RATE = 1.0
SLOT_RATE = 2.0
BF16 = jnp.bfloat16
F32 = jnp.float32
MESH = pl.DeviceIdType.MESH


def layer_norm(values, gain, shift):
    row_mean = jnp.mean(values, axis=-1, keepdims=True)
    centered = values - row_mean
    variance = jnp.mean(centered * centered, axis=-1, keepdims=True)
    return centered * lax.rsqrt(variance + NORM_EPS) * gain + shift


def panel_deviations():
    inner_dev = D ** (-0.5)
    deviations = [inner_dev] * 3 + [(D // (2 * S)) ** (-0.5)] + [inner_dev] * RATIO
    deviations = deviations + [FF ** (-0.5)] * RATIO + [(3 * D) ** (-0.5)] * 3
    return jnp.array(deviations, F32)


def adam_update(gradient, first_old, second_old, weight_old, step_rate):
    first_new = BETA_ONE * first_old + (1.0 - BETA_ONE) * gradient
    second_new = BETA_TWO * second_old + (1.0 - BETA_TWO) * gradient * gradient
    fix_one = 1.0 - BETA_ONE**STEP
    fix_two = 1.0 - BETA_TWO**STEP
    movement = first_new / fix_one / (jnp.sqrt(second_new / fix_two) + ADAM_EPS)
    return (first_new, second_new, weight_old - step_rate * (movement + WEIGHT_DECAY * weight_old))


def matmul(left, right):
    return jnp.dot(left, right, preferred_element_type=F32)


def times_transposed(left, right):
    return lax.dot_general(left, right, (((1,), (1,)), ((), ())), preferred_element_type=F32)


def contract_rows(left, right):
    return lax.dot_general(left, right, (((0,), (0,)), ((), ())), preferred_element_type=F32)


class Place:
    def __init__(self, lines):
        self.lines = lines
        self.grp = lax.axis_index("grp")
        self.seq = lax.axis_index("seq")
        self.line = self.seq // 2
        self.core = self.seq % 2
        self.row = self.grp // 2
        self.col = self.grp % 2
        self.grp_x = self.row * 2 + 1 - self.col
        self.grp_y = (1 - self.row) * 2 + self.col
        self.x_dev = {"grp": self.grp_x, "seq": self.seq}
        self.y_dev = {"grp": self.grp_y, "seq": self.seq}
        self.core_dev = {"grp": self.grp, "seq": self.line * 2 + 1 - self.core}

    def other_line(self, k):
        return lax.rem(self.line + k, self.lines)

    def line_dev(self, k):
        return {"grp": self.grp, "seq": self.other_line(k) * 2 + self.core}

    def enter(self):
        barrier = pltpu.get_barrier_semaphore()
        partners = [self.line_dev(k) for k in range(1, self.lines)]
        partners = partners + [self.x_dev, self.y_dev, self.core_dev]
        for device in partners:
            pl.semaphore_signal(barrier, inc=1, device_id=device, device_id_type=MESH)
        pl.semaphore_wait(barrier, self.lines + 2)


def remote(src, dst, send, recv, device):
    return pltpu.make_async_remote_copy(
        src_ref=src,
        dst_ref=dst,
        send_sem=send,
        recv_sem=recv,
        device_id=device,
        device_id_type=MESH,
    )


def reduce_kernel(
    panels, lines, grad_ref, out_ref, own, cross_in, first_in, second_in, line_in,
    own_sem, cs, cr, s1, r1, s2, r2, zs, zr,
):
    at = Place(lines)
    wide = out_ref.shape[-1]
    pairs = lines // 2

    def cols(g):
        return pl.ds(g * wide, wide)

    def load(p, g):
        src = grad_ref.at[p, :, :, at.core, :, cols(g)]
        return pltpu.make_async_copy(src, own.at[p, :, :, g // 2, g % 2], own_sem.at[p, g])

    def cross(p, g):
        src = grad_ref.at[p, :, :, 1 - at.core, :, cols(g)]
        dst = cross_in.at[p, :, :, g // 2, g % 2]
        return remote(src, dst, cs.at[p, g], cr.at[p, g], at.core_dev)

    def first(p, h):
        if h == 0:
            src = own.at[p, :, 0, 1 - at.row]
            return remote(src, first_in.at[p, 0], s1.at[p, 0], r1.at[p, 0], at.y_dev)
        src = own.at[p, :, 1, :, 1 - at.col]
        return remote(src, first_in.at[p, 1], s1.at[p, 1], r1.at[p, 1], at.x_dev)

    def second(p, h):
        if h == 0:
            src = own.at[p, :, 0, at.row, 1 - at.col]
            return remote(src, second_in.at[p, 0], s2.at[p, 0], r2.at[p, 0], at.x_dev)
        src = own.at[p, :, 1, 1 - at.row, at.col]
        return remote(src, second_in.at[p, 1], s2.at[p, 1], r2.at[p, 1], at.y_dev)

    def line_copy(p, k):
        z = at.other_line(k)
        src = own.at[p, z // 2, z % 2, at.row, at.col]
        return remote(src, line_in.at[p, at.line], zs.at[p, k], zr.at[p, at.line], at.line_dev(k))

    def line_arrival(p, k):
        z = at.other_line(k)
        src = own.at[p, z // 2, z % 2, at.row, at.col]
        return remote(src, line_in.at[p, z], zs.at[p, k], zr.at[p, z], at.line_dev(k))

    def add(dst, src):
        dst[...] = (dst[...].astype(F32) + src[...].astype(F32)).astype(BF16)

    def start(p):
        for g in range(4):
            cross(p, g).start()
            load(p, g).start()

    def start_first(p):
        for g in range(4):
            cross(p, g).wait_recv()
            load(p, g).wait()
        for h in (0, 1):
            for i in range(pairs):
                for g in range(4):
                    add(own.at[p, i, h, g // 2, g % 2], cross_in.at[p, i, h, g // 2, g % 2])
            first(p, h).start()

    def start_second(p):
        for h in (0, 1):
            first(p, h).wait_recv()
            for i in range(pairs):
                for j in (0, 1):
                    row, col = (at.row, j) if h == 0 else (j, at.col)
                    add(own.at[p, i, h, row, col], first_in.at[p, h, i, j])
            second(p, h).start()

    def start_lines(p):
        for h in (0, 1):
            second(p, h).wait_recv()
            for i in range(pairs):
                add(own.at[p, i, h, at.row, at.col], second_in.at[p, h, i])
        for k in range(1, lines):
            line_copy(p, k).start()

    def finish(p):
        total = own[p, at.line // 2, at.line % 2, at.row, at.col].astype(F32)
        for k in range(1, lines):
            line_arrival(p, k).wait_recv()
            total = total + line_in[p, at.other_line(k)].astype(F32)
        out_ref[p] = total.astype(BF16)
        for h in (0, 1):
            first(p, h).wait_send()
            second(p, h).wait_send()
        for g in range(4):
            cross(p, g).wait_send()
        for k in range(1, lines):
            line_copy(p, k).wait_send()

    at.enter()
    start(0)

    def step(t, carry):
        @pl.when(t + 1 < panels)
        def _():
            start(t + 1)

        @pl.when(t < panels)
        def _():
            start_first(t)

        @pl.when((t >= 1) & (t < panels + 1))
        def _():
            start_second(t - 1)

        @pl.when((t >= 2) & (t < panels + 2))
        def _():
            start_lines(t - 2)

        @pl.when(t >= 3)
        def _():
            finish(t - 3)

        return carry

    lax.fori_loop(0, panels + 3, step, 0)


def reduce_panels(grads, lines):
    panels = grads.shape[0]
    rows, wide, pairs = D // (2 * lines), D // 4, lines // 2
    dma = pltpu.SemaphoreType.DMA
    return pl.pallas_call(
        functools.partial(reduce_kernel, panels, lines),
        out_shape=jax.ShapeDtypeStruct((panels, rows, wide), BF16),
        in_specs=[pl.BlockSpec(memory_space=pl.ANY)],
        out_specs=pl.BlockSpec(memory_space=pltpu.VMEM),
        scratch_shapes=[
            pltpu.VMEM((panels, pairs, 2, 2, 2, rows, wide), BF16),
            pltpu.VMEM((panels, pairs, 2, 2, 2, rows, wide), BF16),
            pltpu.VMEM((panels, 2, pairs, 2, rows, wide), BF16),
            pltpu.VMEM((panels, 2, pairs, rows, wide), BF16),
            pltpu.VMEM((panels, lines, rows, wide), BF16),
            dma((panels, 4)),
            dma((panels, 4)),
            dma((panels, 4)),
            dma((panels, 2)),
            dma((panels, 2)),
            dma((panels, 2)),
            dma((panels, 2)),
            dma((panels, lines)),
            dma((panels, lines)),
        ],
        compiler_params=pltpu.CompilerParams(
            collective_id=1, has_side_effects=True, vmem_limit_bytes=56 * MIB
        ),
        name="reduce_panels",
    )(grads.reshape(panels, pairs, 2, 2, rows, D))


def memory_start(position):
    return (position // S - 1) * S


def comp_window_first(seq, tok_dev):
    return jnp.maximum(memory_start(seq * tok_dev) - 3 * CM, 0) // tok_dev


def raw_devices(tok_dev):
    return (RAW_KEYS - QB + tok_dev - 1) // tok_dev + 1


def comp_devices(tok_dev, seq_count):
    return min((3 * CM + S) // tok_dev + 1, seq_count)


def needs_raw(reader, owner, tok_dev):
    return (owner >= 0) & ((owner + 1) * tok_dev > memory_start(reader * tok_dev))


def needs_comp(reader, owner, tok_dev):
    last = jnp.maximum(memory_start(reader * tok_dev + tok_dev - 1), 0) // 3
    inside = (owner >= 0) & (owner >= comp_window_first(reader, tok_dev))
    return inside & (owner * (tok_dev // 3) < last)


def block_window(seq, i, tok_dev, raw_rows, comp_rows):
    position = seq * tok_dev + i * QB
    memory = memory_start(position)
    raw_base = (seq + 1) * tok_dev - raw_rows
    raw_at = jnp.minimum(memory - raw_base, raw_rows - RAW_KEYS)
    comp_end = jnp.maximum(memory, 0) // 3
    comp_low = jnp.maximum(comp_end - CM, 0)
    comp_base = comp_window_first(seq, tok_dev) * (tok_dev // 3)
    comp_at = jnp.minimum((comp_low - comp_base) // QB * QB, comp_rows - COMP_KEYS)
    return (
        position,
        pl.multiple_of(raw_at, QB),
        pl.multiple_of(comp_at, QB),
        raw_base + raw_at,
        comp_base + comp_at,
        memory,
        comp_low,
        comp_end,
    )


def row_sum(values):
    return jnp.sum(values, axis=1, keepdims=True)


def norm_rows(values, params, first):
    mean = row_sum(values) * (1.0 / D)
    centered = values - mean
    variance = row_sum(centered * centered) * (1.0 / D)
    gain, shift = params[first : first + 1, :], params[first + 1 : first + 2, :]
    return centered * lax.rsqrt(variance + NORM_EPS) * gain + shift


GELU_IN = (2.0 / 3.141592653589793) ** 0.5
GELU_CUBE = 0.044715


def gelu_pair(f):
    square = f * f
    t = jnp.tanh(GELU_IN * f * (1.0 + GELU_CUBE * square))
    half = 0.5 * (1.0 + t)
    slope = half + 0.5 * f * (1.0 - t * t) * (GELU_IN * (1.0 + 3.0 * GELU_CUBE * square))
    return f * half, slope


class Attention:
    def __init__(self, seq, i, tok_dev, raw_rows, comp_rows):
        place = block_window(seq, i, tok_dev, raw_rows, comp_rows)
        self.pos, raw_at, comp_at, self.raw_pos, self.comp_pos = place[:5]
        self.memory, self.comp_low, self.comp_end = place[5:]
        self.rows = pl.ds(i * QB, QB)
        self.raw = pl.ds(raw_at, RAW_KEYS)
        self.comp = pl.ds(comp_at, COMP_KEYS)

    def sees_raw(self, shape, key_dim):
        key_pos = self.raw_pos + lax.broadcasted_iota(jnp.int32, shape, key_dim)
        query_pos = self.pos + lax.broadcasted_iota(jnp.int32, shape, 1 - key_dim)
        return (key_pos >= jnp.maximum(self.memory, 0)) & (key_pos <= query_pos)

    def sees_comp(self, shape, key_dim):
        index = self.comp_pos + lax.broadcasted_iota(jnp.int32, shape, key_dim)
        return (index >= self.comp_low) & (index < self.comp_end)


def attend_head(seq, tok_dev, cols, q, kr, vr, kc, vc, out, lse, lse_row):
    scale = HEAD_DIM ** (-0.5)
    for i in range(tok_dev // QB):
        at = Attention(seq, i, tok_dev, kr.shape[0], kc.shape[0])
        query = q[at.rows, cols]
        raw = times_transposed(query, kr[at.raw, cols]) * scale
        raw = jnp.where(at.sees_raw(raw.shape, 1), raw, NEG_SCORE)
        comp = times_transposed(query, kc[at.comp, cols]) * scale
        comp = jnp.where(at.sees_comp(comp.shape, 1), comp, NEG_SCORE)
        top = jnp.maximum(
            jnp.max(raw, axis=1, keepdims=True), jnp.max(comp, axis=1, keepdims=True)
        )
        raw = jnp.exp(raw - top)
        comp = jnp.exp(comp - top)
        total = row_sum(raw) + row_sum(comp)
        mixed = matmul(raw.astype(BF16), vr[at.raw, cols])
        mixed = mixed + matmul(comp.astype(BF16), vc[at.comp, cols])
        out[at.rows, cols] = mixed / total
        stat = jnp.broadcast_to(top + jnp.log(total), (QB, QB))
        lse[lse_row, :, at.rows] = stat.T[:8]


TAPS = [4 + 2 * RATIO + i for i in range(3)]
ARRIVAL = TAPS + [1, 2, 0, 3]
for _i in range(RATIO):
    ARRIVAL = ARRIVAL + [4 + _i, 4 + RATIO + _i]
LAG = 4


def forward_kernel(
    panels, lines, ahead,
    block_ref, tok_ref, tok3_ref, dy_ref, valid_ref, norm_ref,
    full_ref, a_out, c_out, q_out, kr_out, vr_out, kc_out, vc_out, o_out, z_out, df_out, b_out,
    h_out, db_out, lse_ref, mixed_ref,
    wbuf, a_win, a3, c_win, q, kr, vr, kc, vc, o, z, df, b, h, y, db,
    own_sem, zs, zr, s1, r1, s2, r2, cs, cr, wsem, a_s, a_r, c_s, c_r, out_sem,
):
    at = Place(lines)
    seq = at.seq
    seq_count = 2 * lines
    tok_dev = tok_ref.shape[0]
    comp_dev = tok_dev // 3
    raw_devs = a_win.shape[0] // tok_dev
    comp_devs = c_win.shape[0] // comp_dev
    reach = min(seq_count - 1, (2 * S + 3 * CM + tok_dev - 1) // tok_dev)
    wide = block_ref.shape[-1]

    def cols(g):
        return pl.ds(pl.multiple_of(g * wide, wide), wide)

    def line_copy(p, k):
        dst = full_ref.at[p, at.line // 2, at.line % 2, at.core, :, cols(at.grp)]
        return remote(block_ref.at[p], dst, zs.at[p, k], zr.at[p, at.line], at.line_dev(k))

    def line_arrival(p, k):
        line = at.other_line(k)
        dst = full_ref.at[p, line // 2, line % 2, at.core, :, cols(at.grp)]
        return remote(block_ref.at[p], dst, zs.at[p, k], zr.at[p, line], at.line_dev(k))

    def part(p, half, g):
        return full_ref.at[p, :, half, at.core, :, cols(g)]

    def first(p, half, g):
        device = at.x_dev if half == 0 else at.y_dev
        return remote(part(p, half, g), part(p, half, g), s1.at[p, half], r1.at[p, half], device)

    def second(p, half, j, g):
        device = at.y_dev if half == 0 else at.x_dev
        ref = part(p, half, g)
        return remote(ref, ref, s2.at[p, half, j], r2.at[p, half, j], device)

    def cross(p, half, core):
        ref = full_ref.at[p, :, half, core]
        return remote(ref, ref, cs.at[p, half], cr.at[p, half], at.core_dev)

    def load(p):
        slot = lax.rem(p, wbuf.shape[0])
        return pltpu.make_async_copy(full_ref.at[p], wbuf.at[slot], wsem.at[slot])

    def start_lines(p):
        for k in range(1, lines):
            line_copy(p, k).start()

    def start_first(p):
        for k in range(1, lines):
            line_arrival(p, k).wait_recv()
        for half in (0, 1):
            first(p, half, at.grp).start()

    def start_second(p):
        for half in (0, 1):
            near = at.grp_x if half == 0 else at.grp_y
            first(p, half, near).wait_recv()
            second(p, half, 0, at.grp).start()
            second(p, half, 1, near).start()

    def start_cross(p):
        for half in (0, 1):
            second(p, half, 0, at.grp_y if half == 0 else at.grp_x).wait_recv()
            second(p, half, 1, 3 - at.grp).wait_recv()
            cross(p, half, at.core).start()

    def finish(p):
        for half in (0, 1):
            cross(p, half, 1 - at.core).wait_recv()
            first(p, half, at.grp).wait_send()
            second(p, half, 0, at.grp).wait_send()
            second(p, half, 1, at.grp_x if half == 0 else at.grp_y).wait_send()
            cross(p, half, at.core).wait_send()
        for k in range(1, lines):
            line_copy(p, k).wait_send()
        load(p).start()

    def seq_dev(d):
        return {"grp": at.grp, "seq": lax.rem(seq + d + seq_count, seq_count)}

    def a_rows(d):
        return a_win.at[pl.ds((raw_devs - 1 - d) * tok_dev, tok_dev), :]

    def a_copy(d):
        return remote(a_rows(0), a_rows(d), a_s.at[d], a_r.at[d], seq_dev(d))

    def c_rows(reader, owner):
        place = owner - comp_window_first(reader, tok_dev)
        place = jnp.clip(place, 0, comp_devs - 1)
        return c_win.at[pl.ds(pl.multiple_of(place * comp_dev, comp_dev), comp_dev), :]

    def c_copy(d, own_c):
        return remote(own_c, c_rows(seq + d, seq), c_s.at[d], c_r.at[d], seq_dev(d))

    def c_arrival(d, own_c):
        return remote(own_c, c_rows(seq, seq - d), c_s.at[d], c_r.at[d], seq_dev(-d))

    def reads_a(d):
        return (seq + d < seq_count) & needs_raw(seq + d, seq, tok_dev)

    def reads_c(d):
        return (seq + d < seq_count) & needs_comp(seq + d, seq, tok_dev)

    outs = [
        (a_win, a_out), (c_win, c_out), (q, q_out), (kr, kr_out), (vr, vr_out), (kc, kc_out),
        (vc, vc_out), (o, o_out), (z, z_out), (df, df_out), (b, b_out), (h, h_out), (db, db_out),
    ]

    def flush(*names):
        for i, (src, dst) in enumerate(outs):
            if any(src is name for name in names):
                pltpu.make_async_copy(src, dst, out_sem.at[i]).start()

    barrier = pltpu.get_barrier_semaphore()
    partners = [seq_dev(d) for d in range(1, seq_count)] + [at.x_dev, at.y_dev]
    for device in partners:
        pl.semaphore_signal(barrier, inc=1, device_id=device, device_id_type=MESH)
    pl.semaphore_wait(barrier, seq_count + 1)

    own_place = full_ref.at[:, at.line // 2, at.line % 2, at.core, :, cols(at.grp)]
    own = pltpu.make_async_copy(block_ref, own_place, own_sem)
    own.start()
    for p in range(ahead):
        start_lines(p)

    params = norm_ref[...]
    a_win[pl.ds((raw_devs - 1) * tok_dev, tok_dev), :] = norm_rows(
        tok_ref[...].astype(F32), params, 0
    ).astype(BF16)
    for d in range(1, raw_devs):
        pl.when(reads_a(d))(lambda d=d: a_copy(d).start())
        absent = jnp.logical_not(needs_raw(seq, seq - d, tok_dev))

        @pl.when(absent)
        def _(d=d):
            a_rows(d)[...] = jnp.zeros((tok_dev, D), BF16)

    for k in range(3):
        a3[k] = norm_rows(tok3_ref[k].astype(F32), params, 0).astype(BF16)
    for i in range(comp_devs):
        owner = comp_window_first(seq, tok_dev) + i
        absent = jnp.logical_not(needs_comp(seq, owner, tok_dev))

        @pl.when(absent)
        def _(i=i):
            c_win[pl.ds(i * comp_dev, comp_dev), :] = jnp.zeros((comp_dev, D), BF16)

    own.wait()
    own_c = b.at[pl.ds(0, comp_dev), :]
    tile = 4 * wbuf.shape[4]

    def weight(slot, col):
        return wbuf[slot, :, :, :, :, col].reshape(D, wide)

    def columns(body):
        def one(j, carry):
            body(pl.ds(pl.multiple_of(j * wide, wide), wide))
            return carry

        lax.fori_loop(0, D // wide, one, 0)

    def tap(k, slot):
        def body(col):
            part_sum = matmul(a3[k], weight(slot, col))
            if k == 0:
                y[pl.ds(0, comp_dev), col] = part_sum
            elif k == 1:
                y[pl.ds(0, comp_dev), col] += part_sum
            else:
                own_c[:, col] = (y[pl.ds(0, comp_dev), col] + part_sum).astype(BF16)

        columns(body)

    def project(dst, src, slot):
        block = min(src.shape[0], tok_dev)

        def body(col):
            for i in range(src.shape[0] // block):
                rows = pl.ds(i * block, block)
                dst[rows, col] = matmul(src[rows, :], weight(slot, col)).astype(BF16)

        columns(body)

    def heads(low, high):
        def one(i, carry):
            col = pl.ds(pl.multiple_of(i * HEAD_DIM, HEAD_DIM), HEAD_DIM)
            attend_head(seq, tok_dev, col, q, kr, vr, kc, vc, o, lse_ref, i)
            return carry

        lax.fori_loop(low, high, one, 0)

    def work(p):
        slot = lax.rem(p, wbuf.shape[0])
        for k in range(3):
            pl.when(p == k)(lambda k=k: tap(k, slot))

        @pl.when(p == 2)
        def _():
            for d in range(1, reach + 1):
                pl.when(reads_c(d))(lambda d=d: c_copy(d, own_c).start())
            place = seq - comp_window_first(seq, tok_dev)
            for d in range(1, raw_devs):
                pl.when(needs_raw(seq, seq - d, tok_dev))(lambda d=d: a_copy(d).wait_recv())
                pl.when(reads_a(d))(lambda d=d: a_copy(d).wait_send())
            flush(a_win)

        @pl.when(p == 3)
        def _():
            project(kr, a_win, slot)
            for d in range(1, reach + 1):
                pl.when(needs_comp(seq, seq - d, tok_dev))(lambda d=d: c_arrival(d, own_c).wait_recv())
            project(kc, c_win, slot)
            flush(c_win, kr, kc)

        @pl.when(p == 4)
        def _():
            project(vr, a_win, slot)
            project(vc, c_win, slot)
            flush(vr, vc)

        @pl.when(p == 5)
        def _():
            project(q, a_win.at[pl.ds((raw_devs - 1) * tok_dev, tok_dev), :], slot)
            flush(q)
            heads(0, 2)

        @pl.when(p == 6)
        def _():
            heads(2, 5)

        @pl.when(p == 7)
        def _():
            heads(5, 8)
            flush(o)
            for d in range(1, reach + 1):
                pl.when(reads_c(d))(lambda d=d: c_copy(d, own_c).wait_send())
            out_slot = 6 % wbuf.shape[0]

            def body(col):
                sent = matmul(o[...].astype(BF16), weight(out_slot, col))
                h[:, col] = tok_ref[:, col].astype(F32) + sent

            columns(body)
            for i in range(tok_dev // QB):
                rows = pl.ds(i * QB, QB)
                b[rows, :] = norm_rows(h[rows, :], params, 2).astype(BF16)
            y[...] = h[...]
            db[...] = jnp.zeros_like(db)
            flush(b, h)

        @pl.when((p >= 8) & (lax.rem(p, 2) == 0))
        def _():
            up = lax.rem(p - 1, wbuf.shape[0])
            base = (p // 2 - 4) * D

            def hidden(i, carry):
                up_rows = wbuf[up, i].reshape(tile, D)
                down_rows = wbuf[slot, i].reshape(tile, D)
                value, slope = gelu_pair(times_transposed(b[...], up_rows))
                units = pl.ds(pl.multiple_of(base + i * tile, tile), tile)
                z[:, units] = value.astype(BF16)
                df[:, units] = (times_transposed(dy_ref[...], down_rows) * slope).astype(BF16)
                return carry

            lax.fori_loop(0, wbuf.shape[1], hidden, 0)
            units = pl.ds(pl.multiple_of(base, D), D)

            def body(col):
                y[:, col] += matmul(z[:, units], weight(slot, col))
                db[:, col] += matmul(df[:, units], weight(up, col))

            columns(body)

    def step(t, carry):
        pl.when(t + ahead < panels)(lambda: start_lines(t + ahead))
        pl.when(t < panels)(lambda: start_first(t))
        pl.when((t >= 1) & (t < panels + 1))(lambda: start_second(t - 1))
        pl.when((t >= 2) & (t < panels + 2))(lambda: start_cross(t - 2))

        @pl.when(t >= LAG)
        def _():
            load(t - LAG).wait()
            work(t - LAG)

        pl.when((t >= 3) & (t < panels + 3))(lambda: finish(t - 3))
        return carry

    lax.fori_loop(0, panels + LAG, step, 0)
    flush(z, df, db)
    mixed_ref[...] = (y[...] * valid_ref[...]).astype(BF16)
    for i, (src, dst) in enumerate(outs):
        pltpu.make_async_copy(src, dst, out_sem.at[i]).wait()


def forward(block, tokens, tokens3, grad_out, valid, norm_params, lines):
    panels, rows, wide = block.shape
    tok_dev = tokens.shape[0]
    raw = raw_devices(tok_dev) * tok_dev
    comp = comp_devices(tok_dev, 2 * lines) * (tok_dev // 3)
    dma = pltpu.SemaphoreType.DMA
    shapes = [
        ((raw, D), BF16), ((comp, D), BF16), ((tok_dev, D), BF16), ((raw, D), BF16),
        ((raw, D), BF16), ((comp, D), BF16), ((comp, D), BF16), ((tok_dev, D), F32),
        ((tok_dev, FF), BF16), ((tok_dev, FF), BF16), ((tok_dev, D), BF16), ((tok_dev, D), F32),
        ((tok_dev, D), F32),
    ]
    scratch = [pltpu.VMEM(shape, kind) for shape, kind in shapes]
    scratch.insert(1, pltpu.VMEM((3, tok_dev // 3, D), BF16))
    scratch.insert(len(scratch) - 1, pltpu.VMEM((tok_dev, D), F32))
    any_spec, vmem = pl.BlockSpec(memory_space=pl.ANY), pl.BlockSpec(memory_space=pltpu.VMEM)
    return pl.pallas_call(
        functools.partial(forward_kernel, panels, lines, 3),
        out_shape=[jax.ShapeDtypeStruct((panels, lines // 2, 2, 2, rows, D), BF16)]
        + [jax.ShapeDtypeStruct(shape, kind) for shape, kind in shapes]
        + [jax.ShapeDtypeStruct((HEADS, 8, tok_dev), F32), jax.ShapeDtypeStruct((tok_dev, D), BF16)],
        in_specs=[any_spec] + [vmem] * 5,
        out_specs=[any_spec] * (1 + len(shapes)) + [vmem] * 2,
        scratch_shapes=[pltpu.VMEM((4, lines // 2, 2, 2, rows, D), BF16)]
        + scratch
        + [
            dma(()),
            dma((panels, lines)), dma((panels, lines)),
            dma((panels, 2)), dma((panels, 2)),
            dma((panels, 2, 2)), dma((panels, 2, 2)),
            dma((panels, 2)), dma((panels, 2)),
            dma((4,)),
            dma((8,)), dma((8,)), dma((8,)), dma((8,)),
            dma((len(shapes),)),
        ],
        compiler_params=pltpu.CompilerParams(
            collective_id=0, has_side_effects=True, vmem_limit_bytes=58 * MIB
        ),
        name="forward",
    )(block, tokens, tokens3, grad_out, valid, norm_params)


def attend_back_kernel(
    tok_dev, q_ref, kr_ref, vr_ref, kc_ref, vc_ref, do_ref, lse_ref, delta_ref,
    dq_ref, dkr_ref, dvr_ref, dkc_ref, dvc_ref, acc_kr, acc_vr, acc_kc, acc_vc,
):
    seq = lax.axis_index("seq")
    scale = HEAD_DIM ** (-0.5)
    for acc in (acc_kr, acc_vr, acc_kc, acc_vc):
        acc[...] = jnp.zeros_like(acc)
    for i in range(tok_dev // QB):
        at = Attention(seq, i, tok_dev, kr_ref.shape[0], kc_ref.shape[0])
        rows = at.rows
        q = q_ref[rows, :]
        do = do_ref[rows, :]
        lse = lse_ref[0, 0:1, rows]
        delta = delta_ref[0, 0:1, rows]

        def part(k_ref, v_ref, acc_k, acc_v, keys, seen):
            k = k_ref[keys, :]
            s = times_transposed(k, q) * scale
            p = jnp.where(seen, jnp.exp(jnp.where(seen, s, NEG_SCORE) - lse), 0.0)
            dp = times_transposed(v_ref[keys, :], do)
            ds = (p * (dp - delta)).astype(BF16)
            acc_v[keys, :] += matmul(p.astype(BF16), do)
            acc_k[keys, :] += matmul(ds, q)
            return contract_rows(ds, k)

        seen = at.sees_raw((RAW_KEYS, QB), 0)
        dq = part(kr_ref, vr_ref, acc_kr, acc_vr, at.raw, seen)
        seen = at.sees_comp((COMP_KEYS, QB), 0)
        dq = dq + part(kc_ref, vc_ref, acc_kc, acc_vc, at.comp, seen)
        dq_ref[rows, :] = (dq * scale).astype(BF16)
    dkr_ref[...] = (acc_kr[...] * scale).astype(BF16)
    dkc_ref[...] = (acc_kc[...] * scale).astype(BF16)
    dvr_ref[...] = acc_vr[...].astype(BF16)
    dvc_ref[...] = acc_vc[...].astype(BF16)


def attend_back(q, kr, vr, kc, vc, do, lse, delta):
    tok_dev, raw_rows, comp_rows = q.shape[0], kr.shape[0], kc.shape[0]

    def head(rows):
        return pl.BlockSpec((rows, HEAD_DIM), lambda h: (0, h))

    stat = pl.BlockSpec((1, 8, tok_dev), lambda h: (h, 0, 0))
    outs = [tok_dev, raw_rows, raw_rows, comp_rows, comp_rows]
    return pl.pallas_call(
        functools.partial(attend_back_kernel, tok_dev),
        grid=(HEADS,),
        in_specs=[head(x.shape[0]) for x in (q, kr, vr, kc, vc, do)] + [stat, stat],
        out_specs=[head(rows) for rows in outs],
        out_shape=[jax.ShapeDtypeStruct((rows, D), BF16) for rows in outs],
        scratch_shapes=[
            pltpu.VMEM((raw_rows, HEAD_DIM), F32),
            pltpu.VMEM((raw_rows, HEAD_DIM), F32),
            pltpu.VMEM((comp_rows, HEAD_DIM), F32),
            pltpu.VMEM((comp_rows, HEAD_DIM), F32),
        ],
        compiler_params=pltpu.CompilerParams(vmem_limit_bytes=40 * MIB),
        name="attend_back",
    )(q, kr, vr, kc, vc, do, lse, delta)


def local(
    tokens, cotangent, master, first_moment, second_moment, norm_params, norm_first, norm_second,
    seg_valid, book_of_group, panel_slot,
):
    seq_count = lax.axis_size("seq")
    group_count = lax.axis_size("grp")
    seq_index = lax.axis_index("seq")
    group_index = lax.axis_index("grp")
    lines = seq_count // 2
    tok_dev = tokens.shape[0]
    slot_count, slot_rows = master.shape[0], master.shape[1]
    all_slots = slot_count * group_count
    comp_dev = tok_dev // 3
    wide = D // group_count

    slot_ids = jnp.arange(all_slots, dtype=jnp.int32)
    is_panel = panel_slot[None, :] == slot_ids[:, None]
    slot_used = jnp.any(is_panel, 1)
    slot_panel = jnp.argmax(is_panel, 1).astype(jnp.int32)
    scale_all = jnp.sum(jnp.where(is_panel, panel_deviations()[None, :], 0.0), 1)
    slot_scale = lax.dynamic_slice_in_dim(scale_all, group_index * slot_count, slot_count, 0)
    scaled = (master * slot_scale[:, None, None]).astype(BF16)
    scaled = scaled.reshape(slot_count, slot_rows, group_count, wide).transpose(2, 0, 1, 3)
    slots_in = lax.all_to_all(scaled, "grp", 0, 0, tiled=True)
    block = slots_in.reshape(all_slots, slot_rows, wide)[panel_slot[jnp.array(ARRIVAL)]]

    positions = seq_index * tok_dev + jnp.arange(tok_dev, dtype=jnp.int32)
    book_id = jnp.sum(jnp.where(jnp.arange(group_count) == group_index, book_of_group, 0))
    book_counts = jnp.sum(jnp.where((jnp.arange(group_count) == book_id)[:, None], seg_valid, 0), 0)
    segments = seg_valid.shape[1]
    row_counts = jnp.sum(
        jnp.where((positions // S)[:, None] == jnp.arange(segments)[None, :], book_counts[None, :], 0), 1
    )
    row_valid = (positions % S < row_counts).astype(F32)

    inputs = tokens.astype(F32)
    tokens3 = tokens.reshape(comp_dev, 3, D).transpose(1, 0, 2)
    grad_out = cotangent.astype(F32) * row_valid[:, None]
    grad_out_low = grad_out.astype(BF16)
    (
        weights, normed_raw, compressed, queries, keys_raw, values_raw, keys_comp, values_comp,
        attended_sum, active, grad_pre, normed_two, hidden, grad_normed_two, log_total, mixed,
    ) = forward(block, tokens, tokens3, grad_out_low, row_valid[:, None], norm_params, lines)
    weights = weights.reshape(PANELS, D, D)
    key_weight, value_weight, query_weight, out_weight = [weights[i] for i in range(3, 7)]
    conv_weight = weights[:3]
    raw_devs = raw_devices(tok_dev)
    comp_first = comp_window_first(seq_index, tok_dev)
    normed = normed_raw[(raw_devs - 1) * tok_dev :]
    attended = attended_sum.astype(BF16)
    norm_value, norm_two_back = jax.vjp(layer_norm, hidden, norm_params[2], norm_params[3])
    grad_hidden_norm, grad_gain_two, grad_shift_two = norm_two_back(grad_normed_two)
    grad_hidden = grad_out + grad_hidden_norm
    grad_branch = grad_hidden.astype(BF16)
    grad_attended = times_transposed(grad_branch, out_weight).astype(BF16)
    delta = jnp.sum(
        (grad_attended.astype(F32) * attended_sum).reshape(tok_dev, HEADS, HEAD_DIM), -1
    ).T
    delta = jnp.broadcast_to(delta[:, None, :], (HEADS, 8, tok_dev))
    grad_queries, dkr, dvr, dkc, dvc = attend_back(
        queries, keys_raw, values_raw, keys_comp, values_comp, grad_attended, log_total, delta
    )

    grad_comp = (times_transposed(dkc, key_weight) + times_transposed(dvc, value_weight)).astype(BF16)
    placed = lax.dynamic_update_slice_in_dim(
        jnp.zeros((seq_count * comp_dev, D), BF16), grad_comp, comp_first * comp_dev, 0
    )
    grad_compressed = lax.psum_scatter(placed, "seq", scatter_dimension=0, tiled=True)
    grad_raw = times_transposed(dkr, key_weight) + times_transposed(dvr, value_weight)
    grad_normed = grad_raw[(raw_devs - 1) * tok_dev :]
    for back in range(1, raw_devs):
        rows = grad_raw[(raw_devs - 1 - back) * tok_dev : (raw_devs - back) * tok_dev].astype(BF16)
        pairs = [(s, s - back) for s in range(back, seq_count)]
        grad_normed = grad_normed + lax.ppermute(rows, "seq", pairs).astype(F32)
    grad_normed = grad_normed + times_transposed(grad_queries, query_weight)
    grad_windows = times_transposed(grad_compressed, conv_weight.reshape(3 * D, D))
    grad_normed = grad_normed + grad_windows.reshape(tok_dev, D)
    norm_value_one, norm_one_back = jax.vjp(layer_norm, inputs, norm_params[0], norm_params[1])
    grad_inputs_norm, grad_gain_one, grad_shift_one = norm_one_back(grad_normed)
    input_grad = grad_hidden + grad_inputs_norm
    norm_local = jnp.stack([grad_gain_one, grad_shift_one, grad_gain_two, grad_shift_two], 0)
    norm_grad = lax.psum(norm_local, ("grp", "seq"))

    windows = normed.reshape(comp_dev, 3, D)
    grads = [
        contract_rows(normed, grad_queries),
        contract_rows(normed_raw, dkr) + contract_rows(compressed, dkc),
        contract_rows(normed_raw, dvr) + contract_rows(compressed, dvc),
        contract_rows(attended, grad_branch),
    ]
    grads = grads + [contract_rows(grad_pre[:, i * D : (i + 1) * D], normed_two) for i in range(RATIO)]
    grads = grads + [contract_rows(active[:, i * D : (i + 1) * D], grad_out_low) for i in range(RATIO)]
    grads = grads + [contract_rows(windows[:, i], grad_compressed) for i in range(3)]
    row_grads = reduce_panels(jnp.stack([g.astype(BF16) for g in grads], 0), lines)

    slotted = row_grads[slot_panel].astype(F32) * scale_all[:, None, None]
    slotted = jnp.where(slot_used[:, None, None], slotted, 0.0).astype(BF16)
    slotted = slotted.reshape(group_count, slot_count, slot_rows, wide)
    slot_parts = lax.all_to_all(slotted, "grp", 0, 0, tiled=True)
    slot_grad = slot_parts.transpose(1, 2, 0, 3).reshape(slot_count, slot_rows, D).astype(F32)
    slot_first, slot_second, slot_weight = adam_update(
        slot_grad, first_moment, second_moment, master, SLOT_RATE
    )
    norm_first_new, norm_second_all, norm_weight = adam_update(
        norm_grad, norm_first, norm_second, norm_params, NORM_RATE
    )
    return (
        mixed, input_grad, slot_grad, slot_first, slot_second, slot_weight, norm_grad,
        norm_first_new, norm_second_all[:2], norm_second_all[2:], norm_weight,
    )


def solution(mesh):
    rows, slots, whole = P(("grp", "seq"), None), P("grp", "seq", None), P()
    return jax.shard_map(
        local,
        mesh=mesh,
        in_specs=(rows, rows, slots, slots, slots) + (whole,) * 6,
        out_specs=(rows, rows, slots, slots, slots, slots) + (whole,) * 5,
        check_vma=False,
    )
```

```python
import functools

import jax
import jax.numpy as jnp
from jax import lax
from jax.experimental import pallas as pl
from jax.experimental.pallas import tpu as pltpu
from jax.sharding import PartitionSpec as P

D = 1024
HEADS = 8
HEAD_DIM = 128
FF = 4096
S = 512
CM = 512
STEP = 10
PANELS = 15
RATIO = FF // D
QB = 128
RAW_KEYS = 2 * S
COMP_KEYS = CM + QB
MIB = 1 << 20

NEG_SCORE = -1e30
NORM_EPS = 1e-05
BETA_ONE = 0.9
BETA_TWO = 0.999
WEIGHT_DECAY = 0.1
ADAM_EPS = 1e-08
NORM_RATE = 1.0
SLOT_RATE = 2.0
BF16 = jnp.bfloat16
F32 = jnp.float32
MESH = pl.DeviceIdType.MESH


def layer_norm(values, gain, shift):
    row_mean = jnp.mean(values, axis=-1, keepdims=True)
    centered = values - row_mean
    variance = jnp.mean(centered * centered, axis=-1, keepdims=True)
    return centered * lax.rsqrt(variance + NORM_EPS) * gain + shift


def panel_deviations():
    inner_dev = D ** (-0.5)
    deviations = [inner_dev] * 3 + [(D // (2 * S)) ** (-0.5)] + [inner_dev] * RATIO
    deviations = deviations + [FF ** (-0.5)] * RATIO + [(3 * D) ** (-0.5)] * 3
    return jnp.array(deviations, F32)


def adam_update(gradient, first_old, second_old, weight_old, step_rate):
    first_new = BETA_ONE * first_old + (1.0 - BETA_ONE) * gradient
    second_new = BETA_TWO * second_old + (1.0 - BETA_TWO) * gradient * gradient
    fix_one = 1.0 - BETA_ONE**STEP
    fix_two = 1.0 - BETA_TWO**STEP
    movement = first_new / fix_one / (jnp.sqrt(second_new / fix_two) + ADAM_EPS)
    return (first_new, second_new, weight_old - step_rate * (movement + WEIGHT_DECAY * weight_old))


def matmul(left, right):
    return jnp.dot(left, right, preferred_element_type=F32)


def times_transposed(left, right):
    return lax.dot_general(left, right, (((1,), (1,)), ((), ())), preferred_element_type=F32)


def contract_rows(left, right):
    return lax.dot_general(left, right, (((0,), (0,)), ((), ())), preferred_element_type=F32)


class Place:
    def __init__(self, lines):
        self.lines = lines
        self.grp = lax.axis_index("grp")
        self.seq = lax.axis_index("seq")
        self.line = self.seq // 2
        self.core = self.seq % 2
        self.row = self.grp // 2
        self.col = self.grp % 2
        self.grp_x = self.row * 2 + 1 - self.col
        self.grp_y = (1 - self.row) * 2 + self.col
        self.x_dev = {"grp": self.grp_x, "seq": self.seq}
        self.y_dev = {"grp": self.grp_y, "seq": self.seq}
        self.core_dev = {"grp": self.grp, "seq": self.line * 2 + 1 - self.core}

    def other_line(self, k):
        return lax.rem(self.line + k, self.lines)

    def line_dev(self, k):
        return {"grp": self.grp, "seq": self.other_line(k) * 2 + self.core}

    def enter(self):
        barrier = pltpu.get_barrier_semaphore()
        partners = [self.line_dev(k) for k in range(1, self.lines)]
        partners = partners + [self.x_dev, self.y_dev, self.core_dev]
        for device in partners:
            pl.semaphore_signal(barrier, inc=1, device_id=device, device_id_type=MESH)
        pl.semaphore_wait(barrier, self.lines + 2)


def remote(src, dst, send, recv, device):
    return pltpu.make_async_remote_copy(
        src_ref=src,
        dst_ref=dst,
        send_sem=send,
        recv_sem=recv,
        device_id=device,
        device_id_type=MESH,
    )


def memory_start(position):
    return (position // S - 1) * S


def comp_window_first(seq, tok_dev):
    return jnp.maximum(memory_start(seq * tok_dev) - 3 * CM, 0) // tok_dev


def raw_devices(tok_dev):
    return (RAW_KEYS - QB + tok_dev - 1) // tok_dev + 1


def comp_devices(tok_dev, seq_count):
    return min((3 * CM + S) // tok_dev + 1, seq_count)


def needs_raw(reader, owner, tok_dev):
    return (owner >= 0) & ((owner + 1) * tok_dev > memory_start(reader * tok_dev))


def needs_comp(reader, owner, tok_dev):
    last = jnp.maximum(memory_start(reader * tok_dev + tok_dev - 1), 0) // 3
    inside = (owner >= 0) & (owner >= comp_window_first(reader, tok_dev))
    return inside & (owner * (tok_dev // 3) < last)


def block_window(seq, i, tok_dev, raw_rows, comp_rows):
    position = seq * tok_dev + i * QB
    memory = memory_start(position)
    raw_base = (seq + 1) * tok_dev - raw_rows
    raw_at = jnp.minimum(memory - raw_base, raw_rows - RAW_KEYS)
    comp_end = jnp.maximum(memory, 0) // 3
    comp_low = jnp.maximum(comp_end - CM, 0)
    comp_base = comp_window_first(seq, tok_dev) * (tok_dev // 3)
    comp_at = jnp.minimum((comp_low - comp_base) // QB * QB, comp_rows - COMP_KEYS)
    return (
        position,
        pl.multiple_of(raw_at, QB),
        pl.multiple_of(comp_at, QB),
        raw_base + raw_at,
        comp_base + comp_at,
        memory,
        comp_low,
        comp_end,
    )


def row_sum(values):
    return jnp.sum(values, axis=1, keepdims=True)


def norm_rows(values, params, first):
    mean = row_sum(values) * (1.0 / D)
    centered = values - mean
    variance = row_sum(centered * centered) * (1.0 / D)
    gain, shift = params[first : first + 1, :], params[first + 1 : first + 2, :]
    return centered * lax.rsqrt(variance + NORM_EPS) * gain + shift


GELU_IN = (2.0 / 3.141592653589793) ** 0.5
GELU_CUBE = 0.044715


def gelu_pair(f):
    square = f * f
    t = jnp.tanh(GELU_IN * f * (1.0 + GELU_CUBE * square))
    half = 0.5 * (1.0 + t)
    slope = half + 0.5 * f * (1.0 - t * t) * (GELU_IN * (1.0 + 3.0 * GELU_CUBE * square))
    return f * half, slope


class Attention:
    def __init__(self, seq, i, tok_dev, raw_rows, comp_rows):
        place = block_window(seq, i, tok_dev, raw_rows, comp_rows)
        self.pos, raw_at, comp_at, self.raw_pos, self.comp_pos = place[:5]
        self.memory, self.comp_low, self.comp_end = place[5:]
        self.rows = pl.ds(i * QB, QB)
        self.raw = pl.ds(raw_at, RAW_KEYS)
        self.comp = pl.ds(comp_at, COMP_KEYS)

    def sees_raw(self, shape, key_dim):
        key_pos = self.raw_pos + lax.broadcasted_iota(jnp.int32, shape, key_dim)
        query_pos = self.pos + lax.broadcasted_iota(jnp.int32, shape, 1 - key_dim)
        return (key_pos >= jnp.maximum(self.memory, 0)) & (key_pos <= query_pos)

    def sees_comp(self, shape, key_dim):
        index = self.comp_pos + lax.broadcasted_iota(jnp.int32, shape, key_dim)
        return (index >= self.comp_low) & (index < self.comp_end)


def attend_head(seq, tok_dev, cols, q, kr, vr, kc, vc, out, lse, lse_row):
    scale = HEAD_DIM ** (-0.5)
    for i in range(tok_dev // QB):
        at = Attention(seq, i, tok_dev, kr.shape[0], kc.shape[0])
        query = q[at.rows, cols]
        raw = times_transposed(query, kr[at.raw, cols]) * scale
        raw = jnp.where(at.sees_raw(raw.shape, 1), raw, NEG_SCORE)
        comp = times_transposed(query, kc[at.comp, cols]) * scale
        comp = jnp.where(at.sees_comp(comp.shape, 1), comp, NEG_SCORE)
        top = jnp.maximum(
            jnp.max(raw, axis=1, keepdims=True), jnp.max(comp, axis=1, keepdims=True)
        )
        raw = jnp.exp(raw - top)
        comp = jnp.exp(comp - top)
        total = row_sum(raw) + row_sum(comp)
        mixed = matmul(raw.astype(BF16), vr[at.raw, cols])
        mixed = mixed + matmul(comp.astype(BF16), vc[at.comp, cols])
        out[at.rows, cols] = mixed / total
        stat = jnp.broadcast_to(top + jnp.log(total), (QB, QB))
        lse[lse_row, :, at.rows] = stat.T[:8]


TAPS = [4 + 2 * RATIO + i for i in range(3)]
ARRIVAL = TAPS + [1, 2, 0, 3]
for _i in range(RATIO):
    ARRIVAL = ARRIVAL + [4 + _i, 4 + RATIO + _i]
LAG = 4


def forward_kernel(
    panels, lines, ahead,
    block_ref, tok_ref, tok3_ref, dy_ref, valid_ref, norm_ref,
    full_ref, a_out, c_out, q_out, kr_out, vr_out, kc_out, vc_out, o_out, z_out, df_out, b_out,
    h_out, db_out, a3_out, lse_ref, mixed_ref,
    wbuf, a_win, a3, c_win, q, kr, vr, kc, vc, o, z, df, b, h, y, db,
    own_sem, zs, zr, s1, r1, s2, r2, cs, cr, wsem, a_s, a_r, c_s, c_r, out_sem,
):
    at = Place(lines)
    seq = at.seq
    seq_count = 2 * lines
    tok_dev = tok_ref.shape[0]
    comp_dev = tok_dev // 3
    raw_devs = a_win.shape[0] // tok_dev
    comp_devs = c_win.shape[0] // comp_dev
    reach = min(seq_count - 1, (2 * S + 3 * CM + tok_dev - 1) // tok_dev)
    wide = block_ref.shape[-1]

    def cols(g):
        return pl.ds(pl.multiple_of(g * wide, wide), wide)

    def line_copy(p, k):
        dst = full_ref.at[p, at.line // 2, at.line % 2, at.core, :, cols(at.grp)]
        return remote(block_ref.at[p], dst, zs.at[p, k], zr.at[p, at.line], at.line_dev(k))

    def line_arrival(p, k):
        line = at.other_line(k)
        dst = full_ref.at[p, line // 2, line % 2, at.core, :, cols(at.grp)]
        return remote(block_ref.at[p], dst, zs.at[p, k], zr.at[p, line], at.line_dev(k))

    def part(p, half, g):
        return full_ref.at[p, :, half, at.core, :, cols(g)]

    def first(p, half, g):
        device = at.x_dev if half == 0 else at.y_dev
        return remote(part(p, half, g), part(p, half, g), s1.at[p, half], r1.at[p, half], device)

    def second(p, half, j, g):
        device = at.y_dev if half == 0 else at.x_dev
        ref = part(p, half, g)
        return remote(ref, ref, s2.at[p, half, j], r2.at[p, half, j], device)

    def cross(p, half, core):
        ref = full_ref.at[p, :, half, core]
        return remote(ref, ref, cs.at[p, half], cr.at[p, half], at.core_dev)

    def load(p):
        slot = lax.rem(p, wbuf.shape[0])
        return pltpu.make_async_copy(full_ref.at[p], wbuf.at[slot], wsem.at[slot])

    def start_lines(p):
        for k in range(1, lines):
            line_copy(p, k).start()

    def start_first(p):
        for k in range(1, lines):
            line_arrival(p, k).wait_recv()
        for half in (0, 1):
            first(p, half, at.grp).start()

    def start_second(p):
        for half in (0, 1):
            near = at.grp_x if half == 0 else at.grp_y
            first(p, half, near).wait_recv()
            second(p, half, 0, at.grp).start()
            second(p, half, 1, near).start()

    def start_cross(p):
        for half in (0, 1):
            second(p, half, 0, at.grp_y if half == 0 else at.grp_x).wait_recv()
            second(p, half, 1, 3 - at.grp).wait_recv()
            cross(p, half, at.core).start()

    def finish(p):
        for half in (0, 1):
            cross(p, half, 1 - at.core).wait_recv()
            first(p, half, at.grp).wait_send()
            second(p, half, 0, at.grp).wait_send()
            second(p, half, 1, at.grp_x if half == 0 else at.grp_y).wait_send()
            cross(p, half, at.core).wait_send()
        for k in range(1, lines):
            line_copy(p, k).wait_send()
        load(p).start()

    def seq_dev(d):
        return {"grp": at.grp, "seq": lax.rem(seq + d + seq_count, seq_count)}

    def a_rows(d):
        return a_win.at[pl.ds((raw_devs - 1 - d) * tok_dev, tok_dev), :]

    def a_copy(d):
        return remote(a_rows(0), a_rows(d), a_s.at[d], a_r.at[d], seq_dev(d))

    def c_rows(reader, owner):
        place = owner - comp_window_first(reader, tok_dev)
        place = jnp.clip(place, 0, comp_devs - 1)
        return c_win.at[pl.ds(pl.multiple_of(place * comp_dev, comp_dev), comp_dev), :]

    def c_copy(d, own_c):
        return remote(own_c, c_rows(seq + d, seq), c_s.at[d], c_r.at[d], seq_dev(d))

    def c_arrival(d, own_c):
        return remote(own_c, c_rows(seq, seq - d), c_s.at[d], c_r.at[d], seq_dev(-d))

    def reads_a(d):
        return (seq + d < seq_count) & needs_raw(seq + d, seq, tok_dev)

    def reads_c(d):
        return (seq + d < seq_count) & needs_comp(seq + d, seq, tok_dev)

    outs = [
        (a_win, a_out), (c_win, c_out), (q, q_out), (kr, kr_out), (vr, vr_out), (kc, kc_out),
        (vc, vc_out), (o, o_out), (z, z_out), (df, df_out), (b, b_out), (h, h_out), (db, db_out),
        (a3, a3_out),
    ]

    def flush(*names):
        for i, (src, dst) in enumerate(outs):
            if any(src is name for name in names):
                pltpu.make_async_copy(src, dst, out_sem.at[i]).start()

    barrier = pltpu.get_barrier_semaphore()
    partners = [seq_dev(d) for d in range(1, seq_count)] + [at.x_dev, at.y_dev]
    for device in partners:
        pl.semaphore_signal(barrier, inc=1, device_id=device, device_id_type=MESH)
    pl.semaphore_wait(barrier, seq_count + 1)

    own_place = full_ref.at[:, at.line // 2, at.line % 2, at.core, :, cols(at.grp)]
    own = pltpu.make_async_copy(block_ref, own_place, own_sem)
    own.start()
    for p in range(ahead):
        start_lines(p)

    params = norm_ref[...]
    a_win[pl.ds((raw_devs - 1) * tok_dev, tok_dev), :] = norm_rows(
        tok_ref[...].astype(F32), params, 0
    ).astype(BF16)
    for d in range(1, raw_devs):
        pl.when(reads_a(d))(lambda d=d: a_copy(d).start())
        absent = jnp.logical_not(needs_raw(seq, seq - d, tok_dev))

        @pl.when(absent)
        def _(d=d):
            a_rows(d)[...] = jnp.zeros((tok_dev, D), BF16)

    for k in range(3):
        a3[k] = norm_rows(tok3_ref[k].astype(F32), params, 0).astype(BF16)
    for i in range(comp_devs):
        owner = comp_window_first(seq, tok_dev) + i
        absent = jnp.logical_not(needs_comp(seq, owner, tok_dev))

        @pl.when(absent)
        def _(i=i):
            c_win[pl.ds(i * comp_dev, comp_dev), :] = jnp.zeros((comp_dev, D), BF16)

    own.wait()
    own_c = b.at[pl.ds(0, comp_dev), :]
    tile = 4 * wbuf.shape[4]

    def weight(slot, col):
        return wbuf[slot, :, :, :, :, col].reshape(D, wide)

    def columns(body):
        def one(j, carry):
            body(pl.ds(pl.multiple_of(j * wide, wide), wide))
            return carry

        lax.fori_loop(0, D // wide, one, 0)

    def tap(k, slot):
        def body(col):
            part_sum = matmul(a3[k], weight(slot, col))
            if k == 0:
                y[pl.ds(0, comp_dev), col] = part_sum
            elif k == 1:
                y[pl.ds(0, comp_dev), col] += part_sum
            else:
                own_c[:, col] = (y[pl.ds(0, comp_dev), col] + part_sum).astype(BF16)

        columns(body)

    def project(dst, src, slot):
        block = min(src.shape[0], tok_dev)

        def body(col):
            for i in range(src.shape[0] // block):
                rows = pl.ds(i * block, block)
                dst[rows, col] = matmul(src[rows, :], weight(slot, col)).astype(BF16)

        columns(body)

    def heads(low, high):
        def one(i, carry):
            col = pl.ds(pl.multiple_of(i * HEAD_DIM, HEAD_DIM), HEAD_DIM)
            attend_head(seq, tok_dev, col, q, kr, vr, kc, vc, o, lse_ref, i)
            return carry

        lax.fori_loop(low, high, one, 0)

    def work(p):
        slot = lax.rem(p, wbuf.shape[0])
        for k in range(3):
            pl.when(p == k)(lambda k=k: tap(k, slot))

        @pl.when(p == 2)
        def _():
            for d in range(1, reach + 1):
                pl.when(reads_c(d))(lambda d=d: c_copy(d, own_c).start())
            place = seq - comp_window_first(seq, tok_dev)
            for d in range(1, raw_devs):
                pl.when(needs_raw(seq, seq - d, tok_dev))(lambda d=d: a_copy(d).wait_recv())
                pl.when(reads_a(d))(lambda d=d: a_copy(d).wait_send())
            flush(a_win, a3)

        @pl.when(p == 3)
        def _():
            project(kr, a_win, slot)
            for d in range(1, reach + 1):
                pl.when(needs_comp(seq, seq - d, tok_dev))(lambda d=d: c_arrival(d, own_c).wait_recv())
            project(kc, c_win, slot)
            flush(c_win, kr, kc)

        @pl.when(p == 4)
        def _():
            project(vr, a_win, slot)
            project(vc, c_win, slot)
            flush(vr, vc)

        @pl.when(p == 5)
        def _():
            project(q, a_win.at[pl.ds((raw_devs - 1) * tok_dev, tok_dev), :], slot)
            flush(q)
            heads(0, 2)

        @pl.when(p == 6)
        def _():
            heads(2, 5)

        @pl.when(p == 7)
        def _():
            heads(5, 8)
            flush(o)
            for d in range(1, reach + 1):
                pl.when(reads_c(d))(lambda d=d: c_copy(d, own_c).wait_send())
            out_slot = 6 % wbuf.shape[0]

            def body(col):
                sent = matmul(o[...].astype(BF16), weight(out_slot, col))
                h[:, col] = tok_ref[:, col].astype(F32) + sent

            columns(body)
            for i in range(tok_dev // QB):
                rows = pl.ds(i * QB, QB)
                b[rows, :] = norm_rows(h[rows, :], params, 2).astype(BF16)
            y[...] = h[...]
            db[...] = jnp.zeros_like(db)
            flush(b, h)

        @pl.when((p >= 8) & (lax.rem(p, 2) == 0))
        def _():
            up = lax.rem(p - 1, wbuf.shape[0])
            base = (p // 2 - 4) * D

            def hidden(i, carry):
                up_rows = wbuf[up, i].reshape(tile, D)
                down_rows = wbuf[slot, i].reshape(tile, D)
                value, slope = gelu_pair(times_transposed(b[...], up_rows))
                units = pl.ds(pl.multiple_of(base + i * tile, tile), tile)
                z[:, units] = value.astype(BF16)
                df[:, units] = (times_transposed(dy_ref[...], down_rows) * slope).astype(BF16)
                return carry

            lax.fori_loop(0, wbuf.shape[1], hidden, 0)
            units = pl.ds(pl.multiple_of(base, D), D)

            def body(col):
                y[:, col] += matmul(z[:, units], weight(slot, col))
                db[:, col] += matmul(df[:, units], weight(up, col))

            columns(body)

    def step(t, carry):
        pl.when(t + ahead < panels)(lambda: start_lines(t + ahead))
        pl.when(t < panels)(lambda: start_first(t))
        pl.when((t >= 1) & (t < panels + 1))(lambda: start_second(t - 1))
        pl.when((t >= 2) & (t < panels + 2))(lambda: start_cross(t - 2))

        @pl.when(t >= LAG)
        def _():
            load(t - LAG).wait()
            work(t - LAG)

        pl.when((t >= 3) & (t < panels + 3))(lambda: finish(t - 3))
        return carry

    lax.fori_loop(0, panels + LAG, step, 0)
    flush(z, df, db)
    mixed_ref[...] = (y[...] * valid_ref[...]).astype(BF16)
    for i, (src, dst) in enumerate(outs):
        pltpu.make_async_copy(src, dst, out_sem.at[i]).wait()


def forward(block, tokens, tokens3, grad_out, valid, norm_params, lines):
    panels, rows, wide = block.shape
    tok_dev = tokens.shape[0]
    raw = raw_devices(tok_dev) * tok_dev
    comp = comp_devices(tok_dev, 2 * lines) * (tok_dev // 3)
    dma = pltpu.SemaphoreType.DMA
    shapes = [
        ((raw, D), BF16), ((comp, D), BF16), ((tok_dev, D), BF16), ((raw, D), BF16),
        ((raw, D), BF16), ((comp, D), BF16), ((comp, D), BF16), ((tok_dev, D), F32),
        ((tok_dev, FF), BF16), ((tok_dev, FF), BF16), ((tok_dev, D), BF16), ((tok_dev, D), F32),
        ((tok_dev, D), F32), ((3, tok_dev // 3, D), BF16),
    ]
    scratch = [pltpu.VMEM(shape, kind) for shape, kind in shapes]
    scratch.insert(1, scratch.pop())
    scratch.insert(len(scratch) - 1, pltpu.VMEM((tok_dev, D), F32))
    any_spec, vmem = pl.BlockSpec(memory_space=pl.ANY), pl.BlockSpec(memory_space=pltpu.VMEM)
    return pl.pallas_call(
        functools.partial(forward_kernel, panels, lines, 3),
        out_shape=[jax.ShapeDtypeStruct((panels, lines // 2, 2, 2, rows, D), BF16)]
        + [jax.ShapeDtypeStruct(shape, kind) for shape, kind in shapes]
        + [jax.ShapeDtypeStruct((HEADS, 8, tok_dev), F32), jax.ShapeDtypeStruct((tok_dev, D), BF16)],
        in_specs=[any_spec] + [vmem] * 5,
        out_specs=[any_spec] * (1 + len(shapes)) + [vmem] * 2,
        scratch_shapes=[pltpu.VMEM((4, lines // 2, 2, 2, rows, D), BF16)]
        + scratch
        + [
            dma(()),
            dma((panels, lines)), dma((panels, lines)),
            dma((panels, 2)), dma((panels, 2)),
            dma((panels, 2, 2)), dma((panels, 2, 2)),
            dma((panels, 2)), dma((panels, 2)),
            dma((4,)),
            dma((8,)), dma((8,)), dma((8,)), dma((8,)),
            dma((len(shapes),)),
        ],
        compiler_params=pltpu.CompilerParams(
            collective_id=0, has_side_effects=True, vmem_limit_bytes=58 * MIB
        ),
        name="forward",
    )(block, tokens, tokens3, grad_out, valid, norm_params)


RETURN = [4 + RATIO + _i for _i in range(RATIO)] + [4 + _i for _i in range(RATIO)] + [3, 0, 1, 2] + TAPS
RING = 3
HELD = 5
BACK_LAG = 4


def norm_back(grad, values, params, first):
    mean = row_sum(values) * (1.0 / D)
    centered = values - mean
    scale = lax.rsqrt(row_sum(centered * centered) * (1.0 / D) + NORM_EPS)
    unit = centered * scale
    inner = grad * params[first : first + 1, :]
    back = inner - row_sum(inner) * (1.0 / D) - unit * (row_sum(inner * unit) * (1.0 / D))
    gain = jnp.sum(grad * unit, axis=0, keepdims=True)
    return back * scale, gain, jnp.sum(grad, axis=0, keepdims=True)


def attend_head_back(
    seq, tok_dev, cols, q, do, o, kr, vr, kc, vc, lse, lse_row, dkr, dvr, dkc, dvc,
    acc_kr, acc_vr, acc_kc, acc_vc,
):
    scale = HEAD_DIM ** (-0.5)
    for acc in (acc_kr, acc_vr, acc_kc, acc_vc):
        acc[...] = jnp.zeros_like(acc)
    for i in range(tok_dev // QB):
        at = Attention(seq, i, tok_dev, kr.shape[0], kc.shape[0])
        query = q[at.rows, cols]
        grad = do[at.rows, cols]
        delta = row_sum(grad.astype(F32) * o[at.rows, cols])
        delta = jnp.broadcast_to(delta, (QB, QB)).T[0:1]
        stat = lse[lse_row, 0:1, at.rows]

        def part(k_ref, v_ref, acc_k, acc_v, keys, seen):
            k = k_ref[keys, :]
            s = times_transposed(k, query) * scale
            p = jnp.where(seen, jnp.exp(jnp.where(seen, s, NEG_SCORE) - stat), 0.0)
            dp = times_transposed(v_ref[keys, :], grad)
            ds = (p * (dp - delta)).astype(BF16)
            acc_v[keys, :] += matmul(p.astype(BF16), grad)
            acc_k[keys, :] += matmul(ds, query)
            return contract_rows(ds, k)

        dq = part(kr, vr, acc_kr, acc_vr, at.raw, at.sees_raw((RAW_KEYS, QB), 0))
        seen = at.sees_comp((COMP_KEYS, QB), 0)
        dq = dq + part(kc, vc, acc_kc, acc_vc, at.comp, seen)
        q[at.rows, cols] = (dq * scale).astype(BF16)
    dkr[:, cols] = (acc_kr[...] * scale).astype(BF16)
    dkc[:, cols] = (acc_kc[...] * scale).astype(BF16)
    dvr[:, cols] = acc_vr[...].astype(BF16)
    dvc[:, cols] = acc_vc[...].astype(BF16)


def backward_kernel(
    panels, lines,
    full_ref, a_hbm, c_hbm, a3_hbm, q_hbm, kr_hbm, vr_hbm, kc_hbm, vc_hbm, o_hbm, z_hbm, df_hbm,
    b_hbm, h_hbm, db_hbm, dy_hbm, tok_hbm, lse_ref, norm_ref,
    out_ref, in_grad_out, norm_out,
    held, cross_in, first_in, second_in, line_in,
    opnd, lhs_t, c_win, a3, h, db, o, pair, q, kr, vr, kc, vc, acc_kr, acc_vr, acc_kc, acc_vc,
    dkr, dvr, dkc, dvc, wbuf, dc, dc_in, da_in, n_src, n_in, n_line,
    cs, cr, s1, r1, s2, r2, zs, zr, free_cross, free_first, free_second,
    lsem, osem, hsem, wsem, dcs, dcr, das, dar, ns, nr, nzs, nzr,
):
    at = Place(lines)
    seq = at.seq
    seq_count = 2 * lines
    tok_dev = q.shape[0]
    comp_dev = tok_dev // 3
    raw_devs = dkr.shape[0] // tok_dev
    comp_devs = dkc.shape[0] // comp_dev
    reach = min(seq_count - 1, (2 * S + 3 * CM + tok_dev - 1) // tok_dev)
    wide = out_ref.shape[-1]
    rows_dev = out_ref.shape[1]
    pairs = lines // 2
    params = norm_ref[...]
    block = [pl.ds(i * tok_dev, tok_dev) for i in range(raw_devs)]
    dhb, do = pair.at[block[0], :], pair.at[block[1], :]

    def cross(p):
        src = held.at[lax.rem(p, HELD), :, :, 1 - at.core]
        slot = lax.rem(p, RING)
        return remote(src, cross_in.at[slot], cs.at[slot], cr.at[slot], at.core_dev)

    def mine(p):
        return held.at[lax.rem(p, HELD), :, :, at.core]

    def first(p, half):
        slot = lax.rem(p, RING)
        if half == 0:
            src, device = mine(p).at[:, 0, 1 - at.row], at.y_dev
        else:
            src, device = mine(p).at[:, 1, :, 1 - at.col], at.x_dev
        return remote(src, first_in.at[slot, half], s1.at[slot, half], r1.at[slot, half], device)

    def second(p, half):
        slot = lax.rem(p, RING)
        if half == 0:
            src, device = mine(p).at[:, 0, at.row, 1 - at.col], at.x_dev
        else:
            src, device = mine(p).at[:, 1, 1 - at.row, at.col], at.y_dev
        return remote(src, second_in.at[slot, half], s2.at[slot, half], r2.at[slot, half], device)

    def line_copy(p, k):
        line = at.other_line(k)
        src = mine(p).at[line // 2, line % 2, at.row, at.col]
        return remote(src, line_in.at[p, at.line], zs.at[p, k], zr.at[p, at.line], at.line_dev(k))

    def line_arrival(p, k):
        line = at.other_line(k)
        src = mine(p).at[line // 2, line % 2, at.row, at.col]
        return remote(src, line_in.at[p, line], zs.at[p, k], zr.at[p, line], at.line_dev(k))

    def give(semaphore, device):
        pl.semaphore_signal(semaphore, inc=1, device_id=device, device_id_type=MESH)

    def add(dst, src):
        dst[...] = (dst[...].astype(F32) + src[...].astype(F32)).astype(BF16)

    def start_first(p):
        cross(p).wait_recv()
        for half in (0, 1):
            for i in range(pairs):
                for g in range(4):
                    add(
                        mine(p).at[i, half, g // 2, g % 2],
                        cross_in.at[lax.rem(p, RING), i, half, g // 2, g % 2],
                    )
            pl.when(p >= RING)(lambda half=half: pl.semaphore_wait(free_first.at[half], 1))
            first(p, half).start()
        cross(p).wait_send()
        pl.when(p + RING < panels)(lambda: give(free_cross, at.core_dev))

    def start_second(p):
        slot = lax.rem(p, RING)
        for half in (0, 1):
            first(p, half).wait_recv()
            for i in range(pairs):
                for j in (0, 1):
                    row, col = (at.row, j) if half == 0 else (j, at.col)
                    add(mine(p).at[i, half, row, col], first_in.at[slot, half, i, j])
            pl.when(p >= RING)(lambda half=half: pl.semaphore_wait(free_second.at[half], 1))
            second(p, half).start()
            first(p, half).wait_send()
            device = at.y_dev if half == 0 else at.x_dev
            pl.when(p + RING < panels)(
                lambda half=half, device=device: give(free_first.at[half], device)
            )

    def start_lines(p):
        slot = lax.rem(p, RING)
        for half in (0, 1):
            second(p, half).wait_recv()
            for i in range(pairs):
                add(mine(p).at[i, half, at.row, at.col], second_in.at[slot, half, i])
            second(p, half).wait_send()
            device = at.x_dev if half == 0 else at.y_dev
            pl.when(p + RING < panels)(
                lambda half=half, device=device: give(free_second.at[half], device)
            )
        for k in range(1, lines):
            line_copy(p, k).start()

    def finish(p):
        total = mine(p)[at.line // 2, at.line % 2, at.row, at.col].astype(F32)
        for k in range(1, lines):
            line_arrival(p, k).wait_recv()
            total = total + line_in[p, at.other_line(k)].astype(F32)
        out_ref[p] = total.astype(BF16)
        for k in range(1, lines):
            line_copy(p, k).wait_send()

    def produce(p, *terms):
        slot = lax.rem(p, HELD)
        lefts = []
        for left, right in terms:
            rows = left.shape[0]
            lhs_t[:, pl.ds(0, rows)] = left[...].astype(BF16).T

            def columns(j, carry, right=right, rows=rows):
                col = pl.ds(pl.multiple_of(j * wide, wide), wide)
                total = matmul(lhs_t[:, pl.ds(0, rows)], right[:, col])
                total = total.reshape(pairs, 2, 2, rows_dev, wide)
                place = held.at[slot, :, :, :, j // 2, j % 2]
                if len(lefts) > 0:
                    total = total + place[...].astype(F32)
                place[...] = total.astype(BF16)
                return carry

            lax.fori_loop(0, 4, columns, 0)
            lefts.append(left)
        pl.when(p >= RING)(lambda: pl.semaphore_wait(free_cross, 1))
        cross(p).start()

    def left_load(p):
        rows = block[2] if p % 2 == 0 else block[3]
        src = z_hbm if p < RATIO else df_hbm
        place = opnd.at[rows, :]
        units = pl.ds((p % RATIO) * D, D)
        return pltpu.make_async_copy(src.at[:, units], place, lsem.at[p % 2])

    early = [
        (dy_hbm, opnd.at[block[0], :]), (b_hbm, opnd.at[block[1], :]), (h_hbm, h), (db_hbm, db),
        (o_hbm, o), (q_hbm, q), (c_hbm, c_win), (a3_hbm, a3),
    ]

    def early_load(i):
        return pltpu.make_async_copy(early[i][0], early[i][1], osem.at[i])

    def late_load(i):
        if i == 0:
            return pltpu.make_async_copy(a_hbm, opnd, osem.at[len(early)])
        if i == 1:
            return pltpu.make_async_copy(tok_hbm, dhb, osem.at[len(early) + 1])
        return pltpu.make_async_copy(h, in_grad_out, osem.at[len(early) + 2])

    def head_loads(i):
        col = pl.ds(pl.multiple_of(i * HEAD_DIM, HEAD_DIM), HEAD_DIM)
        refs = [(kr_hbm, kr), (vr_hbm, vr), (kc_hbm, kc), (vc_hbm, vc)]
        return [
            pltpu.make_async_copy(src.at[:, col], dst, hsem.at[j])
            for j, (src, dst) in enumerate(refs)
        ]

    def weight_load(panel, slot):
        return pltpu.make_async_copy(full_ref.at[panel], wbuf.at[slot], wsem.at[slot])

    def weight(slot):
        return wbuf[slot].reshape(D, D)

    def seq_dev(d):
        return {"grp": at.grp, "seq": lax.rem(seq + d + seq_count, seq_count)}

    def comp_rows(reader, owner):
        place = jnp.clip(owner - comp_window_first(reader, tok_dev), 0, comp_devs - 1)
        return pair.at[pl.ds(pl.multiple_of(place * comp_dev, comp_dev), comp_dev), :]

    def dc_copy(d):
        return remote(comp_rows(seq, seq - d), dc_in.at[d - 1], dcs.at[d], dcr.at[d], seq_dev(-d))

    def da_copy(d):
        src = dkr.at[block[raw_devs - 1 - d], :]
        return remote(src, da_in.at[d - 1], das.at[d], dar.at[d], seq_dev(-d))

    def reads_comp(d):
        return needs_comp(seq, seq - d, tok_dev)

    def read_comp(d):
        return (seq + d < seq_count) & needs_comp(seq + d, seq, tok_dev)

    def reads_raw(d):
        return needs_raw(seq, seq - d, tok_dev)

    def read_raw(d):
        return (seq + d < seq_count) & needs_raw(seq + d, seq, tok_dev)

    def norm_copy(i):
        device = (at.core_dev, at.x_dev, at.y_dev)[i]
        return remote(n_src.at[i], n_in.at[i], ns.at[i], nr.at[i], device)

    def norm_line(k):
        return remote(n_src.at[3], n_line.at[at.line], nzs.at[k], nzr.at[at.line], at.line_dev(k))

    def norm_line_arrival(k):
        line = at.other_line(k)
        return remote(n_src.at[3], n_line.at[line], nzs.at[k], nzr.at[line], at.line_dev(k))

    def second_norm_back():
        gains, shifts = [], []
        for i in range(tok_dev // QB):
            rows = pl.ds(i * QB, QB)
            back, gain, shift = norm_back(db[rows, :], h[rows, :], params, 2)
            db[rows, :] = opnd[rows, :].astype(F32) + back
            dhb[rows, :] = db[rows, :].astype(BF16)
            gains.append(gain)
            shifts.append(shift)
        n_src[0, 2:3, :] = sum(gains)
        n_src[0, 3:4, :] = sum(shifts)
        do[...] = times_transposed(dhb[...], weight(0)).astype(BF16)

    def work(t):
        @pl.when(t == 0)
        def _():
            for i in range(2, 6):
                early_load(i).wait()
            weight_load(6, 0).wait()
            second_norm_back()
            weight_load(5, 0).start()

        @pl.when((t >= 1) & (t <= HEADS))
        def _():
            for copy in head_loads(t - 1):
                copy.wait()
            cols = pl.ds(pl.multiple_of((t - 1) * HEAD_DIM, HEAD_DIM), HEAD_DIM)
            attend_head_back(
                seq, tok_dev, cols, q, do, o, kr, vr, kc, vc, lse_ref, t - 1, dkr, dvr, dkc, dvc,
                acc_kr, acc_vr, acc_kc, acc_vc,
            )

            @pl.when(t < HEADS)
            def _():
                for copy in head_loads(t):
                    copy.start()

        @pl.when(t == HEADS + 1)
        def _():
            weight_load(3, 1).wait()
            weight_load(4, 2).wait()
            half = pair.shape[0] // 2
            for i in range(2):
                rows = pl.ds(i * half, half)
                total = times_transposed(dkc[rows, :], weight(1))
                total = total + times_transposed(dvc[rows, :], weight(2))
                pair[rows, :] = total.astype(BF16)
            for d in range(1, reach + 1):
                pl.when(reads_comp(d))(lambda d=d: dc_copy(d).start())

        @pl.when(t == HEADS + 2)
        def _():
            weight_load(5, 0).wait()
            h[...] = times_transposed(q[...], weight(0))
            weight_load(0, 0).start()

        @pl.when(t == HEADS + 4)
        def _():
            for i in range(raw_devs):
                total = times_transposed(dkr[block[i], :], weight(1))
                total = total + times_transposed(dvr[block[i], :], weight(2))
                if i < raw_devs - 1:
                    dkr[block[i], :] = total.astype(BF16)
                    d = raw_devs - 1 - i
                    pl.when(reads_raw(d))(lambda d=d: da_copy(d).start())
                else:
                    h[...] += total
            weight_load(1, 1).start()
            weight_load(2, 2).start()

        @pl.when(t == HEADS + 5)
        def _():
            weight_load(0, 0).wait()
            weight_load(1, 1).wait()
            weight_load(2, 2).wait()
            heads_of = acc_kr.shape[0] // tok_dev
            for k in range(3):
                total = times_transposed(dc[...], weight(k))
                for c in range(HEADS):
                    acc = (acc_kr, acc_vr)[c // heads_of]
                    place = pl.ds(c % heads_of * tok_dev + k, comp_dev, stride=3)
                    acc[place, :] = total[:, c * HEAD_DIM : (c + 1) * HEAD_DIM]
            for c in range(HEADS):
                acc = (acc_kr, acc_vr)[c // heads_of]
                cols = pl.ds(c * HEAD_DIM, HEAD_DIM)
                h[:, cols] += acc[pl.ds(c % heads_of * tok_dev, tok_dev), :]
            for d in range(1, reach + 1):
                pl.when(reads_comp(d))(lambda d=d: dc_copy(d).wait_send())
            late_load(1).start()

        @pl.when(t == HEADS + 6)
        def _():
            for d in range(1, raw_devs):

                @pl.when(read_raw(d))
                def _(d=d):
                    da_copy(d).wait_recv()
                    h[...] += da_in[d - 1].astype(F32)

                pl.when(reads_raw(d))(lambda d=d: da_copy(d).wait_send())
            late_load(1).wait()
            gains, shifts = [], []
            for i in range(tok_dev // QB):
                rows = pl.ds(i * QB, QB)
                x = dhb[rows, :].astype(F32)
                back, gain, shift = norm_back(h[rows, :], x, params, 0)
                h[rows, :] = db[rows, :] + back
                gains.append(gain)
                shifts.append(shift)
            n_src[0, 0:1, :] = sum(gains)
            n_src[0, 1:2, :] = sum(shifts)
            norm_copy(0).start()
            late_load(2).start()

        @pl.when(t == HEADS + 7)
        def _():
            norm_copy(0).wait_recv()
            n_src[1] = n_src[0] + n_in[0]
            norm_copy(1).start()

        @pl.when(t == HEADS + 8)
        def _():
            norm_copy(1).wait_recv()
            n_src[2] = n_src[1] + n_in[1]
            norm_copy(2).start()

        @pl.when(t == HEADS + 9)
        def _():
            norm_copy(2).wait_recv()
            n_src[3] = n_src[2] + n_in[2]
            n_line[at.line] = n_src[3]
            for k in range(1, lines):
                norm_line(k).start()

    def make(t):
        for p in range(2 * RATIO):

            @pl.when(t == p)
            def _(p=p):
                if p + 1 < 2 * RATIO:
                    left_load(p + 1).start()
                left_load(p).wait()
                right = 0 if p < RATIO else 1
                if p == right * RATIO:
                    early_load(right).wait()
                produce(t, (opnd.at[block[2 + p % 2], :], opnd.at[block[right], :]))
                if p + 1 == 2 * RATIO:
                    late_load(0).start()

        pl.when(t == 8)(lambda: produce(t, (o, dhb)))

        @pl.when(t == 9)
        def _():
            late_load(0).wait()
            early_load(6).wait()
            early_load(7).wait()
            produce(t, (opnd.at[block[raw_devs - 1], :], q))

        def window(dr, dcomp):
            terms = [(opnd.at[rows, :], dr.at[rows, :]) for rows in block]
            comp = [pl.ds(i * tok_dev, tok_dev) for i in range(dcomp.shape[0] // tok_dev)]
            terms = terms + [(c_win.at[rows, :], dcomp.at[rows, :]) for rows in comp]
            produce(t, *terms)

        pl.when(t == 10)(lambda: window(dkr, dkc))
        pl.when(t == 11)(lambda: window(dvr, dvc))

        @pl.when(t == 12)
        def _():
            acc = lhs_t
            h_dc = o.at[pl.ds(0, comp_dev), :]
            h_dc[...] = jnp.zeros_like(h_dc)
            for d in range(1, reach + 1):

                @pl.when(read_comp(d))
                def _(d=d):
                    dc_copy(d).wait_recv()
                    h_dc[...] += dc_in[d - 1].astype(F32)

            dc[...] = h_dc[...].astype(BF16)

        for k in range(3):
            pl.when(t == 12 + k)(lambda k=k: produce(t, (a3.at[k], dc)))

    for i in range(len(early)):
        early_load(i).start()
    left_load(0).start()
    for panel, slot in ((6, 0), (3, 1), (4, 2)):
        weight_load(panel, slot).start()
    for copy in head_loads(0):
        copy.start()
    barrier = pltpu.get_barrier_semaphore()
    partners = [seq_dev(d) for d in range(1, seq_count)] + [at.x_dev, at.y_dev]
    for device in partners:
        pl.semaphore_signal(barrier, inc=1, device_id=device, device_id_type=MESH)
    pl.semaphore_wait(barrier, seq_count + 1)

    def step(t, carry):
        pl.when((t >= 1) & (t < panels + 1))(lambda: start_first(t - 1))
        pl.when((t >= 2) & (t < panels + 2))(lambda: start_second(t - 2))
        pl.when((t >= 3) & (t < panels + 3))(lambda: start_lines(t - 3))
        pl.when(t >= BACK_LAG)(lambda: finish(t - BACK_LAG))
        pl.when(t < panels)(lambda: make(t))
        work(t)
        return carry

    lax.fori_loop(0, panels + BACK_LAG, step, 0)
    for i in range(3):
        norm_copy(i).wait_send()
    for k in range(1, lines):
        norm_line_arrival(k).wait_recv()
        norm_line(k).wait_send()
    total = n_line[0]
    for i in range(1, lines):
        total = total + n_line[i]
    norm_out[...] = total
    late_load(2).wait()


def backward(weights, arrays, lse, norm_params, lines):
    panels, rows = weights.shape[0], weights.shape[4]
    wide, pairs, seq_count = D // 4, lines // 2, 2 * lines
    a_win, c_win = arrays[0], arrays[1]
    tok_dev = arrays[3].shape[0]
    raw, comp, comp_dev = a_win.shape[0], c_win.shape[0], tok_dev // 3
    raw_devs = raw // tok_dev
    reach = min(seq_count - 1, (2 * S + 3 * CM + tok_dev - 1) // tok_dev)
    dma = pltpu.SemaphoreType.DMA
    regular = pltpu.SemaphoreType.REGULAR
    any_spec, vmem = pl.BlockSpec(memory_space=pl.ANY), pl.BlockSpec(memory_space=pltpu.VMEM)

    def buffer(kind, *shape):
        return pltpu.VMEM(shape, kind)

    return pl.pallas_call(
        functools.partial(backward_kernel, panels, lines),
        out_shape=[
            jax.ShapeDtypeStruct((panels, rows, wide), BF16),
            jax.ShapeDtypeStruct((tok_dev, D), F32),
            jax.ShapeDtypeStruct((4, D), F32),
        ],
        in_specs=[any_spec] * (1 + len(arrays)) + [vmem] * 2,
        out_specs=[vmem, any_spec, vmem],
        scratch_shapes=[
            buffer(BF16, HELD, pairs, 2, 2, 2, 2, rows, wide),
            buffer(BF16, RING, pairs, 2, 2, 2, rows, wide),
            buffer(BF16, RING, 2, pairs, 2, rows, wide),
            buffer(BF16, RING, 2, pairs, rows, wide),
            buffer(BF16, panels, lines, rows, wide),
            buffer(BF16, raw, D),
            buffer(BF16, D, tok_dev),
            buffer(BF16, comp, D),
            buffer(BF16, 3, comp_dev, D),
            buffer(F32, tok_dev, D),
            buffer(F32, tok_dev, D),
            buffer(F32, tok_dev, D),
            buffer(BF16, max(comp, 2 * tok_dev), D),
            buffer(BF16, tok_dev, D),
            buffer(BF16, raw, HEAD_DIM),
            buffer(BF16, raw, HEAD_DIM),
            buffer(BF16, comp, HEAD_DIM),
            buffer(BF16, comp, HEAD_DIM),
            buffer(F32, raw, HEAD_DIM),
            buffer(F32, raw, HEAD_DIM),
            buffer(F32, comp, HEAD_DIM),
            buffer(F32, comp, HEAD_DIM),
            buffer(BF16, raw, D),
            buffer(BF16, raw, D),
            buffer(BF16, comp, D),
            buffer(BF16, comp, D),
            buffer(BF16, 3, pairs, 2, 2, rows, D),
            buffer(BF16, comp_dev, D),
            buffer(BF16, reach, comp_dev, D),
            buffer(BF16, raw_devs - 1, tok_dev, D),
            buffer(F32, 4, 4, D),
            buffer(F32, 3, 4, D),
            buffer(F32, lines, 4, D),
            dma((RING,)), dma((RING,)),
            dma((RING, 2)), dma((RING, 2)),
            dma((RING, 2)), dma((RING, 2)),
            dma((panels, lines)), dma((panels, lines)),
            regular, regular((2,)), regular((2,)),
            dma((2,)), dma((11,)), dma((4,)), dma((3,)),
            dma((reach + 1,)), dma((reach + 1,)),
            dma((raw_devs,)), dma((raw_devs,)),
            dma((3,)), dma((3,)),
            dma((lines,)), dma((lines,)),
        ],
        compiler_params=pltpu.CompilerParams(
            collective_id=1, has_side_effects=True, vmem_limit_bytes=62 * MIB
        ),
        name="backward",
    )(weights, *arrays, lse, norm_params)


def local(
    tokens, cotangent, master, first_moment, second_moment, norm_params, norm_first, norm_second,
    seg_valid, book_of_group, panel_slot,
):
    seq_count = lax.axis_size("seq")
    group_count = lax.axis_size("grp")
    seq_index = lax.axis_index("seq")
    group_index = lax.axis_index("grp")
    lines = seq_count // 2
    tok_dev = tokens.shape[0]
    slot_count, slot_rows = master.shape[0], master.shape[1]
    all_slots = slot_count * group_count
    comp_dev = tok_dev // 3
    wide = D // group_count

    slot_ids = jnp.arange(all_slots, dtype=jnp.int32)
    is_panel = panel_slot[None, :] == slot_ids[:, None]
    slot_used = jnp.any(is_panel, 1)
    slot_panel = jnp.argmax(is_panel, 1).astype(jnp.int32)
    scale_all = jnp.sum(jnp.where(is_panel, panel_deviations()[None, :], 0.0), 1)
    slot_scale = lax.dynamic_slice_in_dim(scale_all, group_index * slot_count, slot_count, 0)
    scaled = (master * slot_scale[:, None, None]).astype(BF16)
    scaled = scaled.reshape(slot_count, slot_rows, group_count, wide).transpose(2, 0, 1, 3)
    slots_in = lax.all_to_all(scaled, "grp", 0, 0, tiled=True)
    block = slots_in.reshape(all_slots, slot_rows, wide)[panel_slot[jnp.array(ARRIVAL)]]

    positions = seq_index * tok_dev + jnp.arange(tok_dev, dtype=jnp.int32)
    book_id = jnp.sum(jnp.where(jnp.arange(group_count) == group_index, book_of_group, 0))
    book_counts = jnp.sum(jnp.where((jnp.arange(group_count) == book_id)[:, None], seg_valid, 0), 0)
    segments = seg_valid.shape[1]
    row_counts = jnp.sum(
        jnp.where((positions // S)[:, None] == jnp.arange(segments)[None, :], book_counts[None, :], 0), 1
    )
    row_valid = (positions % S < row_counts).astype(F32)

    tokens3 = tokens.reshape(comp_dev, 3, D).transpose(1, 0, 2)
    grad_out = (cotangent.astype(F32) * row_valid[:, None]).astype(BF16)
    results = forward(block, tokens, tokens3, grad_out, row_valid[:, None], norm_params, lines)
    weights, saved, log_total, mixed = results[0], results[1:-2], results[-2], results[-1]
    a_win, c_win, q, kr, vr, kc, vc, o, z, df, b, h, db, a3 = saved
    arrays = (a_win, c_win, a3, q, kr, vr, kc, vc, o, z, df, b, h, db, grad_out, tokens)
    row_grads, input_grad, norm_grad = backward(weights, arrays, log_total, norm_params, lines)

    place = jnp.argsort(jnp.array(RETURN, jnp.int32))
    slotted = row_grads[place[slot_panel]].astype(F32) * scale_all[:, None, None]
    slotted = jnp.where(slot_used[:, None, None], slotted, 0.0).astype(BF16)
    slotted = slotted.reshape(group_count, slot_count, slot_rows, wide)
    slot_parts = lax.all_to_all(slotted, "grp", 0, 0, tiled=True)
    slot_grad = slot_parts.transpose(1, 2, 0, 3).reshape(slot_count, slot_rows, D).astype(F32)
    slot_first, slot_second, slot_weight = adam_update(
        slot_grad, first_moment, second_moment, master, SLOT_RATE
    )
    norm_first_new, norm_second_all, norm_weight = adam_update(
        norm_grad, norm_first, norm_second, norm_params, NORM_RATE
    )
    return (
        mixed, input_grad, slot_grad, slot_first, slot_second, slot_weight, norm_grad,
        norm_first_new, norm_second_all[:2], norm_second_all[2:], norm_weight,
    )


def solution(mesh):
    rows, slots, whole = P(("grp", "seq"), None), P("grp", "seq", None), P()
    return jax.shard_map(
        local,
        mesh=mesh,
        in_specs=(rows, rows, slots, slots, slots) + (whole,) * 6,
        out_specs=(rows, rows, slots, slots, slots, slots) + (whole,) * 5,
        check_vma=False,
    )
```

```python
import functools

import jax
import jax.numpy as jnp
from jax import lax
from jax.experimental import pallas as pl
from jax.experimental.pallas import tpu as pltpu
from jax.sharding import PartitionSpec as P

D = 1024
HEADS = 8
HEAD_DIM = 128
FF = 4096
S = 512
CM = 512
STEP = 10
PANELS = 15
RATIO = FF // D
QB = 128
RAW_KEYS = 2 * S
COMP_KEYS = CM + QB
MIB = 1 << 20

NEG_SCORE = -1e30
NORM_EPS = 1e-05
BETA_ONE = 0.9
BETA_TWO = 0.999
WEIGHT_DECAY = 0.1
ADAM_EPS = 1e-08
NORM_RATE = 1.0
SLOT_RATE = 2.0
BF16 = jnp.bfloat16
F32 = jnp.float32
MESH = pl.DeviceIdType.MESH


def layer_norm(values, gain, shift):
    row_mean = jnp.mean(values, axis=-1, keepdims=True)
    centered = values - row_mean
    variance = jnp.mean(centered * centered, axis=-1, keepdims=True)
    return centered * lax.rsqrt(variance + NORM_EPS) * gain + shift


def panel_deviations():
    inner_dev = D ** (-0.5)
    deviations = [inner_dev] * 3 + [(D // (2 * S)) ** (-0.5)] + [inner_dev] * RATIO
    deviations = deviations + [FF ** (-0.5)] * RATIO + [(3 * D) ** (-0.5)] * 3
    return jnp.array(deviations, F32)


def adam_update(gradient, first_old, second_old, weight_old, step_rate):
    first_new = BETA_ONE * first_old + (1.0 - BETA_ONE) * gradient
    second_new = BETA_TWO * second_old + (1.0 - BETA_TWO) * gradient * gradient
    fix_one = 1.0 - BETA_ONE**STEP
    fix_two = 1.0 - BETA_TWO**STEP
    movement = first_new / fix_one / (jnp.sqrt(second_new / fix_two) + ADAM_EPS)
    return (first_new, second_new, weight_old - step_rate * (movement + WEIGHT_DECAY * weight_old))


def matmul(left, right):
    return jnp.dot(left, right, preferred_element_type=F32)


def times_transposed(left, right):
    return lax.dot_general(left, right, (((1,), (1,)), ((), ())), preferred_element_type=F32)


def contract_rows(left, right):
    return lax.dot_general(left, right, (((0,), (0,)), ((), ())), preferred_element_type=F32)


class Place:
    def __init__(self, lines):
        self.lines = lines
        self.grp = lax.axis_index("grp")
        self.seq = lax.axis_index("seq")
        self.line = self.seq // 2
        self.core = self.seq % 2
        self.row = self.grp // 2
        self.col = self.grp % 2
        self.grp_x = self.row * 2 + 1 - self.col
        self.grp_y = (1 - self.row) * 2 + self.col
        self.x_dev = {"grp": self.grp_x, "seq": self.seq}
        self.y_dev = {"grp": self.grp_y, "seq": self.seq}
        self.far_dev = {"grp": 3 - self.grp, "seq": self.seq}
        self.core_dev = {"grp": self.grp, "seq": self.line * 2 + 1 - self.core}

    def other_line(self, k):
        return lax.rem(self.line + k, self.lines)

    def line_dev(self, k):
        return {"grp": self.grp, "seq": self.other_line(k) * 2 + self.core}

    def seq_dev(self, d):
        count = 2 * self.lines
        return {"grp": self.grp, "seq": lax.rem(self.seq + d + count, count)}

    def announce(self):
        barrier = pltpu.get_barrier_semaphore()
        partners = [self.seq_dev(d) for d in range(1, 2 * self.lines)]
        for device in partners + [self.x_dev, self.y_dev, self.far_dev]:
            pl.semaphore_signal(barrier, inc=1, device_id=device, device_id_type=MESH)

    def enter(self):
        pl.semaphore_wait(pltpu.get_barrier_semaphore(), 2 * self.lines + 2)

    def exchange(self, parts, arrived, send, recv):
        count = parts.shape[0] // 4
        copies = []
        for i, device in enumerate((self.x_dev, self.y_dev, self.far_dev)):
            src = parts.at[pl.ds(device["grp"] * count, count)]
            dst = arrived.at[pl.ds(self.grp * count, count)]
            copies.append(remote(src, dst, send.at[i], recv.at[i], device))
        return copies


def remote(src, dst, send, recv, device):
    return pltpu.make_async_remote_copy(
        src_ref=src,
        dst_ref=dst,
        send_sem=send,
        recv_sem=recv,
        device_id=device,
        device_id_type=MESH,
    )


def memory_start(position):
    return (position // S - 1) * S


def comp_window_first(seq, tok_dev):
    return jnp.maximum(memory_start(seq * tok_dev) - 3 * CM, 0) // tok_dev


def raw_devices(tok_dev):
    return (RAW_KEYS - QB + tok_dev - 1) // tok_dev + 1


def comp_devices(tok_dev, seq_count):
    return min((3 * CM + S) // tok_dev + 1, seq_count)


def needs_raw(reader, owner, tok_dev):
    return (owner >= 0) & ((owner + 1) * tok_dev > memory_start(reader * tok_dev))


def needs_comp(reader, owner, tok_dev):
    last = jnp.maximum(memory_start(reader * tok_dev + tok_dev - 1), 0) // 3
    inside = (owner >= 0) & (owner >= comp_window_first(reader, tok_dev))
    return inside & (owner * (tok_dev // 3) < last)


def chip_needs_comp(reader, owner, tok_dev):
    even = reader // 2 * 2
    return needs_comp(even, owner, tok_dev) | needs_comp(even + 1, owner, tok_dev)


def chain_needs_comp(reader, owner, tok_dev, seq_count, reach):
    needed = chip_needs_comp(reader, owner, tok_dev)
    for ahead in range(2, reach + 1, 2):
        later = reader + ahead
        needed = needed | ((later < seq_count) & chip_needs_comp(later, owner, tok_dev))
    return needed & (owner >= 0) & (reader < seq_count)


def block_window(seq, i, tok_dev, raw_rows, comp_rows):
    position = seq * tok_dev + i * QB
    memory = memory_start(position)
    raw_base = (seq + 1) * tok_dev - raw_rows
    raw_at = jnp.minimum(memory - raw_base, raw_rows - RAW_KEYS)
    comp_end = jnp.maximum(memory, 0) // 3
    comp_low = jnp.maximum(comp_end - CM, 0)
    comp_base = comp_window_first(seq, tok_dev) * (tok_dev // 3)
    comp_at = jnp.minimum((comp_low - comp_base) // QB * QB, comp_rows - COMP_KEYS)
    return (
        position,
        pl.multiple_of(raw_at, QB),
        pl.multiple_of(comp_at, QB),
        raw_base + raw_at,
        comp_base + comp_at,
        memory,
        comp_low,
        comp_end,
    )


def row_sum(values):
    return jnp.sum(values, axis=1, keepdims=True)


def norm_rows(values, params, first):
    mean = row_sum(values) * (1.0 / D)
    centered = values - mean
    variance = row_sum(centered * centered) * (1.0 / D)
    gain, shift = params[first : first + 1, :], params[first + 1 : first + 2, :]
    return centered * lax.rsqrt(variance + NORM_EPS) * gain + shift


GELU_IN = (2.0 / 3.141592653589793) ** 0.5
GELU_CUBE = 0.044715


def gelu_pair(f):
    square = f * f
    t = jnp.tanh(GELU_IN * f * (1.0 + GELU_CUBE * square))
    half = 0.5 * (1.0 + t)
    slope = half + 0.5 * f * (1.0 - t * t) * (GELU_IN * (1.0 + 3.0 * GELU_CUBE * square))
    return f * half, slope


class Attention:
    def __init__(self, seq, i, tok_dev, raw_rows, comp_rows):
        place = block_window(seq, i, tok_dev, raw_rows, comp_rows)
        self.pos, raw_at, comp_at, self.raw_pos, self.comp_pos = place[:5]
        self.memory, self.comp_low, self.comp_end = place[5:]
        self.rows = pl.ds(i * QB, QB)
        self.raw = pl.ds(raw_at, RAW_KEYS)
        self.comp = pl.ds(comp_at, COMP_KEYS)

    def sees_raw(self, shape, key_dim):
        key_pos = self.raw_pos + lax.broadcasted_iota(jnp.int32, shape, key_dim)
        query_pos = self.pos + lax.broadcasted_iota(jnp.int32, shape, 1 - key_dim)
        return (key_pos >= jnp.maximum(self.memory, 0)) & (key_pos <= query_pos)

    def sees_comp(self, shape, key_dim):
        index = self.comp_pos + lax.broadcasted_iota(jnp.int32, shape, key_dim)
        return (index >= self.comp_low) & (index < self.comp_end)


def attend_head(seq, tok_dev, cols, q, kr, vr, kc, vc, out, lse, lse_row):
    scale = HEAD_DIM ** (-0.5)
    for i in range(tok_dev // QB):
        at = Attention(seq, i, tok_dev, kr.shape[0], kc.shape[0])
        query = q[at.rows, cols]
        raw = times_transposed(query, kr[at.raw, cols]) * scale
        raw = jnp.where(at.sees_raw(raw.shape, 1), raw, NEG_SCORE)
        comp = times_transposed(query, kc[at.comp, cols]) * scale
        comp = jnp.where(at.sees_comp(comp.shape, 1), comp, NEG_SCORE)
        top = jnp.maximum(
            jnp.max(raw, axis=1, keepdims=True), jnp.max(comp, axis=1, keepdims=True)
        )
        raw = jnp.exp(raw - top)
        comp = jnp.exp(comp - top)
        total = row_sum(raw) + row_sum(comp)
        mixed = matmul(raw.astype(BF16), vr[at.raw, cols])
        mixed = mixed + matmul(comp.astype(BF16), vc[at.comp, cols])
        out[at.rows, cols] = mixed / total
        stat = jnp.broadcast_to(top + jnp.log(total), (QB, QB))
        lse[lse_row, :, at.rows] = stat.T[:8]


TAPS = [4 + 2 * RATIO + i for i in range(3)]
ARRIVAL = TAPS + [0, 1, 2, 3]
for _i in range(RATIO):
    ARRIVAL = ARRIVAL + [4 + _i, 4 + RATIO + _i]
AHEAD = 4
LAG = 4
SEMS = 8
KEPT = 4


def forward_kernel(
    panels, lines,
    scale_ref, order_ref, master_ref, tok_ref, tok3_ref, dy_ref, valid_ref, norm_ref,
    full_ref, a_out, c_out, q_out, kr_out, vr_out, kc_out, vc_out, o_out, z_out, df_out, b_out,
    h_out, db_out, a3_out, lse_ref, mixed_ref,
    wbuf, a_win, a3, c_win, q, kr, vr, kc, vc, o, z, df, b, h, y, db, slots, slots_in, block,
    own_sem, zs, zr, s1, r1, s2, r2, cs, cr, wsem, a_s, a_r, c_s, c_r, f_s, f_r, es, er, out_sem,
):
    at = Place(lines)
    seq = at.seq
    seq_count = 2 * lines
    chunks = 2 * panels
    tok_dev = tok_ref.shape[0]
    comp_dev = tok_dev // 3
    raw_devs = a_win.shape[0] // tok_dev
    comp_devs = c_win.shape[0] // comp_dev
    reach = min(seq_count - 1, (2 * S + 3 * CM + tok_dev - 1) // tok_dev)
    wide = block.shape[-1]
    half_rows = block.shape[1] // 2

    def cols(g):
        return pl.ds(pl.multiple_of(g * wide, wide), wide)

    def rows_of(u):
        return pl.ds(pl.multiple_of(u % 2 * half_rows, half_rows), half_rows)

    def line_place(u, line):
        return full_ref.at[u // 2, line // 2, line % 2, at.core, rows_of(u), cols(at.grp)]

    def line_copy(u, k):
        src = block.at[u // 2, rows_of(u), :]
        return remote(src, line_place(u, at.line), zs.at[u, k], zr.at[u, at.line], at.line_dev(k))

    def line_arrival(u, k):
        src, line = block.at[u // 2, rows_of(u), :], at.other_line(k)
        return remote(src, line_place(u, line), zs.at[u, k], zr.at[u, line], at.line_dev(k))

    def part(u, half, g):
        return full_ref.at[u // 2, :, half, at.core, rows_of(u), cols(g)]

    def first(u, half, g):
        device, i = (at.x_dev if half == 0 else at.y_dev), u % SEMS
        return remote(part(u, half, g), part(u, half, g), s1.at[i, half], r1.at[i, half], device)

    def second(u, half, j, g):
        device, i = (at.y_dev if half == 0 else at.x_dev), u % SEMS
        ref = part(u, half, g)
        return remote(ref, ref, s2.at[i, half, j], r2.at[i, half, j], device)

    def cross(u, half, core):
        ref, i = full_ref.at[u // 2, :, half, core, rows_of(u)], u % SEMS
        return remote(ref, ref, cs.at[i, half], cr.at[i, half], at.core_dev)

    def load(u):
        src = full_ref.at[u // 2, :, :, :, rows_of(u)]
        dst = wbuf.at[u // 2 % KEPT, :, :, :, rows_of(u)]
        return pltpu.make_async_copy(src, dst, wsem.at[u % SEMS])

    def start_lines(u):
        for k in range(1, lines):
            line_copy(u, k).start()

    def start_first(u):
        for k in range(1, lines):
            line_arrival(u, k).wait_recv()
        for half in (0, 1):
            first(u, half, at.grp).start()

    def start_second(u):
        for half in (0, 1):
            near = at.grp_x if half == 0 else at.grp_y
            first(u, half, near).wait_recv()
            second(u, half, 0, at.grp).start()
            second(u, half, 1, near).start()

    def start_cross(u):
        for half in (0, 1):
            second(u, half, 0, at.grp_y if half == 0 else at.grp_x).wait_recv()
            second(u, half, 1, 3 - at.grp).wait_recv()
            cross(u, half, at.core).start()

    def finish(u):
        for half in (0, 1):
            cross(u, half, 1 - at.core).wait_recv()
            first(u, half, at.grp).wait_send()
            second(u, half, 0, at.grp).wait_send()
            second(u, half, 1, at.grp_x if half == 0 else at.grp_y).wait_send()
            cross(u, half, at.core).wait_send()
        for k in range(1, lines):
            line_copy(u, k).wait_send()
        load(u).start()

    def a_rows(d):
        return a_win.at[pl.ds((raw_devs - 1 - d) * tok_dev, tok_dev), :]

    def a_copy(d, place, i, device):
        return remote(a_rows(d), a_rows(place), a_s.at[i], a_r.at[place - 1], device)

    def a_next():
        return a_copy(0, 2, 0, at.seq_dev(2))

    def a_beside():
        return a_copy(0, 1, 1, at.core_dev)

    def a_on(place):
        return a_copy(2, place, 2, at.core_dev)

    odd = at.core == 1
    even = at.core == 0
    gives_next = (seq + 2 < seq_count) & needs_raw(seq + 2, seq, tok_dev)
    gives_beside = even & needs_raw(seq + 1, seq, tok_dev)
    gives_on_far = even & needs_raw(seq + 1, seq - 2, tok_dev)
    gives_on_near = odd & needs_raw(seq - 1, seq - 2, tok_dev)

    def c_rows(reader, owner):
        place = jnp.clip(owner - comp_window_first(reader, tok_dev), 0, comp_devs - 1)
        return c_win.at[pl.ds(pl.multiple_of(place * comp_dev, comp_dev), comp_dev), :]

    def c_from(d):
        return own_c if d == 0 else c_rows(seq, seq - d)

    def c_next(d):
        dst = c_rows(seq + 2, seq - d)
        return remote(c_from(d), dst, c_s.at[d // 2], c_r.at[d // 2 + 1], at.seq_dev(2))

    def c_arrival(d):
        return remote(own_c, c_rows(seq, seq - d), c_s.at[0], c_r.at[d // 2], at.seq_dev(2))

    def c_across(d):
        other = seq + 1 - 2 * at.core
        dst = c_rows(other, seq - d)
        return remote(c_from(d), dst, f_s.at[d // 2], f_r.at[d // 2], at.core_dev)

    def c_across_arrival(d):
        other = seq + 1 - 2 * at.core
        return remote(own_c, c_rows(seq, other - d), f_s.at[0], f_r.at[d // 2], at.core_dev)

    steps_back = [d for d in range(0, reach + 1, 2)]

    def gives_c(d):
        return chain_needs_comp(seq + 2, seq - d, tok_dev, seq_count, reach - 1)

    def takes_c(d):
        return chain_needs_comp(seq, seq - d, tok_dev, seq_count, reach - 1)

    def gives_c_across(d):
        return needs_comp(seq + 1 - 2 * at.core, seq - d, tok_dev)

    def takes_c_across(d):
        return needs_comp(seq, seq + 1 - 2 * at.core - d, tok_dev)

    def pass_c(d):
        if d > 0:
            pl.when(takes_c(d))(lambda: c_arrival(d).wait_recv())
        pl.when(gives_c(d))(lambda: c_next(d).start())
        pl.when(gives_c_across(d))(lambda: c_across(d).start())

    outs = [
        (a_win, a_out), (c_win, c_out), (q, q_out), (kr, kr_out), (vr, vr_out), (kc, kc_out),
        (vc, vc_out), (o, o_out), (z, z_out), (df, df_out), (b, b_out), (h, h_out), (db, db_out),
        (a3, a3_out),
    ]

    def flush(*names):
        for i, (src, dst) in enumerate(outs):
            if any(src is name for name in names):
                pltpu.make_async_copy(src, dst, out_sem.at[i]).start()

    at.announce()
    count = master_ref.shape[0]
    for j in range(count):
        scaled = (master_ref[j] * scale_ref[j]).astype(BF16)
        for g in range(4):
            slots[g * count + j] = scaled[:, g * wide : (g + 1) * wide]
    at.enter()
    handed = at.exchange(slots, slots_in, es, er)
    for copy in handed:
        copy.start()
    slots_in[pl.ds(at.grp * count, count)] = slots[pl.ds(at.grp * count, count)]

    params = norm_ref[...]
    for i in range(tok_dev // QB):
        rows = pl.ds(i * QB, QB)
        mine = norm_rows(tok_ref[rows, :].astype(F32), params, 0).astype(BF16)
        a_win[pl.ds((raw_devs - 1) * tok_dev + i * QB, QB), :] = mine
    pl.when(gives_next)(lambda: a_next().start())
    pl.when(gives_beside)(lambda: a_beside().start())
    for d in range(1, raw_devs):
        absent = jnp.logical_not(needs_raw(seq, seq - d, tok_dev))

        @pl.when(absent)
        def _(d=d):
            a_rows(d)[...] = jnp.zeros((tok_dev, D), BF16)

    for k in range(3):
        a3[k] = norm_rows(tok3_ref[k].astype(F32), params, 0).astype(BF16)
    for i in range(comp_devs):
        owner = comp_window_first(seq, tok_dev) + i
        taken = needs_comp(seq, owner, tok_dev)
        for d in steps_back[1:]:
            taken = taken | ((owner == seq - d) & takes_c(d))

        @pl.when(jnp.logical_not(taken))
        def _(i=i):
            c_win[pl.ds(i * comp_dev, comp_dev), :] = jnp.zeros((comp_dev, D), BF16)

    for copy in handed:
        copy.wait_recv()
    for p in range(panels):
        block[p] = slots_in[order_ref[p]]
    for u in range(AHEAD):
        start_lines(u)
    own_place = full_ref.at[:, at.line // 2, at.line % 2, at.core, :, cols(at.grp)]
    own = pltpu.make_async_copy(block, own_place, own_sem)
    own.start()
    own.wait()

    own_c = b.at[pl.ds(0, comp_dev), :]
    tile = 8 * half_rows

    def weight(slot, col):
        return wbuf[slot, :, :, :, :, col].reshape(D, wide)

    def columns(body):
        def one(j, carry):
            body(pl.ds(pl.multiple_of(j * wide, wide), wide))
            return carry

        lax.fori_loop(0, D // wide, one, 0)

    def tap(k, slot):
        def body(col):
            part_sum = matmul(a3[k], weight(slot, col))
            if k == 0:
                y[pl.ds(0, comp_dev), col] = part_sum
            elif k == 1:
                y[pl.ds(0, comp_dev), col] += part_sum
            else:
                own_c[:, col] = (y[pl.ds(0, comp_dev), col] + part_sum).astype(BF16)

        columns(body)

    def project(dst, src, slot):
        block_rows = min(src.shape[0], tok_dev)

        def body(col):
            for i in range(src.shape[0] // block_rows):
                rows = pl.ds(i * block_rows, block_rows)
                dst[rows, col] = matmul(src[rows, :], weight(slot, col)).astype(BF16)

        columns(body)

    def heads(low, high):
        def one(i, carry):
            col = pl.ds(pl.multiple_of(i * HEAD_DIM, HEAD_DIM), HEAD_DIM)
            attend_head(seq, tok_dev, col, q, kr, vr, kc, vc, o, lse_ref, i)
            return carry

        lax.fori_loop(low, high, one, 0)

    def hidden(pair, low, high):
        up, down = (2 * pair + 7) % KEPT, (2 * pair + 8) % KEPT

        def one(i, carry):
            up_rows = wbuf[up, i].reshape(tile, D)
            down_rows = wbuf[down, i].reshape(tile, D)
            value, slope = gelu_pair(times_transposed(b[...], up_rows))
            units = pl.ds(pl.multiple_of(pair * D + i * tile, tile), tile)
            z[:, units] = value.astype(BF16)
            df[:, units] = (times_transposed(dy_ref[...], down_rows) * slope).astype(BF16)
            return carry

        lax.fori_loop(low, high, one, 0)

    def gather_hidden(pair):
        up, down = (2 * pair + 7) % KEPT, (2 * pair + 8) % KEPT
        units = pl.ds(pl.multiple_of(pair * D, D), D)

        def body(col):
            y[:, col] += matmul(z[:, units], weight(down, col))
            db[:, col] += matmul(df[:, units], weight(up, col))

        columns(body)

    def work(w):
        slot = w // 2 % KEPT
        for k in range(3):
            pl.when(w == 2 * k)(lambda k=k: tap(k, slot))

        @pl.when(w == 1)
        def _():
            for copy in handed:
                copy.wait_send()
            pl.when(needs_raw(seq, seq - 2, tok_dev))(lambda: a_next().wait_recv())
            pl.when(gives_on_far)(lambda: a_on(3).start())
            pl.when(gives_on_near)(lambda: a_on(1).start())

        pl.when(w == 4)(lambda: pass_c(0))

        @pl.when(w == 5)
        def _():
            pl.when(even & needs_raw(seq, seq - 1, tok_dev))(lambda: a_on(1).wait_recv())
            pl.when(odd & needs_raw(seq, seq - 1, tok_dev))(lambda: a_beside().wait_recv())
            pl.when(needs_raw(seq, seq - 3, tok_dev))(lambda: a_on(3).wait_recv())
            pl.when(gives_next)(lambda: a_next().wait_send())
            pl.when(gives_beside)(lambda: a_beside().wait_send())
            pl.when(gives_on_far)(lambda: a_on(3).wait_send())
            pl.when(gives_on_near)(lambda: a_on(1).wait_send())
            flush(a_win, a3)

        @pl.when(w == 6)
        def _():
            project(q, a_win.at[pl.ds((raw_devs - 1) * tok_dev, tok_dev), :], slot)
            flush(q)

        for i, d in enumerate(steps_back[1:]):
            pl.when(w == 6 + 2 * i)(lambda d=d: pass_c(d))

        @pl.when(w == 8)
        def _():
            project(kr, a_win, slot)
            flush(kr)

        @pl.when(w == 10)
        def _():
            project(vr, a_win, slot)
            flush(vr)

        @pl.when(w == 12)
        def _():
            for d in steps_back:
                pl.when(takes_c_across(d))(lambda d=d: c_across_arrival(d).wait_recv())
            flush(c_win)
            project(kc, c_win, 4 % KEPT)
            project(vc, c_win, 5 % KEPT)
            flush(kc, vc)

        @pl.when((w >= 13) & (w < 17))
        def _():
            low = (w - 13) * (HEADS // 4)
            heads(low, low + HEADS // 4)

        @pl.when(w == 17)
        def _():
            flush(o)
            for d in steps_back:
                pl.when(gives_c(d))(lambda d=d: c_next(d).wait_send())
                pl.when(gives_c_across(d))(lambda d=d: c_across(d).wait_send())

            def body(col):
                sent = matmul(o[...].astype(BF16), weight(6 % KEPT, col))
                h[:, col] = tok_ref[:, col].astype(F32) + sent

            columns(body)
            for i in range(tok_dev // QB):
                rows = pl.ds(i * QB, QB)
                b[rows, :] = norm_rows(h[rows, :], params, 2).astype(BF16)
            y[...] = h[...]
            db[...] = jnp.zeros_like(db)
            flush(b, h)

        turn = w - 16
        lines_half = wbuf.shape[1] // 2
        first_turn = ((turn >= 4) & (turn % 4 == 0)) | (turn == 2)
        second_turn = ((turn >= 4) & (turn % 4 == 1)) | (turn == 3)
        pl.when(first_turn)(lambda: hidden(turn // 4, 0, lines_half))

        @pl.when(second_turn)
        def _():
            hidden(turn // 4, lines_half, 2 * lines_half)
            gather_hidden(turn // 4)

    def step(t, carry):
        pl.when(t + AHEAD < chunks)(lambda: start_lines(t + AHEAD))
        pl.when(t < chunks)(lambda: start_first(t))
        pl.when((t >= 1) & (t < chunks + 1))(lambda: start_second(t - 1))
        pl.when((t >= 2) & (t < chunks + 2))(lambda: start_cross(t - 2))

        pl.when((t >= LAG) & (t < chunks + LAG))(lambda: load(t - LAG).wait())
        pl.when(t >= LAG + 1)(lambda: work(t - LAG - 1))
        pl.when((t >= 3) & (t < chunks + 3))(lambda: finish(t - 3))
        return carry

    lax.fori_loop(0, chunks + LAG + 1, step, 0)
    flush(z, df, db)
    mixed_ref[...] = (y[...] * valid_ref[...]).astype(BF16)
    for i, (src, dst) in enumerate(outs):
        pltpu.make_async_copy(src, dst, out_sem.at[i]).wait()


def forward(scale, order, master, tokens, tokens3, grad_out, valid, norm_params, lines):
    panels, slot_count, rows = order.shape[0], master.shape[0], master.shape[1]
    wide = D // 4
    tok_dev = tokens.shape[0]
    raw = raw_devices(tok_dev) * tok_dev
    comp = comp_devices(tok_dev, 2 * lines) * (tok_dev // 3)
    dma = pltpu.SemaphoreType.DMA
    shapes = [
        ((raw, D), BF16), ((comp, D), BF16), ((tok_dev, D), BF16), ((raw, D), BF16),
        ((raw, D), BF16), ((comp, D), BF16), ((comp, D), BF16), ((tok_dev, D), F32),
        ((tok_dev, FF), BF16), ((tok_dev, FF), BF16), ((tok_dev, D), BF16), ((tok_dev, D), F32),
        ((tok_dev, D), F32), ((3, tok_dev // 3, D), BF16),
    ]
    scratch = [pltpu.VMEM(shape, kind) for shape, kind in shapes]
    scratch.insert(1, scratch.pop())
    scratch.insert(len(scratch) - 1, pltpu.VMEM((tok_dev, D), F32))
    any_spec, vmem = pl.BlockSpec(memory_space=pl.ANY), pl.BlockSpec(memory_space=pltpu.VMEM)
    smem = pl.BlockSpec(memory_space=pltpu.SMEM)
    return pl.pallas_call(
        functools.partial(forward_kernel, panels, lines),
        out_shape=[jax.ShapeDtypeStruct((panels, lines // 2, 2, 2, rows, D), BF16)]
        + [jax.ShapeDtypeStruct(shape, kind) for shape, kind in shapes]
        + [jax.ShapeDtypeStruct((HEADS, 8, tok_dev), F32), jax.ShapeDtypeStruct((tok_dev, D), BF16)],
        in_specs=[smem] * 2 + [vmem] * 6,
        out_specs=[any_spec] * (1 + len(shapes)) + [vmem] * 2,
        scratch_shapes=[pltpu.VMEM((KEPT, lines // 2, 2, 2, rows, D), BF16)]
        + scratch
        + [
            pltpu.VMEM((4 * slot_count, rows, wide), BF16),
            pltpu.VMEM((4 * slot_count, rows, wide), BF16),
            pltpu.VMEM((panels, rows, wide), BF16),
            dma(()),
            dma((2 * panels, lines)), dma((2 * panels, lines)),
            dma((SEMS, 2)), dma((SEMS, 2)),
            dma((SEMS, 2, 2)), dma((SEMS, 2, 2)),
            dma((SEMS, 2)), dma((SEMS, 2)),
            dma((SEMS,)),
            dma((3,)), dma((3,)), dma((5,)), dma((5,)), dma((5,)), dma((5,)),
            dma((3,)), dma((3,)),
            dma((len(shapes),)),
        ],
        compiler_params=pltpu.CompilerParams(
            collective_id=0, has_side_effects=True, vmem_limit_bytes=60 * MIB
        ),
        name="forward",
    )(scale, order, master, tokens, tokens3, grad_out, valid, norm_params)


RETURN = [4 + RATIO + _i for _i in range(RATIO)] + [4 + _i for _i in range(RATIO)] + [3, 0, 1, 2] + TAPS
RING = 4
HELD = 5
BACK_LAG = 4


def norm_back(grad, values, params, first):
    mean = row_sum(values) * (1.0 / D)
    centered = values - mean
    scale = lax.rsqrt(row_sum(centered * centered) * (1.0 / D) + NORM_EPS)
    unit = centered * scale
    inner = grad * params[first : first + 1, :]
    back = inner - row_sum(inner) * (1.0 / D) - unit * (row_sum(inner * unit) * (1.0 / D))
    gain = jnp.sum(grad * unit, axis=0, keepdims=True)
    return back * scale, gain, jnp.sum(grad, axis=0, keepdims=True)


def attend_head_back(
    seq, tok_dev, cols, q, do, o, kr, vr, kc, vc, lse, lse_row, dkr, dvr, dkc, dvc,
    acc_kr, acc_vr, acc_kc, acc_vc,
):
    scale = HEAD_DIM ** (-0.5)
    for acc in (acc_kr, acc_vr, acc_kc, acc_vc):
        acc[...] = jnp.zeros_like(acc)
    for i in range(tok_dev // QB):
        at = Attention(seq, i, tok_dev, kr.shape[0], kc.shape[0])
        query = q[at.rows, cols]
        grad = do[at.rows, cols]
        delta = row_sum(grad.astype(F32) * o[at.rows, cols])
        delta = jnp.broadcast_to(delta, (QB, QB)).T[0:1]
        stat = lse[lse_row, 0:1, at.rows]

        def part(k_ref, v_ref, acc_k, acc_v, keys, seen):
            k = k_ref[keys, :]
            s = times_transposed(k, query) * scale
            p = jnp.where(seen, jnp.exp(jnp.where(seen, s, NEG_SCORE) - stat), 0.0)
            dp = times_transposed(v_ref[keys, :], grad)
            ds = (p * (dp - delta)).astype(BF16)
            acc_v[keys, :] += matmul(p.astype(BF16), grad)
            acc_k[keys, :] += matmul(ds, query)
            return contract_rows(ds, k)

        dq = part(kr, vr, acc_kr, acc_vr, at.raw, at.sees_raw((RAW_KEYS, QB), 0))
        seen = at.sees_comp((COMP_KEYS, QB), 0)
        dq = dq + part(kc, vc, acc_kc, acc_vc, at.comp, seen)
        q[at.rows, cols] = (dq * scale).astype(BF16)
    dkr[:, cols] = (acc_kr[...] * scale).astype(BF16)
    dkc[:, cols] = (acc_kc[...] * scale).astype(BF16)
    dvr[:, cols] = acc_vr[...].astype(BF16)
    dvc[:, cols] = acc_vc[...].astype(BF16)


def backward_kernel(
    panels, lines,
    place_ref, slot_scale_ref,
    full_ref, a_hbm, c_hbm, a3_hbm, q_hbm, kr_hbm, vr_hbm, kc_hbm, vc_hbm, o_hbm, z_hbm, df_hbm,
    b_hbm, h_hbm, db_hbm, dy_hbm, tok_hbm, lse_ref, norm_ref,
    slot_out, in_grad_out, norm_out,
    held, cross_in, first_in, second_in, line_in, out, slots, slots_in,
    opnd, lhs_t, c_win, a3, h, db, o, pair, q, kr, vr, kc, vc, acc_kr, acc_vr, acc_kc, acc_vc,
    dkr, dvr, dkc, dvc, wbuf, dc, dc_beside, dc_chain, da_in, n_src, n_in, n_line,
    cs, cr, s1, r1, s2, r2, zs, zr, free_cross, free_first, free_second,
    lsem, osem, hsem, wsem, dbs, dbr, dcs, dcr, das, dar, ns, nr, nzs, nzr, es, er,
):
    at = Place(lines)
    seq = at.seq
    seq_count = 2 * lines
    chunks = 2 * panels
    tok_dev = q.shape[0]
    comp_dev = tok_dev // 3
    raw_devs = dkr.shape[0] // tok_dev
    comp_devs = dkc.shape[0] // comp_dev
    reach = min(seq_count - 1, (2 * S + 3 * CM + tok_dev - 1) // tok_dev)
    wide = out.shape[-1]
    half_rows = out.shape[1] // 2
    pairs = lines // 2
    params = norm_ref[...]
    raw, comp = dkr.shape[0], dkc.shape[0]

    def token_rows(i):
        return pl.ds(pl.multiple_of(i * tok_dev, tok_dev), tok_dev)

    dhb, do = pair.at[token_rows(0), :], pair.at[token_rows(1), :]

    def mine(u):
        return held.at[u % HELD, :, :, at.core]

    def cross(u):
        src, i = held.at[u % HELD, :, :, 1 - at.core], u % RING
        return remote(src, cross_in.at[i], cs.at[i], cr.at[i], at.core_dev)

    def first(u, half):
        i = u % RING
        if half == 0:
            src, device = mine(u).at[:, 0, 1 - at.row], at.y_dev
        else:
            src, device = mine(u).at[:, 1, :, 1 - at.col], at.x_dev
        return remote(src, first_in.at[i, half], s1.at[i, half], r1.at[i, half], device)

    def second(u, half):
        i = u % RING
        if half == 0:
            src, device = mine(u).at[:, 0, at.row, 1 - at.col], at.x_dev
        else:
            src, device = mine(u).at[:, 1, 1 - at.row, at.col], at.y_dev
        return remote(src, second_in.at[i, half], s2.at[i, half], r2.at[i, half], device)

    def line_copy(u, k):
        line = at.other_line(k)
        src = mine(u).at[line // 2, line % 2, at.row, at.col]
        return remote(src, line_in.at[u, at.line], zs.at[u, k], zr.at[u, at.line], at.line_dev(k))

    def line_arrival(u, k):
        line = at.other_line(k)
        src = mine(u).at[line // 2, line % 2, at.row, at.col]
        return remote(src, line_in.at[u, line], zs.at[u, k], zr.at[u, line], at.line_dev(k))

    def give(semaphore, device):
        pl.semaphore_signal(semaphore, inc=1, device_id=device, device_id_type=MESH)

    def add(dst, src):
        dst[...] = (dst[...].astype(F32) + src[...].astype(F32)).astype(BF16)

    def start_first(u):
        cross(u).wait_recv()
        for half in (0, 1):
            for i in range(pairs):
                for g in range(4):
                    add(
                        mine(u).at[i, half, g // 2, g % 2],
                        cross_in.at[u % RING, i, half, g // 2, g % 2],
                    )
            pl.when(u >= RING)(lambda half=half: pl.semaphore_wait(free_first.at[half], 1))
            first(u, half).start()
        cross(u).wait_send()
        pl.when(u + RING < chunks)(lambda: give(free_cross, at.core_dev))

    def start_second(u):
        for half in (0, 1):
            first(u, half).wait_recv()
            for i in range(pairs):
                for j in (0, 1):
                    row, col = (at.row, j) if half == 0 else (j, at.col)
                    add(mine(u).at[i, half, row, col], first_in.at[u % RING, half, i, j])
            pl.when(u >= RING)(lambda half=half: pl.semaphore_wait(free_second.at[half], 1))
            second(u, half).start()
            first(u, half).wait_send()
            device = at.y_dev if half == 0 else at.x_dev
            pl.when(u + RING < chunks)(
                lambda half=half, device=device: give(free_first.at[half], device)
            )

    def start_lines(u):
        for half in (0, 1):
            second(u, half).wait_recv()
            for i in range(pairs):
                add(mine(u).at[i, half, at.row, at.col], second_in.at[u % RING, half, i])
            second(u, half).wait_send()
            device = at.x_dev if half == 0 else at.y_dev
            pl.when(u + RING < chunks)(
                lambda half=half, device=device: give(free_second.at[half], device)
            )
        for k in range(1, lines):
            line_copy(u, k).start()

    def finish(u):
        total = mine(u)[at.line // 2, at.line % 2, at.row, at.col].astype(F32)
        for k in range(1, lines):
            line_arrival(u, k).wait_recv()
            total = total + line_in[u, at.other_line(k)].astype(F32)
        rows = pl.ds(pl.multiple_of(u % 2 * half_rows, half_rows), half_rows)
        out[u // 2, rows, :] = total.astype(BF16)
        for k in range(1, lines):
            line_copy(u, k).wait_send()

    def turn(left, first_row):
        turned = left[...].astype(BF16).T
        count = left.shape[0]
        turned = turned.reshape(2 * pairs, 2, 2, half_rows, count)
        lhs_t[:, :, :, :, pl.ds(first_row, count)] = turned

    def produce(u, *terms):
        def columns(j, carry):
            col = pl.ds(pl.multiple_of(j * wide, wide), wide)
            total = None
            for first_row, right in terms:
                count = right.shape[0]
                left = lhs_t[:, :, u % 2, :, pl.ds(first_row, count)].reshape(D // 2, count)
                term = matmul(left, right[:, col])
                total = term if total is None else total + term
            total = total.reshape(pairs, 2, 2, half_rows, wide)
            held[u % HELD, :, :, :, j // 2, j % 2] = total.astype(BF16)
            return carry

        lax.fori_loop(0, 4, columns, 0)
        pl.when(u >= RING)(lambda: pl.semaphore_wait(free_cross, 1))
        cross(u).start()

    def left_load(p, src):
        units = pl.ds(pl.multiple_of(p % RATIO * D, D), D)
        return pltpu.make_async_copy(src.at[:, units], opnd.at[token_rows(2 + p % 2), :], lsem.at[p % 2])

    def left_start(p):
        pl.when(p < RATIO)(lambda: left_load(p, z_hbm).start())
        pl.when(p >= RATIO)(lambda: left_load(p, df_hbm).start())

    early = [
        (dy_hbm, opnd.at[token_rows(0), :]), (b_hbm, opnd.at[token_rows(1), :]), (h_hbm, h),
        (db_hbm, db), (o_hbm, o), (q_hbm, q), (c_hbm, c_win), (a3_hbm, a3),
    ]

    def early_load(i):
        return pltpu.make_async_copy(early[i][0], early[i][1], osem.at[i])

    def late_load(i):
        src, dst = ((a_hbm, opnd), (tok_hbm, dhb), (h, in_grad_out))[i]
        return pltpu.make_async_copy(src, dst, osem.at[len(early) + i])

    def head_loads(i):
        col = pl.ds(pl.multiple_of(i * HEAD_DIM, HEAD_DIM), HEAD_DIM)
        refs = [(kr_hbm, kr), (vr_hbm, vr), (kc_hbm, kc), (vc_hbm, vc)]
        return [
            pltpu.make_async_copy(src.at[:, col], dst, hsem.at[j])
            for j, (src, dst) in enumerate(refs)
        ]

    def weight_load(panel, slot):
        return pltpu.make_async_copy(full_ref.at[panel], wbuf.at[slot], wsem.at[slot])

    def weight(slot):
        return wbuf[slot].reshape(D, D)

    other = seq + 1 - 2 * at.core

    def comp_rows(owner):
        place = jnp.clip(owner - comp_window_first(seq, tok_dev), 0, comp_devs - 1)
        return pair.at[pl.ds(pl.multiple_of(place * comp_dev, comp_dev), comp_dev), :]

    def dc_across(d):
        i = (d + 1) // 2 - at.core
        return remote(comp_rows(seq - d), dc_beside.at[i], dbs.at[d // 2], dbr.at[i], at.core_dev)

    def dc_join(d):
        i = d // 2

        @pl.when(needs_comp(other, seq - d, tok_dev))
        def _():
            remote(comp_rows(seq - d), dc_beside.at[i], dbs.at[0], dbr.at[i], at.core_dev).wait_recv()
            add(comp_rows(seq - d), dc_beside.at[i])

    def gives_back(d):
        return chain_needs_comp(seq, seq - d, tok_dev, seq_count, reach - 1)

    def takes_back(d):
        return chain_needs_comp(seq + 2, seq - d, tok_dev, seq_count, reach - 1)

    def dc_back(d):
        i = d // 2 - 1
        return remote(comp_rows(seq - d), dc_chain.at[i], dcs.at[i], dcr.at[i], at.seq_dev(-2))

    def dc_arrival(d):
        i = d // 2
        return remote(comp_rows(seq), dc_chain.at[i], dcs.at[0], dcr.at[i], at.seq_dev(-2))

    def pass_back(d):
        @pl.when((d + 2 < reach) & takes_back(d))
        def _():
            dc_arrival(d).wait_recv()
            add(comp_rows(seq - d), dc_chain.at[d // 2])

        pl.when(gives_back(d))(lambda: dc_back(d).start())

    chain = [d for d in range(2, reach + 1, 2)]
    odds = [d for d in range(1, reach + 1, 2)]

    odd = at.core == 1
    even = at.core == 0

    def raw_rows(d):
        return dkr.at[token_rows(raw_devs - 1 - d), :]

    def da_copy(d, i, place, device):
        return remote(raw_rows(d), da_in.at[place], das.at[i], dar.at[place], device)

    def da_join(d):
        return da_copy(d, 0, 0, at.core_dev)

    def da_beside():
        return da_copy(1, 1, 1, at.core_dev)

    def da_back():
        return da_copy(2, 2, 2, at.seq_dev(-2))

    joins_near = even & needs_raw(seq, seq - 1, tok_dev)
    joins_far = odd & needs_raw(seq, seq - 3, tok_dev)
    joined = needs_raw(other, seq - 2, tok_dev)
    gives_beside = odd & needs_raw(seq, seq - 1, tok_dev)
    takes_beside = even & needs_raw(seq + 1, seq, tok_dev)
    gives_raw = needs_raw(seq, seq - 2, tok_dev)
    takes_raw = (seq + 2 < seq_count) & needs_raw(seq + 2, seq, tok_dev)

    def share(i):
        total = times_transposed(dkr[token_rows(i), :], weight(1))
        return total + times_transposed(dvr[token_rows(i), :], weight(2))

    def norm_copy(i):
        device = (at.core_dev, at.x_dev, at.y_dev)[i]
        return remote(n_src.at[i], n_in.at[i], ns.at[i], nr.at[i], device)

    def norm_next(i):
        norm_copy(i).wait_recv()
        n_src[i + 1] = n_src[i] + n_in[i]

    def norm_line(k):
        return remote(n_src.at[3], n_line.at[at.line], nzs.at[k], nzr.at[at.line], at.line_dev(k))

    def norm_line_arrival(k):
        line = at.other_line(k)
        return remote(n_src.at[3], n_line.at[line], nzs.at[k], nzr.at[line], at.line_dev(k))

    def second_norm_back():
        gains, shifts = [], []
        for i in range(tok_dev // QB):
            rows = pl.ds(i * QB, QB)
            back, gain, shift = norm_back(db[rows, :], h[rows, :], params, 2)
            db[rows, :] = opnd[rows, :].astype(F32) + back
            dhb[rows, :] = db[rows, :].astype(BF16)
            gains.append(gain)
            shifts.append(shift)
        n_src[0, 2:3, :] = sum(gains)
        n_src[0, 3:4, :] = sum(shifts)
        do[...] = times_transposed(dhb[...], weight(0)).astype(BF16)

    def first_norm_back():
        gains, shifts = [], []
        for i in range(tok_dev // QB):
            rows = pl.ds(i * QB, QB)
            back, gain, shift = norm_back(h[rows, :], dhb[rows, :].astype(F32), params, 0)
            h[rows, :] = db[rows, :] + back
            gains.append(gain)
            shifts.append(shift)
        n_src[0, 0:1, :] = sum(gains)
        n_src[0, 1:2, :] = sum(shifts)

    def work(t):
        @pl.when(t == 1)
        def _():
            for i in range(2, 6):
                early_load(i).wait()
            weight_load(6, 0).wait()
            second_norm_back()
            weight_load(3, 0).start()

        @pl.when((t >= 3) & (t < 3 + 2 * HEADS) & (t % 2 == 1))
        def _():
            head = (t - 3) // 2
            for copy in head_loads(head):
                copy.wait()
            cols = pl.ds(pl.multiple_of(head * HEAD_DIM, HEAD_DIM), HEAD_DIM)
            attend_head_back(
                seq, tok_dev, cols, q, do, o, kr, vr, kc, vc, lse_ref, head, dkr, dvr, dkc, dvc,
                acc_kr, acc_vr, acc_kc, acc_vc,
            )

            @pl.when(head + 1 < HEADS)
            def _():
                for copy in head_loads(head + 1):
                    copy.start()

        @pl.when(t == 18)
        def _():
            weight_load(4, 1).wait()
            weight_load(5, 2).wait()
            half = comp // 2
            for i in range(2):
                rows = pl.ds(i * half, half)
                total = times_transposed(dkc[rows, :], weight(1))
                total = total + times_transposed(dvc[rows, :], weight(2))
                pair[rows, :] = total.astype(BF16)
            for d in odds:
                pl.when(needs_comp(seq, seq - d, tok_dev))(lambda d=d: dc_across(d).start())

        @pl.when(t == 19)
        def _():
            for d in chain:
                dc_join(d)

        for i, d in enumerate(reversed(chain)):
            pl.when(t == 19 + i)(lambda d=d: pass_back(d))

        @pl.when(t == 20)
        def _():
            weight_load(3, 0).wait()
            h[...] = times_transposed(q[...], weight(0))
            weight_load(0, 0).start()

        @pl.when(t == 22)
        def _():
            raw_rows(1)[...] = share(raw_devs - 2).astype(BF16)
            pl.when(joins_near)(lambda: da_join(1).start())
            pl.when(gives_beside)(lambda: da_beside().start())

            @pl.when(joins_far)
            def _():
                raw_rows(3)[...] = share(raw_devs - 4).astype(BF16)
                da_join(3).start()

        @pl.when(t == 23)
        def _():
            raw_rows(2)[...] = share(raw_devs - 3).astype(BF16)
            h[...] += share(raw_devs - 1)
            weight_load(1, 1).start()
            weight_load(2, 2).start()
            taken = takes_back(0)

            @pl.when(taken)
            def _():
                dc_arrival(0).wait_recv()
                dc[...] = dc_chain[0]

            @pl.when(jnp.logical_not(taken))
            def _():
                dc[...] = jnp.zeros_like(dc)

        @pl.when(t == 25)
        def _():
            @pl.when(joined)
            def _():
                da_join(2).wait_recv()
                add(raw_rows(2), da_in.at[0])

            pl.when(gives_raw)(lambda: da_back().start())

        @pl.when(t == 26)
        def _():
            for panel in range(3):
                weight_load(panel, panel).wait()
            heads_of = acc_kr.shape[0] // tok_dev
            for k in range(3):
                total = times_transposed(dc[...], weight(k))
                for c in range(HEADS):
                    acc = (acc_kr, acc_vr)[c // heads_of]
                    place = pl.ds(c % heads_of * tok_dev + k, comp_dev, stride=3)
                    acc[place, :] = total[:, c * HEAD_DIM : (c + 1) * HEAD_DIM]
            for c in range(HEADS):
                acc = (acc_kr, acc_vr)[c // heads_of]
                cols = pl.ds(c * HEAD_DIM, HEAD_DIM)
                h[:, cols] += acc[pl.ds(c % heads_of * tok_dev, tok_dev), :]
            for d in odds:
                pl.when(needs_comp(seq, seq - d, tok_dev))(lambda d=d: dc_across(d).wait_send())
            for d in chain:
                pl.when(gives_back(d))(lambda d=d: dc_back(d).wait_send())
            late_load(1).start()

        @pl.when(t == 28)
        def _():
            @pl.when(takes_raw)
            def _():
                da_back().wait_recv()
                h[...] += da_in[2].astype(F32)

            @pl.when(takes_beside)
            def _():
                da_beside().wait_recv()
                h[...] += da_in[1].astype(F32)

            pl.when(joins_near)(lambda: da_join(1).wait_send())
            pl.when(joins_far)(lambda: da_join(3).wait_send())
            pl.when(gives_beside)(lambda: da_beside().wait_send())
            pl.when(gives_raw)(lambda: da_back().wait_send())
            late_load(1).wait()
            first_norm_back()
            norm_copy(0).start()
            late_load(2).start()

        for i in range(2):

            @pl.when(t == 29 + i)
            def _(i=i):
                norm_next(i)
                norm_copy(i + 1).start()

        @pl.when(t == 31)
        def _():
            norm_next(2)
            n_line[at.line] = n_src[3]
            for k in range(1, lines):
                norm_line(k).start()

    def make(t):
        @pl.when(t < 4 * RATIO)
        def _():
            p = t // 2

            @pl.when(t % 2 == 0)
            def _():
                pl.when(p + 1 < 2 * RATIO)(lambda: left_start(p + 1))
                left_load(p, z_hbm).wait()
                pl.when(p == 0)(lambda: early_load(0).wait())
                pl.when(p == RATIO)(lambda: early_load(1).wait())
                turn(opnd.at[token_rows(2 + p % 2), :], 0)

            produce(t, (0, opnd.at[token_rows(p // RATIO), :]))
            pl.when(t == 4 * RATIO - 1)(lambda: late_load(0).start())

        base = 4 * RATIO
        pl.when(t == base)(lambda: turn(o, 0))
        pl.when(t // 2 == base // 2)(lambda: produce(t, (0, dhb)))

        @pl.when(t == base + 2)
        def _():
            late_load(0).wait()
            early_load(6).wait()
            early_load(7).wait()
            turn(opnd.at[token_rows(raw_devs - 1), :], raw - tok_dev)

        pl.when(t // 2 == base // 2 + 1)(lambda: produce(t, (raw - tok_dev, q)))

        @pl.when(t == base + 3)
        def _():
            for i in range(raw_devs - 1):
                turn(opnd.at[token_rows(i), :], i * tok_dev)
            for i in range(comp // tok_dev):
                turn(c_win.at[token_rows(i), :], raw + i * tok_dev)

        pl.when(t // 2 == base // 2 + 2)(lambda: produce(t, (0, dkr), (raw, dkc)))
        pl.when(t // 2 == base // 2 + 3)(lambda: produce(t, (0, dvr), (raw, dvc)))
        for k in range(3):
            pl.when(t == base + 8 + 2 * k)(lambda k=k: turn(a3.at[k], 0))
        pl.when((t >= base + 8) & (t < base + 14))(lambda: produce(t, (0, dc)))

    at.announce()
    for i in range(len(early)):
        early_load(i).start()
    left_load(0, z_hbm).start()
    for panel, slot in ((6, 0), (4, 1), (5, 2)):
        weight_load(panel, slot).start()
    for copy in head_loads(0):
        copy.start()
    at.enter()

    def step(t, carry):
        pl.when((t >= 1) & (t < chunks + 1))(lambda: start_first(t - 1))
        pl.when((t >= 2) & (t < chunks + 2))(lambda: start_second(t - 2))
        pl.when((t >= 3) & (t < chunks + 3))(lambda: start_lines(t - 3))
        pl.when(t >= BACK_LAG)(lambda: finish(t - BACK_LAG))
        pl.when(t < chunks)(lambda: make(t))
        work(t)
        return carry

    lax.fori_loop(0, chunks + BACK_LAG, step, 0)
    count = slot_out.shape[0]
    for j in range(4 * count):
        slots[j] = (out[place_ref[j]].astype(F32) * slot_scale_ref[j]).astype(BF16)
    handed = at.exchange(slots, slots_in, es, er)
    for copy in handed:
        copy.start()
    slots_in[pl.ds(at.grp * count, count)] = slots[pl.ds(at.grp * count, count)]
    for i in range(3):
        norm_copy(i).wait_send()
    for k in range(1, lines):
        norm_line_arrival(k).wait_recv()
        norm_line(k).wait_send()
    total = n_line[0]
    for i in range(1, lines):
        total = total + n_line[i]
    norm_out[...] = total
    late_load(2).wait()
    for copy in handed:
        copy.wait_send()
        copy.wait_recv()
    for g in range(4):
        for j in range(count):
            slot_out[j, :, pl.ds(g * wide, wide)] = slots_in[g * count + j]


def backward(place, slot_scale, weights, arrays, lse, norm_params, lines):
    panels, rows = weights.shape[0], weights.shape[4]
    wide, pairs, half_rows = D // 4, lines // 2, weights.shape[4] // 2
    a_win, c_win = arrays[0], arrays[1]
    tok_dev = arrays[3].shape[0]
    raw, comp, comp_dev = a_win.shape[0], c_win.shape[0], tok_dev // 3
    raw_devs, all_slots = raw // tok_dev, place.shape[0]
    reach = min(2 * lines - 1, (2 * S + 3 * CM + tok_dev - 1) // tok_dev)
    dma = pltpu.SemaphoreType.DMA
    regular = pltpu.SemaphoreType.REGULAR
    any_spec, vmem = pl.BlockSpec(memory_space=pl.ANY), pl.BlockSpec(memory_space=pltpu.VMEM)
    smem = pl.BlockSpec(memory_space=pltpu.SMEM)

    def buffer(kind, *shape):
        return pltpu.VMEM(shape, kind)

    return pl.pallas_call(
        functools.partial(backward_kernel, panels, lines),
        out_shape=[
            jax.ShapeDtypeStruct((all_slots // 4, rows, D), BF16),
            jax.ShapeDtypeStruct((tok_dev, D), F32),
            jax.ShapeDtypeStruct((4, D), F32),
        ],
        in_specs=[smem] * 2 + [any_spec] * (1 + len(arrays)) + [vmem] * 2,
        out_specs=[vmem, any_spec, vmem],
        scratch_shapes=[
            buffer(BF16, HELD, pairs, 2, 2, 2, 2, half_rows, wide),
            buffer(BF16, RING, pairs, 2, 2, 2, half_rows, wide),
            buffer(BF16, RING, 2, pairs, 2, half_rows, wide),
            buffer(BF16, RING, 2, pairs, half_rows, wide),
            buffer(BF16, 2 * panels, lines, half_rows, wide),
            buffer(BF16, panels, rows, wide),
            buffer(BF16, all_slots, rows, wide),
            buffer(BF16, all_slots, rows, wide),
            buffer(BF16, raw, D),
            buffer(BF16, 2 * pairs, 2, 2, half_rows, raw + comp),
            buffer(BF16, comp, D),
            buffer(BF16, 3, comp_dev, D),
            buffer(F32, tok_dev, D),
            buffer(F32, tok_dev, D),
            buffer(F32, tok_dev, D),
            buffer(BF16, max(comp, 2 * tok_dev), D),
            buffer(BF16, tok_dev, D),
            buffer(BF16, raw, HEAD_DIM),
            buffer(BF16, raw, HEAD_DIM),
            buffer(BF16, comp, HEAD_DIM),
            buffer(BF16, comp, HEAD_DIM),
            buffer(F32, raw, HEAD_DIM),
            buffer(F32, raw, HEAD_DIM),
            buffer(F32, comp, HEAD_DIM),
            buffer(F32, comp, HEAD_DIM),
            buffer(BF16, raw, D),
            buffer(BF16, raw, D),
            buffer(BF16, comp, D),
            buffer(BF16, comp, D),
            buffer(BF16, 3, pairs, 2, 2, rows, D),
            buffer(BF16, comp_dev, D),
            buffer(BF16, reach // 2 + 2, comp_dev, D),
            buffer(BF16, reach // 2 + 1, comp_dev, D),
            buffer(BF16, 3, tok_dev, D),
            buffer(F32, 4, 4, D),
            buffer(F32, 3, 4, D),
            buffer(F32, lines, 4, D),
            dma((RING,)), dma((RING,)),
            dma((RING, 2)), dma((RING, 2)),
            dma((RING, 2)), dma((RING, 2)),
            dma((2 * panels, lines)), dma((2 * panels, lines)),
            regular, regular((2,)), regular((2,)),
            dma((2,)), dma((11,)), dma((4,)), dma((3,)),
            dma((reach // 2 + 2,)), dma((reach // 2 + 2,)),
            dma((reach // 2 + 1,)), dma((reach // 2 + 1,)),
            dma((3,)), dma((3,)),
            dma((3,)), dma((3,)),
            dma((lines,)), dma((lines,)),
            dma((3,)), dma((3,)),
        ],
        compiler_params=pltpu.CompilerParams(
            collective_id=1, has_side_effects=True, vmem_limit_bytes=62 * MIB
        ),
        name="backward",
    )(place, slot_scale, weights, *arrays, lse, norm_params)


def local(
    tokens, cotangent, master, first_moment, second_moment, norm_params, norm_first, norm_second,
    seg_valid, book_of_group, panel_slot,
):
    seq_count = lax.axis_size("seq")
    group_count = lax.axis_size("grp")
    seq_index = lax.axis_index("seq")
    group_index = lax.axis_index("grp")
    lines = seq_count // 2
    tok_dev = tokens.shape[0]
    slot_count, slot_rows = master.shape[0], master.shape[1]
    all_slots = slot_count * group_count
    comp_dev = tok_dev // 3
    wide = D // group_count

    slot_ids = jnp.arange(all_slots, dtype=jnp.int32)
    is_panel = panel_slot[None, :] == slot_ids[:, None]
    slot_used = jnp.any(is_panel, 1)
    slot_panel = jnp.argmax(is_panel, 1).astype(jnp.int32)
    scale_all = jnp.sum(jnp.where(is_panel, panel_deviations()[None, :], 0.0), 1)
    slot_scale = lax.dynamic_slice_in_dim(scale_all, group_index * slot_count, slot_count, 0)
    order = panel_slot[jnp.array(ARRIVAL)]

    positions = seq_index * tok_dev + jnp.arange(tok_dev, dtype=jnp.int32)
    book_id = jnp.sum(jnp.where(jnp.arange(group_count) == group_index, book_of_group, 0))
    book_counts = jnp.sum(jnp.where((jnp.arange(group_count) == book_id)[:, None], seg_valid, 0), 0)
    segments = seg_valid.shape[1]
    row_counts = jnp.sum(
        jnp.where((positions // S)[:, None] == jnp.arange(segments)[None, :], book_counts[None, :], 0), 1
    )
    row_valid = (positions % S < row_counts).astype(F32)

    tokens3 = tokens.reshape(comp_dev, 3, D).transpose(1, 0, 2)
    grad_out = (cotangent.astype(F32) * row_valid[:, None]).astype(BF16)
    results = forward(
        slot_scale, order, master, tokens, tokens3, grad_out, row_valid[:, None], norm_params, lines
    )
    weights, saved, log_total, mixed = results[0], results[1:-2], results[-2], results[-1]
    a_win, c_win, q, kr, vr, kc, vc, o, z, df, b, h, db, a3 = saved
    arrays = (a_win, c_win, a3, q, kr, vr, kc, vc, o, z, df, b, h, db, grad_out, tokens)
    place = jnp.argsort(jnp.array(RETURN, jnp.int32))[slot_panel]
    slot_scales = jnp.where(slot_used, scale_all, 0.0)
    slot_sums, input_grad, norm_grad = backward(
        place.astype(jnp.int32), slot_scales, weights, arrays, log_total, norm_params, lines
    )
    slot_grad = slot_sums.astype(F32)
    slot_first, slot_second, slot_weight = adam_update(
        slot_grad, first_moment, second_moment, master, SLOT_RATE
    )
    norm_first_new, norm_second_all, norm_weight = adam_update(
        norm_grad, norm_first, norm_second, norm_params, NORM_RATE
    )
    return (
        mixed, input_grad, slot_grad, slot_first, slot_second, slot_weight, norm_grad,
        norm_first_new, norm_second_all[:2], norm_second_all[2:], norm_weight,
    )


def solution(mesh):
    rows, slots, whole = P(("grp", "seq"), None), P("grp", "seq", None), P()
    return jax.shard_map(
        local,
        mesh=mesh,
        in_specs=(rows, rows, slots, slots, slots) + (whole,) * 6,
        out_specs=(rows, rows, slots, slots, slots, slots) + (whole,) * 5,
        check_vma=False,
    )
```

```python
import functools

import jax
import jax.numpy as jnp
from jax import lax
from jax.experimental import pallas as pl
from jax.experimental.pallas import tpu as pltpu
from jax.sharding import PartitionSpec as P

D = 1024
HEADS = 8
HEAD_DIM = 128
FF = 4096
S = 512
CM = 512
STEP = 10
PANELS = 15
RATIO = FF // D
QB = 128
RAW_KEYS = 2 * S
COMP_KEYS = CM + QB
MIB = 1 << 20

NEG_SCORE = -1e30
NORM_EPS = 1e-05
BETA_ONE = 0.9
BETA_TWO = 0.999
WEIGHT_DECAY = 0.1
ADAM_EPS = 1e-08
NORM_RATE = 1.0
SLOT_RATE = 2.0
BF16 = jnp.bfloat16
F32 = jnp.float32
MESH = pl.DeviceIdType.MESH


def layer_norm(values, gain, shift):
    row_mean = jnp.mean(values, axis=-1, keepdims=True)
    centered = values - row_mean
    variance = jnp.mean(centered * centered, axis=-1, keepdims=True)
    return centered * lax.rsqrt(variance + NORM_EPS) * gain + shift


DEVIATIONS = [D ** (-0.5)] * 3 + [(D // (2 * S)) ** (-0.5)] + [D ** (-0.5)] * RATIO
DEVIATIONS = DEVIATIONS + [FF ** (-0.5)] * RATIO + [(3 * D) ** (-0.5)] * 3


def slot_deviation(panel_slot, slot):
    scale = jnp.float32(0.0)
    for panel in range(PANELS):
        scale = jnp.where(panel_slot[panel] == slot, jnp.float32(DEVIATIONS[panel]), scale)
    return scale


def adam_update(gradient, first_old, second_old, weight_old, step_rate):
    first_new = BETA_ONE * first_old + (1.0 - BETA_ONE) * gradient
    second_new = BETA_TWO * second_old + (1.0 - BETA_TWO) * gradient * gradient
    fix_one = 1.0 - BETA_ONE**STEP
    fix_two = 1.0 - BETA_TWO**STEP
    movement = first_new / fix_one / (jnp.sqrt(second_new / fix_two) + ADAM_EPS)
    return (first_new, second_new, weight_old - step_rate * (movement + WEIGHT_DECAY * weight_old))


def matmul(left, right):
    return jnp.dot(left, right, preferred_element_type=F32)


def times_transposed(left, right):
    return lax.dot_general(left, right, (((1,), (1,)), ((), ())), preferred_element_type=F32)


def contract_rows(left, right):
    return lax.dot_general(left, right, (((0,), (0,)), ((), ())), preferred_element_type=F32)


class Place:
    def __init__(self, lines):
        self.lines = lines
        self.grp = lax.axis_index("grp")
        self.seq = lax.axis_index("seq")
        self.line = self.seq // 2
        self.core = self.seq % 2
        self.row = self.grp // 2
        self.col = self.grp % 2
        self.grp_x = self.row * 2 + 1 - self.col
        self.grp_y = (1 - self.row) * 2 + self.col
        self.x_dev = {"grp": self.grp_x, "seq": self.seq}
        self.y_dev = {"grp": self.grp_y, "seq": self.seq}
        self.far_dev = {"grp": 3 - self.grp, "seq": self.seq}
        self.core_dev = {"grp": self.grp, "seq": self.line * 2 + 1 - self.core}

    def other_line(self, k):
        return lax.rem(self.line + k, self.lines)

    def line_dev(self, k):
        return {"grp": self.grp, "seq": self.other_line(k) * 2 + self.core}

    def seq_dev(self, d):
        count = 2 * self.lines
        return {"grp": self.grp, "seq": lax.rem(self.seq + d + count, count)}

    def announce(self):
        barrier = pltpu.get_barrier_semaphore()
        partners = [self.seq_dev(d) for d in range(1, 2 * self.lines)]
        for device in partners + [self.x_dev, self.y_dev, self.far_dev]:
            pl.semaphore_signal(barrier, inc=1, device_id=device, device_id_type=MESH)

    def enter(self):
        pl.semaphore_wait(pltpu.get_barrier_semaphore(), 2 * self.lines + 2)

    def exchange(self, parts, arrived, send, recv):
        count = parts.shape[0] // 4
        copies = []
        for i, device in enumerate((self.x_dev, self.y_dev, self.far_dev)):
            src = parts.at[pl.ds(device["grp"] * count, count)]
            dst = arrived.at[pl.ds(self.grp * count, count)]
            copies.append(remote(src, dst, send.at[i], recv.at[i], device))
        return copies


def remote(src, dst, send, recv, device):
    return pltpu.make_async_remote_copy(
        src_ref=src,
        dst_ref=dst,
        send_sem=send,
        recv_sem=recv,
        device_id=device,
        device_id_type=MESH,
    )


def memory_start(position):
    return (position // S - 1) * S


def comp_window_first(seq, tok_dev):
    return jnp.maximum(memory_start(seq * tok_dev) - 3 * CM, 0) // tok_dev


def raw_devices(tok_dev):
    return (RAW_KEYS - QB + tok_dev - 1) // tok_dev + 1


def comp_devices(tok_dev, seq_count):
    return min((3 * CM + S) // tok_dev + 1, seq_count)


def needs_raw(reader, owner, tok_dev):
    return (owner >= 0) & ((owner + 1) * tok_dev > memory_start(reader * tok_dev))


def needs_comp(reader, owner, tok_dev):
    last = jnp.maximum(memory_start(reader * tok_dev + tok_dev - 1), 0) // 3
    inside = (owner >= 0) & (owner >= comp_window_first(reader, tok_dev))
    return inside & (owner * (tok_dev // 3) < last)


def chip_needs_comp(reader, owner, tok_dev):
    even = reader // 2 * 2
    return needs_comp(even, owner, tok_dev) | needs_comp(even + 1, owner, tok_dev)


def chain_needs_comp(reader, owner, tok_dev, seq_count, reach):
    needed = chip_needs_comp(reader, owner, tok_dev)
    for ahead in range(2, reach + 1, 2):
        later = reader + ahead
        needed = needed | ((later < seq_count) & chip_needs_comp(later, owner, tok_dev))
    return needed & (owner >= 0) & (reader < seq_count)


def block_window(seq, i, tok_dev, raw_rows, comp_rows):
    position = seq * tok_dev + i * QB
    memory = memory_start(position)
    raw_base = (seq + 1) * tok_dev - raw_rows
    raw_at = jnp.minimum(memory - raw_base, raw_rows - RAW_KEYS)
    comp_end = jnp.maximum(memory, 0) // 3
    comp_low = jnp.maximum(comp_end - CM, 0)
    comp_base = comp_window_first(seq, tok_dev) * (tok_dev // 3)
    comp_at = jnp.minimum((comp_low - comp_base) // QB * QB, comp_rows - COMP_KEYS)
    return (
        position,
        pl.multiple_of(raw_at, QB),
        pl.multiple_of(comp_at, QB),
        raw_base + raw_at,
        comp_base + comp_at,
        memory,
        comp_low,
        comp_end,
    )


def row_sum(values):
    return jnp.sum(values, axis=1, keepdims=True)


def norm_rows(values, params, first):
    mean = row_sum(values) * (1.0 / D)
    centered = values - mean
    variance = row_sum(centered * centered) * (1.0 / D)
    gain, shift = params[first : first + 1, :], params[first + 1 : first + 2, :]
    return centered * lax.rsqrt(variance + NORM_EPS) * gain + shift


GELU_IN = (2.0 / 3.141592653589793) ** 0.5
GELU_CUBE = 0.044715


def gelu_pair(f):
    square = f * f
    t = jnp.tanh(GELU_IN * f * (1.0 + GELU_CUBE * square))
    half = 0.5 * (1.0 + t)
    slope = half + 0.5 * f * (1.0 - t * t) * (GELU_IN * (1.0 + 3.0 * GELU_CUBE * square))
    return f * half, slope


class Attention:
    def __init__(self, seq, i, tok_dev, raw_rows, comp_rows):
        place = block_window(seq, i, tok_dev, raw_rows, comp_rows)
        self.pos, raw_at, comp_at, self.raw_pos, self.comp_pos = place[:5]
        self.memory, self.comp_low, self.comp_end = place[5:]
        self.rows = pl.ds(i * QB, QB)
        self.raw = pl.ds(raw_at, RAW_KEYS)
        self.comp = pl.ds(comp_at, COMP_KEYS)

    def raw_bias(self, shape, key_dim):
        key_pos = self.raw_pos + lax.broadcasted_iota(jnp.int32, shape, key_dim)
        query_pos = self.pos + lax.broadcasted_iota(jnp.int32, shape, 1 - key_dim)
        seen = (key_pos >= jnp.maximum(self.memory, 0)) & (key_pos <= query_pos)
        return jnp.where(seen, 0.0, NEG_SCORE)

    def comp_bias(self, shape, key_dim):
        index = self.comp_pos + lax.broadcasted_iota(jnp.int32, shape, key_dim)
        return jnp.where((index >= self.comp_low) & (index < self.comp_end), 0.0, NEG_SCORE)


SCORE_SCALE = HEAD_DIM ** (-0.5) * 1.4426950408889634


def attend_head(seq, tok_dev, cols, q, kr, vr, kc, vc, out, lse, lse_row, raw_bias, comp_bias):
    for i in range(tok_dev // QB):
        at = Attention(seq, i, tok_dev, kr.shape[0], kc.shape[0])
        query = q[at.rows, cols]
        raw = times_transposed(query, kr[at.raw, cols]) * SCORE_SCALE + raw_bias[i]
        comp = times_transposed(query, kc[at.comp, cols]) * SCORE_SCALE + comp_bias[i]
        top = jnp.maximum(
            jnp.max(raw, axis=1, keepdims=True), jnp.max(comp, axis=1, keepdims=True)
        )
        raw = jnp.exp2(raw - top)
        comp = jnp.exp2(comp - top)
        total = row_sum(raw) + row_sum(comp)
        mixed = matmul(raw.astype(BF16), vr[at.raw, cols])
        mixed = mixed + matmul(comp.astype(BF16), vc[at.comp, cols])
        out[at.rows, cols] = mixed / total
        stat = jnp.broadcast_to(top + jnp.log2(total), (QB, QB))
        lse[lse_row, :, at.rows] = stat.T[:8]


TAPS = [4 + 2 * RATIO + i for i in range(3)]
ARRIVAL = TAPS + [0, 1, 2, 3]
for _i in range(RATIO):
    ARRIVAL = ARRIVAL + [4 + _i, 4 + RATIO + _i]
AHEAD = 4
LAG = 4
SEMS = 8
KEPT = 4


def forward_kernel(
    panels, lines,
    slot_ref, book_ref, seg_ref, master_ref, tok_ref, cot_ref, norm_ref,
    full_ref, a_out, c_out, q_out, kr_out, vr_out, kc_out, vc_out, o_out, z_out, df_out, b_out,
    h_out, db_out, a3_out, dy_out, lse_ref, mixed_ref,
    wbuf, a_win, a3, c_win, q, kr, vr, kc, vc, o, z, df, b, h, y, db, dy_ref, slots, slots_in, block,
    normed, raw_bias, comp_bias,
    own_sem, zs, zr, s1, r1, s2, r2, cs, cr, wsem, a_s, a_r, c_s, c_r, f_s, f_r, es, er, out_sem,
    hidden_sem,
):
    at = Place(lines)
    seq = at.seq
    seq_count = 2 * lines
    chunks = 2 * panels
    tok_dev = tok_ref.shape[0]
    comp_dev = tok_dev // 3
    raw_devs = a_win.shape[0] // tok_dev
    comp_devs = c_win.shape[0] // comp_dev
    reach = min(seq_count - 1, (2 * S + 3 * CM + tok_dev - 1) // tok_dev)
    wide = block.shape[-1]
    half_rows = block.shape[1] // 2

    def cols(g):
        return pl.ds(pl.multiple_of(g * wide, wide), wide)

    def rows_of(u):
        return pl.ds(pl.multiple_of(u % 2 * half_rows, half_rows), half_rows)

    def line_place(u, line):
        return full_ref.at[u // 2, line // 2, line % 2, at.core, rows_of(u), cols(at.grp)]

    def line_copy(u, k):
        src = block.at[u // 2, rows_of(u), :]
        return remote(src, line_place(u, at.line), zs.at[u, k], zr.at[u, at.line], at.line_dev(k))

    def line_arrival(u, k):
        src, line = block.at[u // 2, rows_of(u), :], at.other_line(k)
        return remote(src, line_place(u, line), zs.at[u, k], zr.at[u, line], at.line_dev(k))

    def part(u, half, g):
        return full_ref.at[u // 2, :, half, at.core, rows_of(u), cols(g)]

    def first(u, half, g):
        device, i = (at.x_dev if half == 0 else at.y_dev), u % SEMS
        return remote(part(u, half, g), part(u, half, g), s1.at[i, half], r1.at[i, half], device)

    def second(u, half, j, g):
        device, i = (at.y_dev if half == 0 else at.x_dev), u % SEMS
        ref = part(u, half, g)
        return remote(ref, ref, s2.at[i, half, j], r2.at[i, half, j], device)

    def cross(u, half, core):
        ref, i = full_ref.at[u // 2, :, half, core, rows_of(u)], u % SEMS
        return remote(ref, ref, cs.at[i, half], cr.at[i, half], at.core_dev)

    def load(u):
        src = full_ref.at[u // 2, :, :, :, rows_of(u)]
        dst = wbuf.at[u // 2 % KEPT, :, :, :, rows_of(u)]
        return pltpu.make_async_copy(src, dst, wsem.at[u % SEMS])

    def start_lines(u):
        for k in range(1, lines):
            line_copy(u, k).start()

    def start_first(u):
        for k in range(1, lines):
            line_arrival(u, k).wait_recv()
        for half in (0, 1):
            first(u, half, at.grp).start()

    def start_second(u):
        for half in (0, 1):
            near = at.grp_x if half == 0 else at.grp_y
            first(u, half, near).wait_recv()
            second(u, half, 0, at.grp).start()
            second(u, half, 1, near).start()

    def start_cross(u):
        for half in (0, 1):
            second(u, half, 0, at.grp_y if half == 0 else at.grp_x).wait_recv()
            second(u, half, 1, 3 - at.grp).wait_recv()
            cross(u, half, at.core).start()

    def finish(u):
        for half in (0, 1):
            cross(u, half, 1 - at.core).wait_recv()
            first(u, half, at.grp).wait_send()
            second(u, half, 0, at.grp).wait_send()
            second(u, half, 1, at.grp_x if half == 0 else at.grp_y).wait_send()
            cross(u, half, at.core).wait_send()
        for k in range(1, lines):
            line_copy(u, k).wait_send()
        load(u).start()

    def a_rows(d):
        return a_win.at[pl.ds((raw_devs - 1 - d) * tok_dev, tok_dev), :]

    def a_copy(d, place, i, device):
        return remote(a_rows(d), a_rows(place), a_s.at[i], a_r.at[place - 1], device)

    def a_next():
        return a_copy(0, 2, 0, at.seq_dev(2))

    def a_beside():
        return a_copy(0, 1, 1, at.core_dev)

    def a_on(place):
        return a_copy(2, place, 2, at.core_dev)

    odd = at.core == 1
    even = at.core == 0
    gives_next = (seq + 2 < seq_count) & needs_raw(seq + 2, seq, tok_dev)
    gives_beside = even & needs_raw(seq + 1, seq, tok_dev)
    gives_on_far = even & needs_raw(seq + 1, seq - 2, tok_dev)
    gives_on_near = odd & needs_raw(seq - 1, seq - 2, tok_dev)

    def c_rows(reader, owner):
        place = jnp.clip(owner - comp_window_first(reader, tok_dev), 0, comp_devs - 1)
        return c_win.at[pl.ds(pl.multiple_of(place * comp_dev, comp_dev), comp_dev), :]

    def c_from(d):
        return own_c if d == 0 else c_rows(seq, seq - d)

    def c_next(d):
        dst = c_rows(seq + 2, seq - d)
        return remote(c_from(d), dst, c_s.at[d // 2], c_r.at[d // 2 + 1], at.seq_dev(2))

    def c_arrival(d):
        return remote(own_c, c_rows(seq, seq - d), c_s.at[0], c_r.at[d // 2], at.seq_dev(2))

    def c_across(d):
        other = seq + 1 - 2 * at.core
        dst = c_rows(other, seq - d)
        return remote(c_from(d), dst, f_s.at[d // 2], f_r.at[d // 2], at.core_dev)

    def c_across_arrival(d):
        other = seq + 1 - 2 * at.core
        return remote(own_c, c_rows(seq, other - d), f_s.at[0], f_r.at[d // 2], at.core_dev)

    steps_back = [d for d in range(0, reach + 1, 2)]

    def gives_c(d):
        return chain_needs_comp(seq + 2, seq - d, tok_dev, seq_count, reach - 1)

    def takes_c(d):
        return chain_needs_comp(seq, seq - d, tok_dev, seq_count, reach - 1)

    def gives_c_across(d):
        return needs_comp(seq + 1 - 2 * at.core, seq - d, tok_dev)

    def takes_c_across(d):
        return needs_comp(seq, seq + 1 - 2 * at.core - d, tok_dev)

    def pass_c(d):
        if d > 0:
            pl.when(takes_c(d))(lambda: c_arrival(d).wait_recv())
        pl.when(gives_c(d))(lambda: c_next(d).start())
        pl.when(gives_c_across(d))(lambda: c_across(d).start())

    outs = [
        (a_win, a_out), (c_win, c_out), (q, q_out), (kr, kr_out), (vr, vr_out), (kc, kc_out),
        (vc, vc_out), (o, o_out), (b, b_out), (h, h_out), (db, db_out), (a3, a3_out), (dy_ref, dy_out),
    ]

    def flush(*names):
        for i, (src, dst) in enumerate(outs):
            if any(src is name for name in names):
                pltpu.make_async_copy(src, dst, out_sem.at[i]).start()

    def flush_hidden(pair):
        units = pl.ds(pl.multiple_of(pair * D, D), D)
        return [
            pltpu.make_async_copy(src.at[:, units], dst.at[:, units], hidden_sem.at[i, pair])
            for i, (src, dst) in enumerate(((z, z_out), (df, df_out)))
        ]

    at.announce()
    count = master_ref.shape[0]
    for j in range(count):
        scaled = (master_ref[j] * slot_deviation(slot_ref, at.grp * count + j)).astype(BF16)
        for g in range(4):
            slots[g * count + j] = scaled[:, g * wide : (g + 1) * wide]
    at.enter()
    handed = at.exchange(slots, slots_in, es, er)
    for copy in handed:
        copy.start()
    slots_in[pl.ds(at.grp * count, count)] = slots[pl.ds(at.grp * count, count)]

    params = norm_ref[...]
    for i in range(tok_dev // QB):
        rows = pl.ds(i * QB, QB)
        mine = norm_rows(tok_ref[rows, :].astype(F32), params, 0)
        a_win[pl.ds((raw_devs - 1) * tok_dev + i * QB, QB), :] = mine.astype(BF16)
        for c in range(HEADS):
            normed[c, rows, :] = mine[:, c * HEAD_DIM : (c + 1) * HEAD_DIM]
    pl.when(gives_next)(lambda: a_next().start())
    pl.when(gives_beside)(lambda: a_beside().start())
    for d in range(1, raw_devs):
        absent = jnp.logical_not(needs_raw(seq, seq - d, tok_dev))

        @pl.when(absent)
        def _(d=d):
            a_rows(d)[...] = jnp.zeros((tok_dev, D), BF16)

    for k in range(3):
        for c in range(HEADS):
            rows = pl.ds(k, comp_dev, stride=3)
            a3[k, :, pl.ds(c * HEAD_DIM, HEAD_DIM)] = normed[c, rows, :].astype(BF16)
    book = jnp.int32(0)
    for g in range(4):
        book = jnp.where(at.grp == g, book_ref[g], book)
    valid = []
    for i in range(tok_dev // QB):
        rows = pl.ds(i * QB, QB)
        pos = seq * tok_dev + i * QB
        inside = pos % S + lax.broadcasted_iota(jnp.int32, (QB, D), 0)
        valid.append(inside < seg_ref[book, pos // S])
        dy_ref[rows, :] = jnp.where(valid[i], cot_ref[rows, :].astype(F32), 0.0).astype(BF16)
        block_at = Attention(seq, i, tok_dev, kr.shape[0], kc.shape[0])
        raw_bias[i] = block_at.raw_bias((QB, RAW_KEYS), 1)
        comp_bias[i] = block_at.comp_bias((QB, COMP_KEYS), 1)
    for i in range(comp_devs):
        owner = comp_window_first(seq, tok_dev) + i
        taken = needs_comp(seq, owner, tok_dev)
        for d in steps_back[1:]:
            taken = taken | ((owner == seq - d) & takes_c(d))

        @pl.when(jnp.logical_not(taken))
        def _(i=i):
            c_win[pl.ds(i * comp_dev, comp_dev), :] = jnp.zeros((comp_dev, D), BF16)

    for copy in handed:
        copy.wait_recv()
    for p in range(panels):
        block[p] = slots_in[slot_ref[ARRIVAL[p]]]
    for u in range(AHEAD):
        start_lines(u)
    own_place = full_ref.at[:, at.line // 2, at.line % 2, at.core, :, cols(at.grp)]
    own = pltpu.make_async_copy(block, own_place, own_sem)
    own.start()
    own.wait()

    own_c = b.at[pl.ds(0, comp_dev), :]
    tile = 8 * half_rows

    def weight(slot, col):
        return wbuf[slot, :, :, :, :, col].reshape(D, wide)

    def columns(body):
        def one(j, carry):
            body(pl.ds(pl.multiple_of(j * wide, wide), wide))
            return carry

        lax.fori_loop(0, D // wide, one, 0)

    def tap(k, slot):
        def body(col):
            part_sum = matmul(a3[k], weight(slot, col))
            if k == 0:
                y[pl.ds(0, comp_dev), col] = part_sum
            elif k == 1:
                y[pl.ds(0, comp_dev), col] += part_sum
            else:
                own_c[:, col] = (y[pl.ds(0, comp_dev), col] + part_sum).astype(BF16)

        columns(body)

    def project(dst, src, slot):
        block_rows = min(src.shape[0], tok_dev)

        def body(col):
            for i in range(src.shape[0] // block_rows):
                rows = pl.ds(i * block_rows, block_rows)
                dst[rows, col] = matmul(src[rows, :], weight(slot, col)).astype(BF16)

        columns(body)

    def heads(low, high):
        def one(i, carry):
            col = pl.ds(pl.multiple_of(i * HEAD_DIM, HEAD_DIM), HEAD_DIM)
            attend_head(
                seq, tok_dev, col, q, kr, vr, kc, vc, o, lse_ref, i, raw_bias, comp_bias
            )
            return carry

        lax.fori_loop(low, high, one, 0)

    def hidden(pair, low, high):
        up, down = (2 * pair + 7) % KEPT, (2 * pair + 8) % KEPT

        def one(i, carry):
            up_rows = wbuf[up, i].reshape(tile, D)
            down_rows = wbuf[down, i].reshape(tile, D)
            value, slope = gelu_pair(times_transposed(b[...], up_rows))
            units = pl.ds(pl.multiple_of(pair * D + i * tile, tile), tile)
            z[:, units] = value.astype(BF16)
            df[:, units] = (times_transposed(dy_ref[...], down_rows) * slope).astype(BF16)
            return carry

        lax.fori_loop(low, high, one, 0)

    def gather_hidden(pair):
        up, down = (2 * pair + 7) % KEPT, (2 * pair + 8) % KEPT
        units = pl.ds(pl.multiple_of(pair * D, D), D)

        def body(col):
            y[:, col] += matmul(z[:, units], weight(down, col))
            db[:, col] += matmul(df[:, units], weight(up, col))

        columns(body)

    def work(w):
        slot = w // 2 % KEPT
        for k in range(3):
            pl.when(w == 2 * k)(lambda k=k: tap(k, slot))

        @pl.when(w == 1)
        def _():
            for copy in handed:
                copy.wait_send()
            pl.when(needs_raw(seq, seq - 2, tok_dev))(lambda: a_next().wait_recv())
            pl.when(gives_on_far)(lambda: a_on(3).start())
            pl.when(gives_on_near)(lambda: a_on(1).start())

        pl.when(w == 4)(lambda: pass_c(0))

        @pl.when(w == 5)
        def _():
            pl.when(even & needs_raw(seq, seq - 1, tok_dev))(lambda: a_on(1).wait_recv())
            pl.when(odd & needs_raw(seq, seq - 1, tok_dev))(lambda: a_beside().wait_recv())
            pl.when(needs_raw(seq, seq - 3, tok_dev))(lambda: a_on(3).wait_recv())
            pl.when(gives_next)(lambda: a_next().wait_send())
            pl.when(gives_beside)(lambda: a_beside().wait_send())
            pl.when(gives_on_far)(lambda: a_on(3).wait_send())
            pl.when(gives_on_near)(lambda: a_on(1).wait_send())
            flush(a_win, a3, dy_ref)

        @pl.when(w == 6)
        def _():
            project(q, a_win.at[pl.ds((raw_devs - 1) * tok_dev, tok_dev), :], slot)
            flush(q)

        for i, d in enumerate(steps_back[1:]):
            pl.when(w == 6 + 2 * i)(lambda d=d: pass_c(d))

        @pl.when(w == 8)
        def _():
            project(kr, a_win, slot)
            flush(kr)

        @pl.when(w == 10)
        def _():
            project(vr, a_win, slot)
            flush(vr)

        @pl.when(w == 12)
        def _():
            for d in steps_back:
                pl.when(takes_c_across(d))(lambda d=d: c_across_arrival(d).wait_recv())
            flush(c_win)
            project(kc, c_win, 4 % KEPT)
            project(vc, c_win, 5 % KEPT)
            flush(kc, vc)

        @pl.when((w >= 13) & (w < 17))
        def _():
            low = (w - 13) * (HEADS // 4)
            heads(low, low + HEADS // 4)

        @pl.when(w == 17)
        def _():
            flush(o)
            for d in steps_back:
                pl.when(gives_c(d))(lambda d=d: c_next(d).wait_send())
                pl.when(gives_c_across(d))(lambda d=d: c_across(d).wait_send())

            def body(col):
                sent = matmul(o[...].astype(BF16), weight(6 % KEPT, col))
                h[:, col] = tok_ref[:, col].astype(F32) + sent

            columns(body)
            for i in range(tok_dev // QB):
                rows = pl.ds(i * QB, QB)
                b[rows, :] = norm_rows(h[rows, :], params, 2).astype(BF16)
            y[...] = h[...]
            db[...] = jnp.zeros_like(db)
            flush(b, h)

        turn = w - 16
        lines_half = wbuf.shape[1] // 2
        first_turn = ((turn >= 4) & (turn % 4 == 0)) | (turn == 2)
        second_turn = ((turn >= 4) & (turn % 4 == 1)) | (turn == 3)
        pl.when(first_turn)(lambda: hidden(turn // 4, 0, lines_half))

        @pl.when(second_turn)
        def _():
            hidden(turn // 4, lines_half, 2 * lines_half)
            for copy in flush_hidden(turn // 4):
                copy.start()
            gather_hidden(turn // 4)

    def step(t, carry):
        pl.when(t + AHEAD < chunks)(lambda: start_lines(t + AHEAD))
        pl.when(t < chunks)(lambda: start_first(t))
        pl.when((t >= 1) & (t < chunks + 1))(lambda: start_second(t - 1))
        pl.when((t >= 2) & (t < chunks + 2))(lambda: start_cross(t - 2))

        pl.when((t >= LAG) & (t < chunks + LAG))(lambda: load(t - LAG).wait())
        pl.when(t >= LAG + 1)(lambda: work(t - LAG - 1))
        pl.when((t >= 3) & (t < chunks + 3))(lambda: finish(t - 3))
        return carry

    lax.fori_loop(0, chunks + LAG + 1, step, 0)
    flush(db)
    for i in range(tok_dev // QB):
        rows = pl.ds(i * QB, QB)
        mixed_ref[rows, :] = jnp.where(valid[i], y[rows, :], 0.0).astype(BF16)
    for pair in range(RATIO):
        for copy in flush_hidden(pair):
            copy.wait()
    for i, (src, dst) in enumerate(outs):
        pltpu.make_async_copy(src, dst, out_sem.at[i]).wait()


def forward(panel_slot, book_of_group, seg_valid, master, tokens, cotangent, norm_params, lines):
    panels, slot_count, rows = panel_slot.shape[0], master.shape[0], master.shape[1]
    wide = D // 4
    tok_dev = tokens.shape[0]
    raw = raw_devices(tok_dev) * tok_dev
    comp = comp_devices(tok_dev, 2 * lines) * (tok_dev // 3)
    dma = pltpu.SemaphoreType.DMA
    token, wide_token, hidden = ((tok_dev, D), BF16), ((tok_dev, D), F32), ((tok_dev, FF), BF16)
    raw_rows, comp_rows, thirds = ((raw, D), BF16), ((comp, D), BF16), ((3, tok_dev // 3, D), BF16)
    shapes = [raw_rows, comp_rows, token, raw_rows, raw_rows, comp_rows, comp_rows, wide_token]
    shapes = shapes + [hidden, hidden, token, wide_token, wide_token, thirds, token]
    scratch = [raw_rows, thirds, comp_rows, token, raw_rows, raw_rows, comp_rows, comp_rows]
    scratch = scratch + [wide_token, hidden, hidden, token, wide_token, wide_token, wide_token, token]
    scratch = [pltpu.VMEM(shape, kind) for shape, kind in scratch]
    blocks = tok_dev // QB
    any_spec, vmem = pl.BlockSpec(memory_space=pl.ANY), pl.BlockSpec(memory_space=pltpu.VMEM)
    smem = pl.BlockSpec(memory_space=pltpu.SMEM)
    return pl.pallas_call(
        functools.partial(forward_kernel, panels, lines),
        out_shape=[jax.ShapeDtypeStruct((panels, lines // 2, 2, 2, rows, D), BF16)]
        + [jax.ShapeDtypeStruct(shape, kind) for shape, kind in shapes]
        + [jax.ShapeDtypeStruct((HEADS, 8, tok_dev), F32), jax.ShapeDtypeStruct((tok_dev, D), BF16)],
        in_specs=[smem] * 3 + [vmem] * 4,
        out_specs=[any_spec] * (1 + len(shapes)) + [vmem] * 2,
        scratch_shapes=[pltpu.VMEM((KEPT, lines // 2, 2, 2, rows, D), BF16)]
        + scratch
        + [
            pltpu.VMEM((4 * slot_count, rows, wide), BF16),
            pltpu.VMEM((4 * slot_count, rows, wide), BF16),
            pltpu.VMEM((panels, rows, wide), BF16),
            pltpu.VMEM((HEADS, tok_dev, HEAD_DIM), F32),
            pltpu.VMEM((blocks, QB, RAW_KEYS), F32),
            pltpu.VMEM((blocks, QB, COMP_KEYS), F32),
            dma(()),
            dma((2 * panels, lines)), dma((2 * panels, lines)),
            dma((SEMS, 2)), dma((SEMS, 2)),
            dma((SEMS, 2, 2)), dma((SEMS, 2, 2)),
            dma((SEMS, 2)), dma((SEMS, 2)),
            dma((SEMS,)),
            dma((3,)), dma((3,)), dma((5,)), dma((5,)), dma((5,)), dma((5,)),
            dma((3,)), dma((3,)),
            dma((len(shapes),)),
            dma((2, RATIO)),
        ],
        compiler_params=pltpu.CompilerParams(
            collective_id=0, has_side_effects=True, vmem_limit_bytes=60 * MIB
        ),
        name="forward",
    )(panel_slot, book_of_group, seg_valid, master, tokens, cotangent, norm_params)


RETURN = [4 + RATIO + _i for _i in range(RATIO)] + [4 + _i for _i in range(RATIO)] + [3, 0, 1, 2] + TAPS
RING = 3
HELD = 5
BACK_LAG = 4


def norm_back(grad, values, params, first):
    mean = row_sum(values) * (1.0 / D)
    centered = values - mean
    scale = lax.rsqrt(row_sum(centered * centered) * (1.0 / D) + NORM_EPS)
    unit = centered * scale
    inner = grad * params[first : first + 1, :]
    back = inner - row_sum(inner) * (1.0 / D) - unit * (row_sum(inner * unit) * (1.0 / D))
    gain = jnp.sum(grad * unit, axis=0, keepdims=True)
    return back * scale, gain, jnp.sum(grad, axis=0, keepdims=True)


def attend_block_back(
    seq, tok_dev, i, cols, q, do, o, kr, vr, kc, vc, lse, lse_row, raw_bias, comp_bias,
    acc_kr, acc_vr, acc_kc, acc_vc,
):
    at = Attention(seq, i, tok_dev, kr.shape[0], kc.shape[0])
    query = q[at.rows, cols]
    grad = do[at.rows, cols]
    delta = row_sum(grad.astype(F32) * o[at.rows, cols])
    delta = jnp.broadcast_to(delta, (QB, QB)).T[0:1]
    stat = lse[lse_row, 0:1, at.rows]

    def part(k_ref, v_ref, acc_k, acc_v, keys, bias):
        k = k_ref[keys, :]
        s = times_transposed(k, query) * SCORE_SCALE + bias
        p = jnp.exp2(s - stat)
        dp = times_transposed(v_ref[keys, :], grad)
        ds = (p * (dp - delta)).astype(BF16)
        acc_v[keys, :] += matmul(p.astype(BF16), grad)
        acc_k[keys, :] += matmul(ds, query)
        return contract_rows(ds, k)

    dq = part(kr, vr, acc_kr, acc_vr, at.raw, raw_bias[i])
    dq = dq + part(kc, vc, acc_kc, acc_vc, at.comp, comp_bias[i])
    q[at.rows, cols] = (dq * HEAD_DIM ** (-0.5)).astype(BF16)


def backward_kernel(
    panels, lines,
    slot_ref,
    full_ref, a_hbm, c_hbm, a3_hbm, q_hbm, kr_hbm, vr_hbm, kc_hbm, vc_hbm, o_hbm, z_hbm, df_hbm,
    b_hbm, h_hbm, db_hbm, dy_hbm, tok_hbm, lse_ref, norm_ref,
    slot_out, in_grad_out, norm_out,
    held, cross_in, first_in, second_in, line_in, out, slots, slots_in,
    opnd, lhs_t, c_win, a3, h, db, o, pair, q, kr, vr, kc, vc, acc_kr, acc_vr, acc_kc, acc_vc,
    raw_bias, comp_bias, place, scale, dkr, dvr, dkc, dvc, wbuf, dc, dc_beside, dc_chain, da_in, n_src, n_in, n_line,
    cs, cr, s1, r1, s2, r2, zs, zr, free_cross, free_first, free_second,
    lsem, osem, hsem, wsem, dbs, dbr, dcs, dcr, das, dar, ns, nr, nzs, nzr, es, er,
):
    at = Place(lines)
    seq = at.seq
    seq_count = 2 * lines
    chunks = 2 * panels
    tok_dev = q.shape[0]
    comp_dev = tok_dev // 3
    raw_devs = dkr.shape[0] // tok_dev
    comp_devs = dkc.shape[0] // comp_dev
    reach = min(seq_count - 1, (2 * S + 3 * CM + tok_dev - 1) // tok_dev)
    wide = out.shape[-1]
    half_rows = out.shape[1] // 2
    pairs = lines // 2
    params = norm_ref[...]
    raw, comp = dkr.shape[0], dkc.shape[0]

    def token_rows(i):
        return pl.ds(pl.multiple_of(i * tok_dev, tok_dev), tok_dev)

    dhb, do = pair.at[token_rows(0), :], pair.at[token_rows(1), :]

    def mine(u):
        return held.at[u % HELD, :, :, at.core]

    def cross(u):
        src, i = held.at[u % HELD, :, :, 1 - at.core], u % RING
        return remote(src, cross_in.at[i], cs.at[i], cr.at[i], at.core_dev)

    def first(u, half):
        i = u % RING
        if half == 0:
            src, device = mine(u).at[:, 0, 1 - at.row], at.y_dev
        else:
            src, device = mine(u).at[:, 1, :, 1 - at.col], at.x_dev
        return remote(src, first_in.at[i, half], s1.at[i, half], r1.at[i, half], device)

    def second(u, half):
        i = u % RING
        if half == 0:
            src, device = mine(u).at[:, 0, at.row, 1 - at.col], at.x_dev
        else:
            src, device = mine(u).at[:, 1, 1 - at.row, at.col], at.y_dev
        return remote(src, second_in.at[i, half], s2.at[i, half], r2.at[i, half], device)

    def line_copy(u, k):
        line = at.other_line(k)
        src = mine(u).at[line // 2, line % 2, at.row, at.col]
        i = lines - 1 - k
        return remote(src, line_in.at[u, i], zs.at[u, k], zr.at[u, i], at.line_dev(k))

    def line_arrival(u, k):
        line = at.other_line(k)
        src = mine(u).at[line // 2, line % 2, at.row, at.col]
        return remote(src, line_in.at[u, k - 1], zs.at[u, k], zr.at[u, k - 1], at.line_dev(k))

    def give(semaphore, device):
        pl.semaphore_signal(semaphore, inc=1, device_id=device, device_id_type=MESH)

    def add(dst, src):
        dst[...] = (dst[...].astype(F32) + src[...].astype(F32)).astype(BF16)

    def start_first(u):
        cross(u).wait_recv()
        for half in (0, 1):
            for i in range(pairs):
                for g in range(4):
                    add(
                        mine(u).at[i, half, g // 2, g % 2],
                        cross_in.at[u % RING, i, half, g // 2, g % 2],
                    )
            pl.when(u >= RING)(lambda half=half: pl.semaphore_wait(free_first.at[half], 1))
            first(u, half).start()
        cross(u).wait_send()
        pl.when(u + RING < chunks)(lambda: give(free_cross, at.core_dev))

    def start_second(u):
        for half in (0, 1):
            first(u, half).wait_recv()
            for i in range(pairs):
                for j in (0, 1):
                    row, col = (at.row, j) if half == 0 else (j, at.col)
                    add(mine(u).at[i, half, row, col], first_in.at[u % RING, half, i, j])
            pl.when(u >= RING)(lambda half=half: pl.semaphore_wait(free_second.at[half], 1))
            second(u, half).start()
            first(u, half).wait_send()
            device = at.y_dev if half == 0 else at.x_dev
            pl.when(u + RING < chunks)(
                lambda half=half, device=device: give(free_first.at[half], device)
            )

    def start_lines(u):
        for half in (0, 1):
            second(u, half).wait_recv()
            for i in range(pairs):
                add(mine(u).at[i, half, at.row, at.col], second_in.at[u % RING, half, i])
            second(u, half).wait_send()
            device = at.x_dev if half == 0 else at.y_dev
            pl.when(u + RING < chunks)(
                lambda half=half, device=device: give(free_second.at[half], device)
            )
        for k in range(1, lines):
            line_copy(u, k).start()

    def finish(u):
        total = mine(u)[at.line // 2, at.line % 2, at.row, at.col].astype(F32)
        for k in range(1, lines):
            line_arrival(u, k).wait_recv()
            total = total + line_in[u, k - 1].astype(F32)
        rows = pl.ds(pl.multiple_of(u % 2 * half_rows, half_rows), half_rows)
        out[u // 2, rows, :] = total.astype(BF16)
        for k in range(1, lines):
            line_copy(u, k).wait_send()

    def turn(left, first_row):
        turned = left[...].astype(BF16).T
        count = left.shape[0]
        turned = turned.reshape(2 * pairs, 2, 2, half_rows, count)
        lhs_t[:, :, :, :, pl.ds(first_row, count)] = turned

    def produce(u, *terms):
        def columns(j, carry):
            col = pl.ds(pl.multiple_of(j * wide, wide), wide)
            total = None
            for first_row, right in terms:
                count = right.shape[0]
                left = lhs_t[:, :, u % 2, :, pl.ds(first_row, count)].reshape(D // 2, count)
                term = matmul(left, right[:, col])
                total = term if total is None else total + term
            total = total.reshape(pairs, 2, 2, half_rows, wide)
            held[u % HELD, :, :, :, j // 2, j % 2] = total.astype(BF16)
            return carry

        lax.fori_loop(0, 4, columns, 0)
        pl.when(u >= RING)(lambda: pl.semaphore_wait(free_cross, 1))
        cross(u).start()

    def left_load(p, src):
        units = pl.ds(pl.multiple_of(p % RATIO * D, D), D)
        return pltpu.make_async_copy(src.at[:, units], opnd.at[token_rows(2 + p % 2), :], lsem.at[p % 2])

    def left_start(p):
        pl.when(p < RATIO)(lambda: left_load(p, z_hbm).start())
        pl.when(p >= RATIO)(lambda: left_load(p, df_hbm).start())

    early = [
        (dy_hbm, opnd.at[token_rows(0), :]), (b_hbm, opnd.at[token_rows(1), :]), (h_hbm, h),
        (db_hbm, db), (o_hbm, o), (q_hbm, q), (c_hbm, c_win), (a3_hbm, a3),
    ]

    def early_load(i):
        return pltpu.make_async_copy(early[i][0], early[i][1], osem.at[i])

    def late_load(i):
        src, dst = ((a_hbm, opnd), (tok_hbm, dhb), (h, in_grad_out))[i]
        return pltpu.make_async_copy(src, dst, osem.at[len(early) + i])

    def head_loads(i):
        col = pl.ds(pl.multiple_of(i * HEAD_DIM, HEAD_DIM), HEAD_DIM)
        refs = [(kr_hbm, kr), (vr_hbm, vr), (kc_hbm, kc), (vc_hbm, vc)]
        return [
            pltpu.make_async_copy(src.at[:, col], dst, hsem.at[j])
            for j, (src, dst) in enumerate(refs)
        ]

    def weight_load(panel, slot):
        return pltpu.make_async_copy(full_ref.at[panel], wbuf.at[slot], wsem.at[slot])

    def weight(slot):
        return wbuf[slot].reshape(D, D)

    other = seq + 1 - 2 * at.core

    def comp_rows(owner):
        place = jnp.clip(owner - comp_window_first(seq, tok_dev), 0, comp_devs - 1)
        return pair.at[pl.ds(pl.multiple_of(place * comp_dev, comp_dev), comp_dev), :]

    def dc_across(d):
        i = (d + 1) // 2 - at.core
        return remote(comp_rows(seq - d), dc_beside.at[i], dbs.at[d // 2], dbr.at[i], at.core_dev)

    def dc_join(d):
        i = d // 2

        @pl.when(needs_comp(other, seq - d, tok_dev))
        def _():
            remote(comp_rows(seq - d), dc_beside.at[i], dbs.at[0], dbr.at[i], at.core_dev).wait_recv()
            add(comp_rows(seq - d), dc_beside.at[i])

    def gives_back(d):
        return chain_needs_comp(seq, seq - d, tok_dev, seq_count, reach - 1)

    def takes_back(d):
        return chain_needs_comp(seq + 2, seq - d, tok_dev, seq_count, reach - 1)

    def dc_back(d):
        i = d // 2 - 1
        return remote(comp_rows(seq - d), dc_chain.at[i], dcs.at[i], dcr.at[i], at.seq_dev(-2))

    def dc_arrival(d):
        i = d // 2
        return remote(comp_rows(seq), dc_chain.at[i], dcs.at[0], dcr.at[i], at.seq_dev(-2))

    def pass_back(d):
        @pl.when((d + 2 < reach) & takes_back(d))
        def _():
            dc_arrival(d).wait_recv()
            add(comp_rows(seq - d), dc_chain.at[d // 2])

        pl.when(gives_back(d))(lambda: dc_back(d).start())

    chain = [d for d in range(2, reach + 1, 2)]
    odds = [d for d in range(1, reach + 1, 2)]

    odd = at.core == 1
    even = at.core == 0

    def raw_rows(d):
        return dkr.at[token_rows(raw_devs - 1 - d), :]

    def da_copy(d, i, place, device):
        return remote(raw_rows(d), da_in.at[place], das.at[i], dar.at[place], device)

    def da_join(d):
        return da_copy(d, 0, 0, at.core_dev)

    def da_beside():
        return da_copy(1, 1, 1, at.core_dev)

    def da_back():
        return da_copy(2, 2, 2, at.seq_dev(-2))

    joins_near = even & needs_raw(seq, seq - 1, tok_dev)
    joins_far = odd & needs_raw(seq, seq - 3, tok_dev)
    joined = needs_raw(other, seq - 2, tok_dev)
    gives_beside = odd & needs_raw(seq, seq - 1, tok_dev)
    takes_beside = even & needs_raw(seq + 1, seq, tok_dev)
    gives_raw = needs_raw(seq, seq - 2, tok_dev)
    takes_raw = (seq + 2 < seq_count) & needs_raw(seq + 2, seq, tok_dev)

    def share(i):
        total = times_transposed(dkr[token_rows(i), :], weight(1))
        return total + times_transposed(dvr[token_rows(i), :], weight(2))

    def norm_copy(i):
        device = (at.core_dev, at.x_dev, at.y_dev)[i]
        return remote(n_src.at[i], n_in.at[i], ns.at[i], nr.at[i], device)

    def norm_next(i):
        norm_copy(i).wait_recv()
        n_src[i + 1] = n_src[i] + n_in[i]

    def norm_line(k):
        return remote(n_src.at[3], n_line.at[at.line], nzs.at[k], nzr.at[at.line], at.line_dev(k))

    def norm_line_arrival(k):
        line = at.other_line(k)
        return remote(n_src.at[3], n_line.at[line], nzs.at[k], nzr.at[line], at.line_dev(k))

    def second_norm_back():
        gains, shifts = [], []
        for i in range(tok_dev // QB):
            rows = pl.ds(i * QB, QB)
            back, gain, shift = norm_back(db[rows, :], h[rows, :], params, 2)
            db[rows, :] = opnd[rows, :].astype(F32) + back
            dhb[rows, :] = db[rows, :].astype(BF16)
            gains.append(gain)
            shifts.append(shift)
        n_src[0, 2:3, :] = sum(gains)
        n_src[0, 3:4, :] = sum(shifts)
        do[...] = times_transposed(dhb[...], weight(0)).astype(BF16)

    def first_norm_back():
        gains, shifts = [], []
        for i in range(tok_dev // QB):
            rows = pl.ds(i * QB, QB)
            back, gain, shift = norm_back(h[rows, :], dhb[rows, :].astype(F32), params, 0)
            h[rows, :] = db[rows, :] + back
            gains.append(gain)
            shifts.append(shift)
        n_src[0, 0:1, :] = sum(gains)
        n_src[0, 1:2, :] = sum(shifts)

    def work(t):
        @pl.when(t == 0)
        def _():
            for i in range(tok_dev // QB):
                block_at = Attention(seq, i, tok_dev, raw, comp)
                raw_bias[i] = block_at.raw_bias((RAW_KEYS, QB), 0)
                comp_bias[i] = block_at.comp_bias((COMP_KEYS, QB), 0)
            for j in range(place.shape[0]):
                where = jnp.int32(0)
                for r in range(panels):
                    where = jnp.where(slot_ref[RETURN[r]] == j, r, where)
                place[j] = where
                scale[j] = slot_deviation(slot_ref, j)

        @pl.when(t == 1)
        def _():
            for i in range(2, 6):
                early_load(i).wait()
            weight_load(6, 0).wait()
            second_norm_back()
            weight_load(3, 0).start()

        @pl.when((t >= 2) & (t < 2 + 2 * HEADS))
        def _():
            head = t // 2 - 1
            cols = pl.ds(pl.multiple_of(head * HEAD_DIM, HEAD_DIM), HEAD_DIM)

            def blocks(low, high):
                for i in range(low, high):
                    attend_block_back(
                        seq, tok_dev, i, cols, q, do, o, kr, vr, kc, vc, lse_ref, head,
                        raw_bias, comp_bias, acc_kr, acc_vr, acc_kc, acc_vc,
                    )

            @pl.when(t % 2 == 0)
            def _():
                for copy in head_loads(head):
                    copy.wait()
                for acc in (acc_kr, acc_vr, acc_kc, acc_vc):
                    acc[...] = jnp.zeros_like(acc)
                blocks(0, tok_dev // QB // 2)

            @pl.when(t % 2 == 1)
            def _():
                blocks(tok_dev // QB // 2, tok_dev // QB)
                score = HEAD_DIM ** (-0.5)
                dkr[:, cols] = (acc_kr[...] * score).astype(BF16)
                dkc[:, cols] = (acc_kc[...] * score).astype(BF16)
                dvr[:, cols] = acc_vr[...].astype(BF16)
                dvc[:, cols] = acc_vc[...].astype(BF16)

                @pl.when(head + 1 < HEADS)
                def _():
                    for copy in head_loads(head + 1):
                        copy.start()

        @pl.when(t == 18)
        def _():
            weight_load(4, 1).wait()
            weight_load(5, 2).wait()
            half = comp // 2
            for i in range(2):
                rows = pl.ds(i * half, half)
                total = times_transposed(dkc[rows, :], weight(1))
                total = total + times_transposed(dvc[rows, :], weight(2))
                pair[rows, :] = total.astype(BF16)
            for d in odds:
                pl.when(needs_comp(seq, seq - d, tok_dev))(lambda d=d: dc_across(d).start())

        @pl.when(t == 19)
        def _():
            for d in chain:
                dc_join(d)

        for i, d in enumerate(reversed(chain)):
            pl.when(t == 19 + i)(lambda d=d: pass_back(d))

        @pl.when(t == 20)
        def _():
            weight_load(3, 0).wait()
            h[...] = times_transposed(q[...], weight(0))
            weight_load(0, 0).start()

        @pl.when(t == 24)
        def _():
            raw_rows(1)[...] = share(raw_devs - 2).astype(BF16)
            pl.when(joins_near)(lambda: da_join(1).start())
            pl.when(gives_beside)(lambda: da_beside().start())

            @pl.when(joins_far)
            def _():
                raw_rows(3)[...] = share(raw_devs - 4).astype(BF16)
                da_join(3).start()

        @pl.when(t == 25)
        def _():
            raw_rows(2)[...] = share(raw_devs - 3).astype(BF16)
            h[...] += share(raw_devs - 1)
            weight_load(1, 1).start()
            weight_load(2, 2).start()

        @pl.when(t == 23)
        def _():
            taken = takes_back(0)

            @pl.when(taken)
            def _():
                dc_arrival(0).wait_recv()
                dc[...] = dc_chain[0]

            @pl.when(jnp.logical_not(taken))
            def _():
                dc[...] = jnp.zeros_like(dc)

        @pl.when(t == 26)
        def _():
            @pl.when(joined)
            def _():
                da_join(2).wait_recv()
                add(raw_rows(2), da_in.at[0])

            pl.when(gives_raw)(lambda: da_back().start())

        @pl.when(t == 28)
        def _():
            for panel in range(3):
                weight_load(panel, panel).wait()
            heads_of = acc_kr.shape[0] // tok_dev
            for k in range(3):
                total = times_transposed(dc[...], weight(k))
                for c in range(HEADS):
                    acc = (acc_kr, acc_vr)[c // heads_of]
                    place = pl.ds(c % heads_of * tok_dev + k, comp_dev, stride=3)
                    acc[place, :] = total[:, c * HEAD_DIM : (c + 1) * HEAD_DIM]
            for c in range(HEADS):
                acc = (acc_kr, acc_vr)[c // heads_of]
                cols = pl.ds(c * HEAD_DIM, HEAD_DIM)
                h[:, cols] += acc[pl.ds(c % heads_of * tok_dev, tok_dev), :]
            for d in odds:
                pl.when(needs_comp(seq, seq - d, tok_dev))(lambda d=d: dc_across(d).wait_send())
            for d in chain:
                pl.when(gives_back(d))(lambda d=d: dc_back(d).wait_send())
            late_load(1).start()

        @pl.when(t == 30)
        def _():
            @pl.when(takes_raw)
            def _():
                da_back().wait_recv()
                h[...] += da_in[2].astype(F32)

            @pl.when(takes_beside)
            def _():
                da_beside().wait_recv()
                h[...] += da_in[1].astype(F32)

            pl.when(joins_near)(lambda: da_join(1).wait_send())
            pl.when(joins_far)(lambda: da_join(3).wait_send())
            pl.when(gives_beside)(lambda: da_beside().wait_send())
            pl.when(gives_raw)(lambda: da_back().wait_send())
            late_load(1).wait()
            first_norm_back()
            norm_copy(0).start()
            late_load(2).start()

        for i in range(2):

            @pl.when(t == 31 + i)
            def _(i=i):
                norm_next(i)
                norm_copy(i + 1).start()

        @pl.when(t == 33)
        def _():
            norm_next(2)
            n_line[at.line] = n_src[3]
            for k in range(1, lines):
                norm_line(k).start()

    def make(t):
        @pl.when(t < 4 * RATIO)
        def _():
            p = t // 2

            @pl.when(t % 2 == 0)
            def _():
                pl.when(p + 1 < 2 * RATIO)(lambda: left_start(p + 1))
                left_load(p, z_hbm).wait()
                pl.when(p == 0)(lambda: early_load(0).wait())
                pl.when(p == RATIO)(lambda: early_load(1).wait())
                turn(opnd.at[token_rows(2 + p % 2), :], 0)

            produce(t, (0, opnd.at[token_rows(p // RATIO), :]))
            pl.when(t == 4 * RATIO - 1)(lambda: late_load(0).start())

        base = 4 * RATIO
        pl.when(t == base)(lambda: turn(o, 0))
        pl.when(t // 2 == base // 2)(lambda: produce(t, (0, dhb)))

        @pl.when(t == base + 2)
        def _():
            late_load(0).wait()
            early_load(6).wait()
            early_load(7).wait()
            turn(opnd.at[token_rows(raw_devs - 1), :], raw - tok_dev)

        pl.when(t // 2 == base // 2 + 1)(lambda: produce(t, (raw - tok_dev, q)))

        @pl.when(t == base + 3)
        def _():
            for i in range(raw_devs - 1):
                turn(opnd.at[token_rows(i), :], i * tok_dev)
            for i in range(comp // tok_dev):
                turn(c_win.at[token_rows(i), :], raw + i * tok_dev)

        pl.when(t // 2 == base // 2 + 2)(lambda: produce(t, (0, dkr), (raw, dkc)))
        pl.when(t // 2 == base // 2 + 3)(lambda: produce(t, (0, dvr), (raw, dvc)))
        for k in range(3):
            pl.when(t == base + 8 + 2 * k)(lambda k=k: turn(a3.at[k], 0))
        pl.when((t >= base + 8) & (t < base + 14))(lambda: produce(t, (0, dc)))

    at.announce()
    for i in range(len(early)):
        early_load(i).start()
    left_load(0, z_hbm).start()
    for panel, slot in ((6, 0), (4, 1), (5, 2)):
        weight_load(panel, slot).start()
    for copy in head_loads(0):
        copy.start()
    at.enter()

    def step(t, carry):
        pl.when((t >= 1) & (t < chunks + 1))(lambda: start_first(t - 1))
        pl.when((t >= 2) & (t < chunks + 2))(lambda: start_second(t - 2))
        pl.when((t >= 3) & (t < chunks + 3))(lambda: start_lines(t - 3))
        pl.when(t >= BACK_LAG)(lambda: finish(t - BACK_LAG))
        pl.when(t < chunks)(lambda: make(t))
        work(t)
        return carry

    lax.fori_loop(0, chunks + BACK_LAG, step, 0)
    count = slot_out.shape[0]
    for j in range(4 * count):
        slots[j] = (out[place[j]].astype(F32) * scale[j]).astype(BF16)
    handed = at.exchange(slots, slots_in, es, er)
    for copy in handed:
        copy.start()
    slots_in[pl.ds(at.grp * count, count)] = slots[pl.ds(at.grp * count, count)]
    for i in range(3):
        norm_copy(i).wait_send()
    for k in range(1, lines):
        norm_line_arrival(k).wait_recv()
        norm_line(k).wait_send()
    total = n_line[0]
    for i in range(1, lines):
        total = total + n_line[i]
    norm_out[...] = total
    late_load(2).wait()
    for copy in handed:
        copy.wait_send()
        copy.wait_recv()
    for g in range(4):
        for j in range(count):
            slot_out[j, :, pl.ds(g * wide, wide)] = slots_in[g * count + j]


def backward(panel_slot, all_slots, weights, arrays, lse, norm_params, lines):
    panels, rows = weights.shape[0], weights.shape[4]
    wide, pairs, half_rows = D // 4, lines // 2, weights.shape[4] // 2
    a_win, c_win = arrays[0], arrays[1]
    tok_dev = arrays[3].shape[0]
    raw, comp, comp_dev = a_win.shape[0], c_win.shape[0], tok_dev // 3
    raw_devs, blocks = raw // tok_dev, tok_dev // QB
    reach = min(2 * lines - 1, (2 * S + 3 * CM + tok_dev - 1) // tok_dev)
    dma = pltpu.SemaphoreType.DMA
    regular = pltpu.SemaphoreType.REGULAR
    any_spec, vmem = pl.BlockSpec(memory_space=pl.ANY), pl.BlockSpec(memory_space=pltpu.VMEM)
    smem = pl.BlockSpec(memory_space=pltpu.SMEM)

    def buffer(kind, *shape):
        return pltpu.VMEM(shape, kind)

    return pl.pallas_call(
        functools.partial(backward_kernel, panels, lines),
        out_shape=[
            jax.ShapeDtypeStruct((all_slots // 4, rows, D), BF16),
            jax.ShapeDtypeStruct((tok_dev, D), F32),
            jax.ShapeDtypeStruct((4, D), F32),
        ],
        in_specs=[smem] + [any_spec] * (1 + len(arrays)) + [vmem] * 2,
        out_specs=[vmem, any_spec, vmem],
        scratch_shapes=[
            buffer(BF16, HELD, pairs, 2, 2, 2, 2, half_rows, wide),
            buffer(BF16, RING, pairs, 2, 2, 2, half_rows, wide),
            buffer(BF16, RING, 2, pairs, 2, half_rows, wide),
            buffer(BF16, RING, 2, pairs, half_rows, wide),
            buffer(BF16, 2 * panels, lines - 1, half_rows, wide),
            buffer(BF16, panels, rows, wide),
            buffer(BF16, all_slots, rows, wide),
            buffer(BF16, all_slots, rows, wide),
            buffer(BF16, raw, D),
            buffer(BF16, 2 * pairs, 2, 2, half_rows, raw + comp),
            buffer(BF16, comp, D),
            buffer(BF16, 3, comp_dev, D),
            buffer(F32, tok_dev, D),
            buffer(F32, tok_dev, D),
            buffer(F32, tok_dev, D),
            buffer(BF16, max(comp, 2 * tok_dev), D),
            buffer(BF16, tok_dev, D),
            buffer(BF16, raw, HEAD_DIM),
            buffer(BF16, raw, HEAD_DIM),
            buffer(BF16, comp, HEAD_DIM),
            buffer(BF16, comp, HEAD_DIM),
            buffer(F32, raw, HEAD_DIM),
            buffer(F32, raw, HEAD_DIM),
            buffer(F32, comp, HEAD_DIM),
            buffer(F32, comp, HEAD_DIM),
            buffer(F32, blocks, RAW_KEYS, QB),
            buffer(F32, blocks, COMP_KEYS, QB),
            pltpu.SMEM((all_slots,), jnp.int32),
            pltpu.SMEM((all_slots,), F32),
            buffer(BF16, raw, D),
            buffer(BF16, raw, D),
            buffer(BF16, comp, D),
            buffer(BF16, comp, D),
            buffer(BF16, 3, pairs, 2, 2, rows, D),
            buffer(BF16, comp_dev, D),
            buffer(BF16, reach // 2 + 2, comp_dev, D),
            buffer(BF16, reach // 2 + 1, comp_dev, D),
            buffer(BF16, 3, tok_dev, D),
            buffer(F32, 4, 4, D),
            buffer(F32, 3, 4, D),
            buffer(F32, lines, 4, D),
            dma((RING,)), dma((RING,)),
            dma((RING, 2)), dma((RING, 2)),
            dma((RING, 2)), dma((RING, 2)),
            dma((2 * panels, lines)), dma((2 * panels, lines)),
            regular, regular((2,)), regular((2,)),
            dma((2,)), dma((11,)), dma((4,)), dma((3,)),
            dma((reach // 2 + 2,)), dma((reach // 2 + 2,)),
            dma((reach // 2 + 1,)), dma((reach // 2 + 1,)),
            dma((3,)), dma((3,)),
            dma((3,)), dma((3,)),
            dma((lines,)), dma((lines,)),
            dma((3,)), dma((3,)),
        ],
        compiler_params=pltpu.CompilerParams(
            collective_id=1, has_side_effects=True, vmem_limit_bytes=62 * MIB
        ),
        name="backward",
    )(panel_slot, weights, *arrays, lse, norm_params)


def local(
    tokens, cotangent, master, first_moment, second_moment, norm_params, norm_first, norm_second,
    seg_valid, book_of_group, panel_slot,
):
    lines = lax.axis_size("seq") // 2
    all_slots = master.shape[0] * lax.axis_size("grp")
    results = forward(
        panel_slot, book_of_group, seg_valid, master, tokens, cotangent, norm_params, lines
    )
    weights, saved, log_total, mixed = results[0], results[1:-2], results[-2], results[-1]
    a_win, c_win, q, kr, vr, kc, vc, o, z, df, b, h, db, a3, grad_out = saved
    arrays = (a_win, c_win, a3, q, kr, vr, kc, vc, o, z, df, b, h, db, grad_out, tokens)
    slot_sums, input_grad, norm_grad = backward(
        panel_slot, all_slots, weights, arrays, log_total, norm_params, lines
    )
    slot_grad = slot_sums.astype(F32)
    slot_first, slot_second, slot_weight = adam_update(
        slot_grad, first_moment, second_moment, master, SLOT_RATE
    )
    norm_first_new, norm_second_all, norm_weight = adam_update(
        norm_grad, norm_first, norm_second, norm_params, NORM_RATE
    )
    return (
        mixed, input_grad, slot_grad, slot_first, slot_second, slot_weight, norm_grad,
        norm_first_new, norm_second_all[:2], norm_second_all[2:], norm_weight,
    )


def solution(mesh):
    rows, slots, whole = P(("grp", "seq"), None), P("grp", "seq", None), P()
    return jax.shard_map(
        local,
        mesh=mesh,
        in_specs=(rows, rows, slots, slots, slots) + (whole,) * 6,
        out_specs=(rows, rows, slots, slots, slots, slots) + (whole,) * 5,
        check_vma=False,
    )
```

```python
import functools

import jax
import jax.numpy as jnp
from jax import lax
from jax.experimental import pallas as pl
from jax.experimental.pallas import tpu as pltpu
from jax.sharding import PartitionSpec as P

D = 1024
HEADS = 8
HEAD_DIM = 128
FF = 4096
S = 512
CM = 512
STEP = 10
PANELS = 15
RATIO = FF // D
QB = 128
RAW_KEYS = 2 * S
COMP_KEYS = CM + QB
MIB = 1 << 20

NEG_SCORE = -1e30
NORM_EPS = 1e-05
BETA_ONE = 0.9
BETA_TWO = 0.999
WEIGHT_DECAY = 0.1
ADAM_EPS = 1e-08
NORM_RATE = 1.0
SLOT_RATE = 2.0
BF16 = jnp.bfloat16
F32 = jnp.float32
MESH = pl.DeviceIdType.MESH


def layer_norm(values, gain, shift):
    row_mean = jnp.mean(values, axis=-1, keepdims=True)
    centered = values - row_mean
    variance = jnp.mean(centered * centered, axis=-1, keepdims=True)
    return centered * lax.rsqrt(variance + NORM_EPS) * gain + shift


DEVIATIONS = [D ** (-0.5)] * 3 + [(D // (2 * S)) ** (-0.5)] + [D ** (-0.5)] * RATIO
DEVIATIONS = DEVIATIONS + [FF ** (-0.5)] * RATIO + [(3 * D) ** (-0.5)] * 3


def slot_deviation(panel_slot, slot):
    scale = jnp.float32(0.0)
    for panel in range(PANELS):
        scale = jnp.where(panel_slot[panel] == slot, jnp.float32(DEVIATIONS[panel]), scale)
    return scale


def adam_update(gradient, first_old, second_old, weight_old, step_rate):
    first_new = BETA_ONE * first_old + (1.0 - BETA_ONE) * gradient
    second_new = BETA_TWO * second_old + (1.0 - BETA_TWO) * gradient * gradient
    fix_one = 1.0 - BETA_ONE**STEP
    fix_two = 1.0 - BETA_TWO**STEP
    movement = first_new / fix_one / (jnp.sqrt(second_new / fix_two) + ADAM_EPS)
    return (first_new, second_new, weight_old - step_rate * (movement + WEIGHT_DECAY * weight_old))


def matmul(left, right):
    return jnp.dot(left, right, preferred_element_type=F32)


def times_transposed(left, right):
    return lax.dot_general(left, right, (((1,), (1,)), ((), ())), preferred_element_type=F32)


def contract_rows(left, right):
    return lax.dot_general(left, right, (((0,), (0,)), ((), ())), preferred_element_type=F32)


class Place:
    def __init__(self, lines):
        self.lines = lines
        self.grp = lax.axis_index("grp")
        self.seq = lax.axis_index("seq")
        self.line = self.seq // 2
        self.core = self.seq % 2
        self.row = self.grp // 2
        self.col = self.grp % 2
        self.grp_x = self.row * 2 + 1 - self.col
        self.grp_y = (1 - self.row) * 2 + self.col
        self.x_dev = {"grp": self.grp_x, "seq": self.seq}
        self.y_dev = {"grp": self.grp_y, "seq": self.seq}
        self.far_dev = {"grp": 3 - self.grp, "seq": self.seq}
        self.core_dev = {"grp": self.grp, "seq": self.line * 2 + 1 - self.core}

    def other_line(self, k):
        return lax.rem(self.line + k, self.lines)

    def line_dev(self, k):
        return {"grp": self.grp, "seq": self.other_line(k) * 2 + self.core}

    def seq_dev(self, d):
        count = 2 * self.lines
        return {"grp": self.grp, "seq": lax.rem(self.seq + d + count, count)}

    def announce(self):
        barrier = pltpu.get_barrier_semaphore()
        partners = [self.seq_dev(d) for d in range(1, 2 * self.lines)]
        for device in partners + [self.x_dev, self.y_dev, self.far_dev]:
            pl.semaphore_signal(barrier, inc=1, device_id=device, device_id_type=MESH)

    def enter(self):
        pl.semaphore_wait(pltpu.get_barrier_semaphore(), 2 * self.lines + 2)

    def exchange(self, parts, arrived, send, recv):
        count = parts.shape[0] // 4
        copies = []
        for i, device in enumerate((self.x_dev, self.y_dev, self.far_dev)):
            src = parts.at[pl.ds(device["grp"] * count, count)]
            dst = arrived.at[pl.ds(self.grp * count, count)]
            copies.append(remote(src, dst, send.at[i], recv.at[i], device))
        return copies


def remote(src, dst, send, recv, device):
    return pltpu.make_async_remote_copy(
        src_ref=src,
        dst_ref=dst,
        send_sem=send,
        recv_sem=recv,
        device_id=device,
        device_id_type=MESH,
    )


def memory_start(position):
    return (position // S - 1) * S


def comp_window_first(seq, tok_dev):
    return jnp.maximum(memory_start(seq * tok_dev) - 3 * CM, 0) // tok_dev


def raw_devices(tok_dev):
    return (RAW_KEYS - QB + tok_dev - 1) // tok_dev + 1


def comp_devices(tok_dev, seq_count):
    return min((3 * CM + S) // tok_dev + 1, seq_count)


def needs_raw(reader, owner, tok_dev):
    return (owner >= 0) & ((owner + 1) * tok_dev > memory_start(reader * tok_dev))


def needs_comp(reader, owner, tok_dev):
    last = jnp.maximum(memory_start(reader * tok_dev + tok_dev - 1), 0) // 3
    inside = (owner >= 0) & (owner >= comp_window_first(reader, tok_dev))
    return inside & (owner * (tok_dev // 3) < last)


def chip_needs_comp(reader, owner, tok_dev):
    even = reader // 2 * 2
    return needs_comp(even, owner, tok_dev) | needs_comp(even + 1, owner, tok_dev)


def chain_needs_comp(reader, owner, tok_dev, seq_count, reach):
    needed = chip_needs_comp(reader, owner, tok_dev)
    for ahead in range(2, reach + 1, 2):
        later = reader + ahead
        needed = needed | ((later < seq_count) & chip_needs_comp(later, owner, tok_dev))
    return needed & (owner >= 0) & (reader < seq_count)


def block_window(seq, i, tok_dev, raw_rows, comp_rows):
    position = seq * tok_dev + i * QB
    memory = memory_start(position)
    raw_base = (seq + 1) * tok_dev - raw_rows
    raw_at = jnp.minimum(memory - raw_base, raw_rows - RAW_KEYS)
    comp_end = jnp.maximum(memory, 0) // 3
    comp_low = jnp.maximum(comp_end - CM, 0)
    comp_base = comp_window_first(seq, tok_dev) * (tok_dev // 3)
    comp_at = jnp.minimum((comp_low - comp_base) // QB * QB, comp_rows - COMP_KEYS)
    return (
        position,
        pl.multiple_of(raw_at, QB),
        pl.multiple_of(comp_at, QB),
        raw_base + raw_at,
        comp_base + comp_at,
        memory,
        comp_low,
        comp_end,
    )


def row_sum(values):
    return jnp.sum(values, axis=1, keepdims=True)


def norm_rows(values, params, first):
    mean = row_sum(values) * (1.0 / D)
    centered = values - mean
    variance = row_sum(centered * centered) * (1.0 / D)
    gain, shift = params[first : first + 1, :], params[first + 1 : first + 2, :]
    return centered * lax.rsqrt(variance + NORM_EPS) * gain + shift


GELU_IN = (2.0 / 3.141592653589793) ** 0.5
GELU_CUBE = 0.044715


def gelu_pair(f):
    square = f * f
    t = jnp.tanh(GELU_IN * f * (1.0 + GELU_CUBE * square))
    half = 0.5 * (1.0 + t)
    slope = half + 0.5 * f * (1.0 - t * t) * (GELU_IN * (1.0 + 3.0 * GELU_CUBE * square))
    return f * half, slope


class Attention:
    def __init__(self, seq, i, tok_dev, raw_rows, comp_rows):
        place = block_window(seq, i, tok_dev, raw_rows, comp_rows)
        self.pos, raw_at, comp_at, self.raw_pos, self.comp_pos = place[:5]
        self.memory, self.comp_low, self.comp_end = place[5:]
        self.rows = pl.ds(i * QB, QB)
        self.raw = pl.ds(raw_at, RAW_KEYS)
        self.comp = pl.ds(comp_at, COMP_KEYS)

    def raw_bias(self, shape, key_dim):
        key_pos = self.raw_pos + lax.broadcasted_iota(jnp.int32, shape, key_dim)
        query_pos = self.pos + lax.broadcasted_iota(jnp.int32, shape, 1 - key_dim)
        seen = (key_pos >= jnp.maximum(self.memory, 0)) & (key_pos <= query_pos)
        return jnp.where(seen, 0.0, NEG_SCORE)

    def comp_bias(self, shape, key_dim):
        index = self.comp_pos + lax.broadcasted_iota(jnp.int32, shape, key_dim)
        return jnp.where((index >= self.comp_low) & (index < self.comp_end), 0.0, NEG_SCORE)


SCORE_SCALE = HEAD_DIM ** (-0.5) * 1.4426950408889634


def attend_head(seq, tok_dev, head, q, kr, vr, kc, vc, out, lse, raw_bias, comp_bias):
    cols = pl.ds(pl.multiple_of(head * HEAD_DIM, HEAD_DIM), HEAD_DIM)
    for i in range(tok_dev // QB):
        at = Attention(seq, i, tok_dev, kr.shape[1], kc.shape[1])
        query = q[at.rows, cols]
        raw = times_transposed(query, kr[head, at.raw, :]) * SCORE_SCALE + raw_bias[i]
        comp = times_transposed(query, kc[head, at.comp, :]) * SCORE_SCALE + comp_bias[i]
        top = jnp.maximum(
            jnp.max(raw, axis=1, keepdims=True), jnp.max(comp, axis=1, keepdims=True)
        )
        raw = jnp.exp2(raw - top)
        comp = jnp.exp2(comp - top)
        total = row_sum(raw) + row_sum(comp)
        mixed = matmul(raw.astype(BF16), vr[head, at.raw, :])
        mixed = mixed + matmul(comp.astype(BF16), vc[head, at.comp, :])
        out[at.rows, cols] = mixed / total
        stat = jnp.broadcast_to(top + jnp.log2(total), (QB, QB))
        lse[head, :, at.rows] = stat.T[:8]


TAPS = [4 + 2 * RATIO + i for i in range(3)]
ARRIVAL = TAPS + [0, 1, 2, 3]
for _i in range(RATIO):
    ARRIVAL = ARRIVAL + [4 + _i, 4 + RATIO + _i]
AHEAD = 4
LAG = 4
SEMS = 8
KEPT = 4


def forward_kernel(
    panels, lines,
    slot_ref, book_ref, seg_ref, master_ref, tok_ref, cot_ref, norm_ref,
    full_ref, a_out, c_out, q_out, kr_out, vr_out, kc_out, vc_out, o_out, z_out, df_out, b_out,
    h_out, db_out, a3_out, dy_out, lse_ref, mixed_ref,
    wbuf, a_win, a3, c_win, q, kr, vr, kc, vc, o, z, df, b, h, y, db, dy_ref, slots, slots_a, slots_b,
    block, normed, raw_bias, comp_bias,
    own_sem, zs, zr, s1, r1, s2, r2, cs, cr, wsem, a_s, a_r, c_s, c_r, f_s, f_r, es, er, out_sem,
    hidden_sem,
):
    at = Place(lines)
    seq = at.seq
    seq_count = 2 * lines
    chunks = 2 * panels
    tok_dev = tok_ref.shape[0]
    comp_dev = tok_dev // 3
    raw_devs = a_win.shape[0] // tok_dev
    comp_devs = c_win.shape[0] // comp_dev
    reach = min(seq_count - 1, (2 * S + 3 * CM + tok_dev - 1) // tok_dev)
    wide = block.shape[-1]
    half_rows = block.shape[1] // 2

    def cols(g):
        return pl.ds(pl.multiple_of(g * wide, wide), wide)

    def panel_of(u):
        return jnp.where(u < 4, u % 2, u // 2)

    def rows_of(u):
        half = jnp.where(u < 4, u // 2, u % 2)
        return pl.ds(pl.multiple_of(half * half_rows, half_rows), half_rows)

    def line_place(u, line):
        return full_ref.at[panel_of(u), line // 2, line % 2, at.core, rows_of(u), cols(at.grp)]

    def line_copy(u, k):
        src = block.at[panel_of(u), rows_of(u), :]
        return remote(src, line_place(u, at.line), zs.at[u, k], zr.at[u, at.line], at.line_dev(k))

    def line_arrival(u, k):
        src, line = block.at[panel_of(u), rows_of(u), :], at.other_line(k)
        return remote(src, line_place(u, line), zs.at[u, k], zr.at[u, line], at.line_dev(k))

    def part(u, half, g):
        return full_ref.at[panel_of(u), :, half, at.core, rows_of(u), cols(g)]

    def first(u, half, g):
        device, i = (at.x_dev if half == 0 else at.y_dev), u % SEMS
        return remote(part(u, half, g), part(u, half, g), s1.at[i, half], r1.at[i, half], device)

    def second(u, half, j, g):
        device, i = (at.y_dev if half == 0 else at.x_dev), u % SEMS
        ref = part(u, half, g)
        return remote(ref, ref, s2.at[i, half, j], r2.at[i, half, j], device)

    def cross(u, half, core):
        ref, i = full_ref.at[panel_of(u), :, half, core, rows_of(u)], u % SEMS
        return remote(ref, ref, cs.at[i, half], cr.at[i, half], at.core_dev)

    def load(u):
        p = panel_of(u)
        src = full_ref.at[p, :, :, :, rows_of(u)]
        dst = wbuf.at[p % KEPT, :, :, :, rows_of(u)]
        return pltpu.make_async_copy(src, dst, wsem.at[u % SEMS])

    def start_lines(u):
        for k in range(1, lines):
            line_copy(u, k).start()

    def start_first(u):
        for k in range(1, lines):
            line_arrival(u, k).wait_recv()
        for half in (0, 1):
            first(u, half, at.grp).start()

    def start_second(u):
        for half in (0, 1):
            near = at.grp_x if half == 0 else at.grp_y
            first(u, half, near).wait_recv()
            second(u, half, 0, at.grp).start()
            second(u, half, 1, near).start()

    def start_cross(u):
        for half in (0, 1):
            second(u, half, 0, at.grp_y if half == 0 else at.grp_x).wait_recv()
            second(u, half, 1, 3 - at.grp).wait_recv()
            cross(u, half, at.core).start()

    def finish(u):
        for half in (0, 1):
            cross(u, half, 1 - at.core).wait_recv()
            first(u, half, at.grp).wait_send()
            second(u, half, 0, at.grp).wait_send()
            second(u, half, 1, at.grp_x if half == 0 else at.grp_y).wait_send()
            cross(u, half, at.core).wait_send()
        for k in range(1, lines):
            line_copy(u, k).wait_send()
        load(u).start()

    def a_rows(d):
        return a_win.at[pl.ds((raw_devs - 1 - d) * tok_dev, tok_dev), :]

    def a_copy(d, place, i, device):
        return remote(a_rows(d), a_rows(place), a_s.at[i], a_r.at[place - 1], device)

    def a_next():
        return a_copy(0, 2, 0, at.seq_dev(2))

    def a_beside():
        return a_copy(0, 1, 1, at.core_dev)

    def a_on(place):
        return a_copy(2, place, 2, at.core_dev)

    odd = at.core == 1
    even = at.core == 0
    gives_next = (seq + 2 < seq_count) & needs_raw(seq + 2, seq, tok_dev)
    gives_beside = even & needs_raw(seq + 1, seq, tok_dev)
    gives_on_far = even & needs_raw(seq + 1, seq - 2, tok_dev)
    gives_on_near = odd & needs_raw(seq - 1, seq - 2, tok_dev)

    def c_rows(reader, owner):
        place = jnp.clip(owner - comp_window_first(reader, tok_dev), 0, comp_devs - 1)
        return c_win.at[pl.ds(pl.multiple_of(place * comp_dev, comp_dev), comp_dev), :]

    def c_from(d):
        return own_c if d == 0 else c_rows(seq, seq - d)

    def c_next(d):
        dst = c_rows(seq + 2, seq - d)
        return remote(c_from(d), dst, c_s.at[d // 2], c_r.at[d // 2 + 1], at.seq_dev(2))

    def c_arrival(d):
        return remote(own_c, c_rows(seq, seq - d), c_s.at[0], c_r.at[d // 2], at.seq_dev(2))

    def c_across(d):
        other = seq + 1 - 2 * at.core
        dst = c_rows(other, seq - d)
        return remote(c_from(d), dst, f_s.at[d // 2], f_r.at[d // 2], at.core_dev)

    def c_across_arrival(d):
        other = seq + 1 - 2 * at.core
        return remote(own_c, c_rows(seq, other - d), f_s.at[0], f_r.at[d // 2], at.core_dev)

    steps_back = [d for d in range(0, reach + 1, 2)]

    def gives_c(d):
        return chain_needs_comp(seq + 2, seq - d, tok_dev, seq_count, reach - 1)

    def takes_c(d):
        return chain_needs_comp(seq, seq - d, tok_dev, seq_count, reach - 1)

    def gives_c_across(d):
        return needs_comp(seq + 1 - 2 * at.core, seq - d, tok_dev)

    def takes_c_across(d):
        return needs_comp(seq, seq + 1 - 2 * at.core - d, tok_dev)

    def pass_c(d):
        if d > 0:
            pl.when(takes_c(d))(lambda: c_arrival(d).wait_recv())
        pl.when(gives_c(d))(lambda: c_next(d).start())
        pl.when(gives_c_across(d))(lambda: c_across(d).start())

    outs = [
        (a_win, a_out), (c_win, c_out), (q, q_out), (kr, kr_out), (vr, vr_out), (kc, kc_out),
        (vc, vc_out), (o, o_out), (b, b_out), (h, h_out), (db, db_out), (a3, a3_out), (dy_ref, dy_out),
    ]

    def flush(*names):
        for i, (src, dst) in enumerate(outs):
            if any(src is name for name in names):
                pltpu.make_async_copy(src, dst, out_sem.at[i]).start()

    def flush_hidden(pair):
        return [
            pltpu.make_async_copy(src.at[pair], dst.at[pair], hidden_sem.at[i, pair])
            for i, (src, dst) in enumerate(((z, z_out), (df, df_out)))
        ]

    at.announce()
    count = master_ref.shape[0]
    halves = [pl.ds(i * half_rows, half_rows) for i in range(2)]
    arrived = (slots_a, slots_b)
    handed = [
        at.exchange(slots.at[:, halves[i]], arrived[i], es.at[i], er.at[i]) for i in range(2)
    ]

    def hand(i):
        for j in range(count):
            scale = slot_deviation(slot_ref, at.grp * count + j)
            scaled = (master_ref[j, halves[i], :] * scale).astype(BF16)
            for g in range(4):
                slots[g * count + j, halves[i], :] = scaled[:, g * wide : (g + 1) * wide]
        if i == 0:
            at.enter()
        for copy in handed[i]:
            copy.start()
        own = pl.ds(at.grp * count, count)
        arrived[i][own] = slots[own, halves[i], :]

    def take(i):
        for copy in handed[i]:
            copy.wait_recv()
        for p in range(panels):
            block[p, halves[i], :] = arrived[i][slot_ref[ARRIVAL[p]]]
        src = block.at[:, halves[i], :]
        dst = full_ref.at[:, at.line // 2, at.line % 2, at.core, halves[i], cols(at.grp)]
        pltpu.make_async_copy(src, dst, own_sem.at[i]).start()

    hand(0)
    params = norm_ref[...]
    for i in range(tok_dev // QB):
        rows = pl.ds(i * QB, QB)
        mine = norm_rows(tok_ref[rows, :].astype(F32), params, 0)
        a_win[pl.ds((raw_devs - 1) * tok_dev + i * QB, QB), :] = mine.astype(BF16)
        for c in range(HEADS):
            normed[c, rows, :] = mine[:, c * HEAD_DIM : (c + 1) * HEAD_DIM]
    pl.when(gives_next)(lambda: a_next().start())
    pl.when(gives_beside)(lambda: a_beside().start())
    hand(1)
    for d in range(1, raw_devs):
        absent = jnp.logical_not(needs_raw(seq, seq - d, tok_dev))

        @pl.when(absent)
        def _(d=d):
            a_rows(d)[...] = jnp.zeros((tok_dev, D), BF16)

    for k in range(3):
        for c in range(HEADS):
            rows = pl.ds(k, comp_dev, stride=3)
            a3[k, :, pl.ds(c * HEAD_DIM, HEAD_DIM)] = normed[c, rows, :].astype(BF16)
    book = jnp.int32(0)
    for g in range(4):
        book = jnp.where(at.grp == g, book_ref[g], book)
    valid = []
    for i in range(tok_dev // QB):
        rows = pl.ds(i * QB, QB)
        pos = seq * tok_dev + i * QB
        inside = pos % S + lax.broadcasted_iota(jnp.int32, (QB, D), 0)
        valid.append(inside < seg_ref[book, pos // S])
        dy_ref[rows, :] = jnp.where(valid[i], cot_ref[rows, :].astype(F32), 0.0).astype(BF16)
        block_at = Attention(seq, i, tok_dev, kr.shape[1], kc.shape[1])
        raw_bias[i] = block_at.raw_bias((QB, RAW_KEYS), 1)
        comp_bias[i] = block_at.comp_bias((QB, COMP_KEYS), 1)
    for i in range(comp_devs):
        owner = comp_window_first(seq, tok_dev) + i
        taken = needs_comp(seq, owner, tok_dev)
        for d in steps_back[1:]:
            taken = taken | ((owner == seq - d) & takes_c(d))

        @pl.when(jnp.logical_not(taken))
        def _(i=i):
            c_win[pl.ds(i * comp_dev, comp_dev), :] = jnp.zeros((comp_dev, D), BF16)

    take(0)
    start_lines(0)
    start_lines(1)
    take(1)
    for u in range(2, AHEAD):
        start_lines(u)
    for i in range(2):
        src = block.at[:, halves[i], :]
        dst = full_ref.at[:, at.line // 2, at.line % 2, at.core, halves[i], cols(at.grp)]
        pltpu.make_async_copy(src, dst, own_sem.at[i]).wait()

    own_c = b.at[pl.ds(0, comp_dev), :]
    tile = 8 * half_rows

    def weight(slot, col):
        return wbuf[slot, :, :, :, :, col].reshape(D, wide)

    def columns(body):
        def one(j, carry):
            body(pl.ds(pl.multiple_of(j * wide, wide), wide))
            return carry

        lax.fori_loop(0, D // wide, one, 0)

    def tap(k, slot):
        def body(col):
            part_sum = matmul(a3[k], weight(slot, col))
            if k == 0:
                y[pl.ds(0, comp_dev), col] = part_sum
            elif k == 1:
                y[pl.ds(0, comp_dev), col] += part_sum
            else:
                own_c[:, col] = (y[pl.ds(0, comp_dev), col] + part_sum).astype(BF16)

        columns(body)

    def project(dst, src, slot):
        block_rows = min(src.shape[0], tok_dev)

        def body(col):
            for i in range(src.shape[0] // block_rows):
                rows = pl.ds(i * block_rows, block_rows)
                dst[rows, col] = matmul(src[rows, :], weight(slot, col)).astype(BF16)

        columns(body)

    def project_heads(dst, src, slot):
        block_rows = min(src.shape[0], tok_dev)
        many = wide // HEAD_DIM

        def one(j, carry):
            col = pl.ds(pl.multiple_of(j * wide, wide), wide)
            for i in range(src.shape[0] // block_rows):
                rows = pl.ds(i * block_rows, block_rows)
                made = matmul(src[rows, :], weight(slot, col)).astype(BF16)
                for n in range(many):
                    dst[j * many + n, rows, :] = made[:, n * HEAD_DIM : (n + 1) * HEAD_DIM]
            return carry

        lax.fori_loop(0, D // wide, one, 0)

    def heads(low, high):
        def one(i, carry):
            attend_head(seq, tok_dev, i, q, kr, vr, kc, vc, o, lse_ref, raw_bias, comp_bias)
            return carry

        lax.fori_loop(low, high, one, 0)

    def hidden(pair, low, high):
        up, down = (2 * pair + 7) % KEPT, (2 * pair + 8) % KEPT

        def one(i, carry):
            up_rows = wbuf[up, i].reshape(tile, D)
            down_rows = wbuf[down, i].reshape(tile, D)
            value, slope = gelu_pair(times_transposed(b[...], up_rows))
            units = pl.ds(pl.multiple_of(i * tile, tile), tile)
            z[pair, :, units] = value.astype(BF16)
            df[pair, :, units] = (times_transposed(dy_ref[...], down_rows) * slope).astype(BF16)
            return carry

        lax.fori_loop(low, high, one, 0)

    def gather_hidden(pair):
        up, down = (2 * pair + 7) % KEPT, (2 * pair + 8) % KEPT

        def body(col):
            y[:, col] += matmul(z[pair], weight(down, col))
            db[:, col] += matmul(df[pair], weight(up, col))

        columns(body)

    def work(w):
        slot = w // 2 % KEPT
        for k in range(3):
            pl.when(w == 2 + k)(lambda k=k: tap(k, k))

        @pl.when(w == 1)
        def _():
            for copy in handed[0] + handed[1]:
                copy.wait_send()
            pl.when(needs_raw(seq, seq - 2, tok_dev))(lambda: a_next().wait_recv())
            pl.when(gives_on_far)(lambda: a_on(3).start())
            pl.when(gives_on_near)(lambda: a_on(1).start())

        pl.when(w == 4)(lambda: pass_c(0))

        @pl.when(w == 5)
        def _():
            pl.when(even & needs_raw(seq, seq - 1, tok_dev))(lambda: a_on(1).wait_recv())
            pl.when(odd & needs_raw(seq, seq - 1, tok_dev))(lambda: a_beside().wait_recv())
            pl.when(needs_raw(seq, seq - 3, tok_dev))(lambda: a_on(3).wait_recv())
            pl.when(gives_next)(lambda: a_next().wait_send())
            pl.when(gives_beside)(lambda: a_beside().wait_send())
            pl.when(gives_on_far)(lambda: a_on(3).wait_send())
            pl.when(gives_on_near)(lambda: a_on(1).wait_send())
            flush(a_win, a3, dy_ref)

        @pl.when(w == 6)
        def _():
            project(q, a_win.at[pl.ds((raw_devs - 1) * tok_dev, tok_dev), :], slot)
            flush(q)

        for i, d in enumerate(steps_back[1:]):
            pl.when(w == 6 + 2 * i)(lambda d=d: pass_c(d))

        @pl.when(w == 8)
        def _():
            project_heads(kr, a_win, slot)
            flush(kr)

        @pl.when(w == 10)
        def _():
            project_heads(vr, a_win, slot)
            flush(vr)

        @pl.when(w == 12)
        def _():
            for d in steps_back:
                pl.when(takes_c_across(d))(lambda d=d: c_across_arrival(d).wait_recv())
            flush(c_win)
            project_heads(kc, c_win, 4 % KEPT)
            project_heads(vc, c_win, 5 % KEPT)
            flush(kc, vc)

        @pl.when((w >= 13) & (w < 17))
        def _():
            low = (w - 13) * (HEADS // 4)
            heads(low, low + HEADS // 4)

        @pl.when(w == 17)
        def _():
            flush(o)
            for d in steps_back:
                pl.when(gives_c(d))(lambda d=d: c_next(d).wait_send())
                pl.when(gives_c_across(d))(lambda d=d: c_across(d).wait_send())

            def body(col):
                sent = matmul(o[...].astype(BF16), weight(6 % KEPT, col))
                h[:, col] = tok_ref[:, col].astype(F32) + sent

            columns(body)
            for i in range(tok_dev // QB):
                rows = pl.ds(i * QB, QB)
                b[rows, :] = norm_rows(h[rows, :], params, 2).astype(BF16)
            y[...] = h[...]
            db[...] = jnp.zeros_like(db)
            flush(b, h)

        turn = w - 16
        lines_half = wbuf.shape[1] // 2
        first_turn = ((turn >= 4) & (turn % 4 == 0)) | (turn == 2)
        second_turn = ((turn >= 4) & (turn % 4 == 1)) | (turn == 3)
        pl.when(first_turn)(lambda: hidden(turn // 4, 0, lines_half))

        @pl.when(second_turn)
        def _():
            hidden(turn // 4, lines_half, 2 * lines_half)
            for copy in flush_hidden(turn // 4):
                copy.start()
            gather_hidden(turn // 4)

    def step(t, carry):
        pl.when(t + AHEAD < chunks)(lambda: start_lines(t + AHEAD))
        pl.when(t < chunks)(lambda: start_first(t))
        pl.when((t >= 1) & (t < chunks + 1))(lambda: start_second(t - 1))
        pl.when((t >= 2) & (t < chunks + 2))(lambda: start_cross(t - 2))

        pl.when((t >= LAG) & (t < chunks + LAG))(lambda: load(t - LAG).wait())
        pl.when(t >= LAG + 1)(lambda: work(t - LAG - 1))
        pl.when((t >= 3) & (t < chunks + 3))(lambda: finish(t - 3))
        return carry

    lax.fori_loop(0, chunks + LAG + 1, step, 0)
    flush(db)
    for i in range(tok_dev // QB):
        rows = pl.ds(i * QB, QB)
        mixed_ref[rows, :] = jnp.where(valid[i], y[rows, :], 0.0).astype(BF16)
    for pair in range(RATIO):
        for copy in flush_hidden(pair):
            copy.wait()
    for i, (src, dst) in enumerate(outs):
        pltpu.make_async_copy(src, dst, out_sem.at[i]).wait()


def forward(panel_slot, book_of_group, seg_valid, master, tokens, cotangent, norm_params, lines):
    panels, slot_count, rows = panel_slot.shape[0], master.shape[0], master.shape[1]
    wide = D // 4
    tok_dev = tokens.shape[0]
    raw = raw_devices(tok_dev) * tok_dev
    comp = comp_devices(tok_dev, 2 * lines) * (tok_dev // 3)
    dma = pltpu.SemaphoreType.DMA
    token, wide_token, hidden = ((tok_dev, D), BF16), ((tok_dev, D), F32), ((RATIO, tok_dev, D), BF16)
    raw_rows, comp_rows, thirds = ((raw, D), BF16), ((comp, D), BF16), ((3, tok_dev // 3, D), BF16)
    raw_heads, comp_heads = ((HEADS, raw, HEAD_DIM), BF16), ((HEADS, comp, HEAD_DIM), BF16)
    shapes = [raw_rows, comp_rows, token, raw_heads, raw_heads, comp_heads, comp_heads, wide_token]
    shapes = shapes + [hidden, hidden, token, wide_token, wide_token, thirds, token]
    scratch = [raw_rows, thirds, comp_rows, token, raw_heads, raw_heads, comp_heads, comp_heads]
    scratch = scratch + [wide_token, hidden, hidden, token, wide_token, wide_token, wide_token, token]
    scratch = [pltpu.VMEM(shape, kind) for shape, kind in scratch]
    blocks = tok_dev // QB
    any_spec, vmem = pl.BlockSpec(memory_space=pl.ANY), pl.BlockSpec(memory_space=pltpu.VMEM)
    smem = pl.BlockSpec(memory_space=pltpu.SMEM)
    return pl.pallas_call(
        functools.partial(forward_kernel, panels, lines),
        out_shape=[jax.ShapeDtypeStruct((panels, lines // 2, 2, 2, rows, D), BF16)]
        + [jax.ShapeDtypeStruct(shape, kind) for shape, kind in shapes]
        + [jax.ShapeDtypeStruct((HEADS, 8, tok_dev), F32), jax.ShapeDtypeStruct((tok_dev, D), BF16)],
        in_specs=[smem] * 3 + [vmem] * 4,
        out_specs=[any_spec] * (1 + len(shapes)) + [vmem] * 2,
        scratch_shapes=[pltpu.VMEM((KEPT, lines // 2, 2, 2, rows, D), BF16)]
        + scratch
        + [
            pltpu.VMEM((4 * slot_count, rows, wide), BF16),
            pltpu.VMEM((4 * slot_count, rows // 2, wide), BF16),
            pltpu.VMEM((4 * slot_count, rows // 2, wide), BF16),
            pltpu.VMEM((panels, rows, wide), BF16),
            pltpu.VMEM((HEADS, tok_dev, HEAD_DIM), F32),
            pltpu.VMEM((blocks, QB, RAW_KEYS), F32),
            pltpu.VMEM((blocks, QB, COMP_KEYS), F32),
            dma((2,)),
            dma((2 * panels, lines)), dma((2 * panels, lines)),
            dma((SEMS, 2)), dma((SEMS, 2)),
            dma((SEMS, 2, 2)), dma((SEMS, 2, 2)),
            dma((SEMS, 2)), dma((SEMS, 2)),
            dma((SEMS,)),
            dma((3,)), dma((3,)), dma((5,)), dma((5,)), dma((5,)), dma((5,)),
            dma((2, 3)), dma((2, 3)),
            dma((len(shapes),)),
            dma((2, RATIO)),
        ],
        compiler_params=pltpu.CompilerParams(
            collective_id=0, has_side_effects=True, vmem_limit_bytes=60 * MIB
        ),
        name="forward",
    )(panel_slot, book_of_group, seg_valid, master, tokens, cotangent, norm_params)


RETURN = [4 + RATIO + _i for _i in range(RATIO)] + [4 + _i for _i in range(RATIO)] + [3, 0, 1, 2] + TAPS
RING = 3
HELD = 5
BACK_LAG = 4


def norm_back(grad, values, params, first):
    mean = row_sum(values) * (1.0 / D)
    centered = values - mean
    scale = lax.rsqrt(row_sum(centered * centered) * (1.0 / D) + NORM_EPS)
    unit = centered * scale
    inner = grad * params[first : first + 1, :]
    back = inner - row_sum(inner) * (1.0 / D) - unit * (row_sum(inner * unit) * (1.0 / D))
    gain = jnp.sum(grad * unit, axis=0, keepdims=True)
    return back * scale, gain, jnp.sum(grad, axis=0, keepdims=True)


def attend_block_back(
    seq, tok_dev, i, cols, q, do, o, kr, vr, kc, vc, lse, lse_row, raw_bias, comp_bias,
    acc_kr, acc_vr, acc_kc, acc_vc,
):
    at = Attention(seq, i, tok_dev, kr.shape[0], kc.shape[0])
    query = q[at.rows, cols]
    grad = do[at.rows, cols]
    delta = row_sum(grad.astype(F32) * o[at.rows, cols])
    delta = jnp.broadcast_to(delta, (QB, QB)).T[0:1]
    stat = lse[lse_row, 0:1, at.rows]

    def part(k_ref, v_ref, acc_k, acc_v, keys, bias):
        k = k_ref[keys, :]
        s = times_transposed(k, query) * SCORE_SCALE + bias
        p = jnp.exp2(s - stat)
        dp = times_transposed(v_ref[keys, :], grad)
        ds = (p * (dp - delta)).astype(BF16)
        acc_v[keys, :] += matmul(p.astype(BF16), grad)
        acc_k[keys, :] += matmul(ds, query)
        return contract_rows(ds, k)

    dq = part(kr, vr, acc_kr, acc_vr, at.raw, raw_bias[i])
    dq = dq + part(kc, vc, acc_kc, acc_vc, at.comp, comp_bias[i])
    q[at.rows, cols] = (dq * HEAD_DIM ** (-0.5)).astype(BF16)


def backward_kernel(
    panels, lines,
    slot_ref,
    full_ref, a_hbm, c_hbm, a3_hbm, q_hbm, kr_hbm, vr_hbm, kc_hbm, vc_hbm, o_hbm, z_hbm, df_hbm,
    b_hbm, h_hbm, db_hbm, dy_hbm, tok_hbm, lse_ref, norm_ref,
    slot_out, in_grad_out, norm_out,
    held, cross_in, first_in, second_in, line_in, out, slots, slots_in,
    opnd, lhs_t, c_win, a3, h, db, o, pair, q, kr, vr, kc, vc, acc_kr, acc_vr, acc_kc, acc_vc,
    raw_bias, comp_bias, place, scale, dkr, dvr, dkc, dvc, wbuf, dc, dc_beside, dc_chain, da_in, n_src, n_in, n_line,
    cs, cr, s1, r1, s2, r2, zs, zr, free_cross, free_first, free_second,
    lsem, osem, hsem, wsem, dbs, dbr, dcs, dcr, das, dar, ns, nr, nzs, nzr, es, er,
):
    at = Place(lines)
    seq = at.seq
    seq_count = 2 * lines
    chunks = 2 * panels
    tok_dev = q.shape[0]
    comp_dev = tok_dev // 3
    raw_devs = dkr.shape[0] // tok_dev
    comp_devs = dkc.shape[0] // comp_dev
    reach = min(seq_count - 1, (2 * S + 3 * CM + tok_dev - 1) // tok_dev)
    wide = out.shape[-1]
    half_rows = out.shape[1] // 2
    pairs = lines // 2
    params = norm_ref[...]
    raw, comp = dkr.shape[0], dkc.shape[0]

    def token_rows(i):
        return pl.ds(pl.multiple_of(i * tok_dev, tok_dev), tok_dev)

    dhb, do = pair.at[token_rows(0), :], pair.at[token_rows(1), :]

    taps = chunks - 6

    def panel_of(u):
        return jnp.where(u < taps, u // 2, panels - 3 + (u - taps) % 3)

    def half_of(u):
        return jnp.where(u < taps, u % 2, (u - taps) // 3)

    def mine(u):
        return held.at[u % HELD, :, :, at.core]

    def cross(u):
        src, i = held.at[u % HELD, :, :, 1 - at.core], u % RING
        return remote(src, cross_in.at[i], cs.at[i], cr.at[i], at.core_dev)

    def first(u, half):
        i = u % RING
        if half == 0:
            src, device = mine(u).at[:, 0, 1 - at.row], at.y_dev
        else:
            src, device = mine(u).at[:, 1, :, 1 - at.col], at.x_dev
        return remote(src, first_in.at[i, half], s1.at[i, half], r1.at[i, half], device)

    def second(u, half):
        i = u % RING
        if half == 0:
            src, device = mine(u).at[:, 0, at.row, 1 - at.col], at.x_dev
        else:
            src, device = mine(u).at[:, 1, 1 - at.row, at.col], at.y_dev
        return remote(src, second_in.at[i, half], s2.at[i, half], r2.at[i, half], device)

    def line_copy(u, k):
        line = at.other_line(k)
        src = mine(u).at[line // 2, line % 2, at.row, at.col]
        i = lines - 1 - k
        return remote(src, line_in.at[u, i], zs.at[u, k], zr.at[u, i], at.line_dev(k))

    def line_arrival(u, k):
        line = at.other_line(k)
        src = mine(u).at[line // 2, line % 2, at.row, at.col]
        return remote(src, line_in.at[u, k - 1], zs.at[u, k], zr.at[u, k - 1], at.line_dev(k))

    def give(semaphore, device):
        pl.semaphore_signal(semaphore, inc=1, device_id=device, device_id_type=MESH)

    def add(dst, src):
        dst[...] = (dst[...].astype(F32) + src[...].astype(F32)).astype(BF16)

    def start_first(u):
        cross(u).wait_recv()
        for half in (0, 1):
            for i in range(pairs):
                for g in range(4):
                    add(
                        mine(u).at[i, half, g // 2, g % 2],
                        cross_in.at[u % RING, i, half, g // 2, g % 2],
                    )
            pl.when(u >= RING)(lambda half=half: pl.semaphore_wait(free_first.at[half], 1))
            first(u, half).start()
        cross(u).wait_send()
        pl.when(u + RING < chunks)(lambda: give(free_cross, at.core_dev))

    def start_second(u):
        for half in (0, 1):
            first(u, half).wait_recv()
            for i in range(pairs):
                for j in (0, 1):
                    row, col = (at.row, j) if half == 0 else (j, at.col)
                    add(mine(u).at[i, half, row, col], first_in.at[u % RING, half, i, j])
            pl.when(u >= RING)(lambda half=half: pl.semaphore_wait(free_second.at[half], 1))
            second(u, half).start()
            first(u, half).wait_send()
            device = at.y_dev if half == 0 else at.x_dev
            pl.when(u + RING < chunks)(
                lambda half=half, device=device: give(free_first.at[half], device)
            )

    def start_lines(u):
        for half in (0, 1):
            second(u, half).wait_recv()
            for i in range(pairs):
                add(mine(u).at[i, half, at.row, at.col], second_in.at[u % RING, half, i])
            second(u, half).wait_send()
            device = at.x_dev if half == 0 else at.y_dev
            pl.when(u + RING < chunks)(
                lambda half=half, device=device: give(free_second.at[half], device)
            )
        for k in range(1, lines):
            line_copy(u, k).start()

    def finish(u):
        total = mine(u)[at.line // 2, at.line % 2, at.row, at.col].astype(F32)
        for k in range(1, lines):
            line_arrival(u, k).wait_recv()
            total = total + line_in[u, k - 1].astype(F32)
        rows = pl.ds(pl.multiple_of(half_of(u) * half_rows, half_rows), half_rows)
        out[panel_of(u), rows, :] = total.astype(BF16)
        for k in range(1, lines):
            line_copy(u, k).wait_send()

    def turn(left, first_row):
        turned = left[...].astype(BF16).T
        count = left.shape[0]
        turned = turned.reshape(2 * pairs, 2, 2, half_rows, count)
        lhs_t[:, :, :, :, pl.ds(first_row, count)] = turned

    def produce(u, *terms):
        def columns(j, carry):
            col = pl.ds(pl.multiple_of(j * wide, wide), wide)
            total = None
            for first_row, right in terms:
                count = right.shape[0]
                left = lhs_t[:, :, half_of(u), :, pl.ds(first_row, count)].reshape(D // 2, count)
                term = matmul(left, right[:, col])
                total = term if total is None else total + term
            total = total.reshape(pairs, 2, 2, half_rows, wide)
            held[u % HELD, :, :, :, j // 2, j % 2] = total.astype(BF16)
            return carry

        lax.fori_loop(0, 4, columns, 0)
        pl.when(u >= RING)(lambda: pl.semaphore_wait(free_cross, 1))
        cross(u).start()

    def left_load(p, src):
        return pltpu.make_async_copy(src.at[p % RATIO], opnd.at[token_rows(2 + p % 2), :], lsem.at[p % 2])

    def left_start(p):
        pl.when(p < RATIO)(lambda: left_load(p, z_hbm).start())
        pl.when(p >= RATIO)(lambda: left_load(p, df_hbm).start())

    early = [
        (dy_hbm, opnd.at[token_rows(0), :]), (b_hbm, opnd.at[token_rows(1), :]), (h_hbm, h),
        (db_hbm, db), (o_hbm, o), (q_hbm, q), (c_hbm, c_win), (a3_hbm, a3),
    ]

    def early_load(i):
        return pltpu.make_async_copy(early[i][0], early[i][1], osem.at[i])

    def late_load(i):
        src, dst = ((a_hbm, opnd), (tok_hbm, dhb), (h, in_grad_out))[i]
        return pltpu.make_async_copy(src, dst, osem.at[len(early) + i])

    def head_loads(i):
        refs = [(kr_hbm, kr), (vr_hbm, vr), (kc_hbm, kc), (vc_hbm, vc)]
        return [
            pltpu.make_async_copy(src.at[i], dst, hsem.at[j])
            for j, (src, dst) in enumerate(refs)
        ]

    def weight_load(panel, slot):
        return pltpu.make_async_copy(full_ref.at[panel], wbuf.at[slot], wsem.at[slot])

    def weight(slot):
        return wbuf[slot].reshape(D, D)

    other = seq + 1 - 2 * at.core

    def comp_rows(owner):
        place = jnp.clip(owner - comp_window_first(seq, tok_dev), 0, comp_devs - 1)
        return pair.at[pl.ds(pl.multiple_of(place * comp_dev, comp_dev), comp_dev), :]

    def dc_across(d):
        i = (d + 1) // 2 - at.core
        return remote(comp_rows(seq - d), dc_beside.at[i], dbs.at[d // 2], dbr.at[i], at.core_dev)

    def dc_join(d):
        i = d // 2

        @pl.when(needs_comp(other, seq - d, tok_dev))
        def _():
            remote(comp_rows(seq - d), dc_beside.at[i], dbs.at[0], dbr.at[i], at.core_dev).wait_recv()
            add(comp_rows(seq - d), dc_beside.at[i])

    def gives_back(d):
        return chain_needs_comp(seq, seq - d, tok_dev, seq_count, reach - 1)

    def takes_back(d):
        return chain_needs_comp(seq + 2, seq - d, tok_dev, seq_count, reach - 1)

    def dc_back(d):
        i = d // 2 - 1
        return remote(comp_rows(seq - d), dc_chain.at[i], dcs.at[i], dcr.at[i], at.seq_dev(-2))

    def dc_arrival(d):
        i = d // 2
        return remote(comp_rows(seq), dc_chain.at[i], dcs.at[0], dcr.at[i], at.seq_dev(-2))

    def pass_back(d):
        @pl.when((d + 2 < reach) & takes_back(d))
        def _():
            dc_arrival(d).wait_recv()
            add(comp_rows(seq - d), dc_chain.at[d // 2])

        pl.when(gives_back(d))(lambda: dc_back(d).start())

    chain = [d for d in range(2, reach + 1, 2)]
    odds = [d for d in range(1, reach + 1, 2)]

    odd = at.core == 1
    even = at.core == 0

    def raw_rows(d):
        return dkr.at[token_rows(raw_devs - 1 - d), :]

    def da_copy(d, i, place, device):
        return remote(raw_rows(d), da_in.at[place], das.at[i], dar.at[place], device)

    def da_join(d):
        return da_copy(d, 0, 0, at.core_dev)

    def da_beside():
        return da_copy(1, 1, 1, at.core_dev)

    def da_back():
        return da_copy(2, 2, 2, at.seq_dev(-2))

    joins_near = even & needs_raw(seq, seq - 1, tok_dev)
    joins_far = odd & needs_raw(seq, seq - 3, tok_dev)
    joined = needs_raw(other, seq - 2, tok_dev)
    gives_beside = odd & needs_raw(seq, seq - 1, tok_dev)
    takes_beside = even & needs_raw(seq + 1, seq, tok_dev)
    gives_raw = needs_raw(seq, seq - 2, tok_dev)
    takes_raw = (seq + 2 < seq_count) & needs_raw(seq + 2, seq, tok_dev)

    def share(i):
        total = times_transposed(dkr[token_rows(i), :], weight(1))
        return total + times_transposed(dvr[token_rows(i), :], weight(2))

    def norm_copy(i):
        device = (at.core_dev, at.x_dev, at.y_dev)[i]
        return remote(n_src.at[i], n_in.at[i], ns.at[i], nr.at[i], device)

    def norm_next(i):
        norm_copy(i).wait_recv()
        n_src[i + 1] = n_src[i] + n_in[i]

    def norm_line(k):
        return remote(n_src.at[3], n_line.at[at.line], nzs.at[k], nzr.at[at.line], at.line_dev(k))

    def norm_line_arrival(k):
        line = at.other_line(k)
        return remote(n_src.at[3], n_line.at[line], nzs.at[k], nzr.at[line], at.line_dev(k))

    def second_norm_back():
        gains, shifts = [], []
        for i in range(tok_dev // QB):
            rows = pl.ds(i * QB, QB)
            back, gain, shift = norm_back(db[rows, :], h[rows, :], params, 2)
            db[rows, :] = opnd[rows, :].astype(F32) + back
            dhb[rows, :] = db[rows, :].astype(BF16)
            gains.append(gain)
            shifts.append(shift)
        n_src[0, 2:3, :] = sum(gains)
        n_src[0, 3:4, :] = sum(shifts)
        do[...] = times_transposed(dhb[...], weight(0)).astype(BF16)

    def first_norm_back():
        gains, shifts = [], []
        for i in range(tok_dev // QB):
            rows = pl.ds(i * QB, QB)
            back, gain, shift = norm_back(h[rows, :], dhb[rows, :].astype(F32), params, 0)
            h[rows, :] = db[rows, :] + back
            gains.append(gain)
            shifts.append(shift)
        n_src[0, 0:1, :] = sum(gains)
        n_src[0, 1:2, :] = sum(shifts)

    count = slot_out.shape[0]
    halves = [pl.ds(i * half_rows, half_rows) for i in range(2)]
    handed = [
        at.exchange(slots.at[:, halves[i]], slots_in.at[:, halves[i]], es.at[i], er.at[i])
        for i in range(2)
    ]

    def hand(i):
        for j in range(4 * count):
            total = out[place[j], halves[i], :].astype(F32) * scale[j]
            slots[j, halves[i], :] = total.astype(BF16)
        for copy in handed[i]:
            copy.start()
        own = pl.ds(at.grp * count, count)
        slots_in[own, halves[i], :] = slots[own, halves[i], :]

    def take(i):
        for copy in handed[i]:
            copy.wait_recv()
        for g in range(4):
            for j in range(count):
                slot_out[j, halves[i], pl.ds(g * wide, wide)] = slots_in[g * count + j, halves[i], :]

    def work(t):
        pl.when(t == taps + 3 - 1 + BACK_LAG)(lambda: hand(0))

        @pl.when(t == 0)
        def _():
            for i in range(tok_dev // QB):
                block_at = Attention(seq, i, tok_dev, raw, comp)
                raw_bias[i] = block_at.raw_bias((RAW_KEYS, QB), 0)
                comp_bias[i] = block_at.comp_bias((COMP_KEYS, QB), 0)
            for j in range(place.shape[0]):
                where = jnp.int32(0)
                for r in range(panels):
                    where = jnp.where(slot_ref[RETURN[r]] == j, r, where)
                place[j] = where
                scale[j] = slot_deviation(slot_ref, j)

        @pl.when(t == 1)
        def _():
            for i in range(2, 6):
                early_load(i).wait()
            weight_load(6, 0).wait()
            second_norm_back()
            weight_load(3, 0).start()

        @pl.when((t >= 2) & (t < 2 + 2 * HEADS))
        def _():
            head = t // 2 - 1
            cols = pl.ds(pl.multiple_of(head * HEAD_DIM, HEAD_DIM), HEAD_DIM)

            def blocks(low, high):
                for i in range(low, high):
                    attend_block_back(
                        seq, tok_dev, i, cols, q, do, o, kr, vr, kc, vc, lse_ref, head,
                        raw_bias, comp_bias, acc_kr, acc_vr, acc_kc, acc_vc,
                    )

            @pl.when(t % 2 == 0)
            def _():
                for copy in head_loads(head):
                    copy.wait()
                for acc in (acc_kr, acc_vr, acc_kc, acc_vc):
                    acc[...] = jnp.zeros_like(acc)
                blocks(0, tok_dev // QB // 2)

            @pl.when(t % 2 == 1)
            def _():
                blocks(tok_dev // QB // 2, tok_dev // QB)
                score = HEAD_DIM ** (-0.5)
                dkr[:, cols] = (acc_kr[...] * score).astype(BF16)
                dkc[:, cols] = (acc_kc[...] * score).astype(BF16)
                dvr[:, cols] = acc_vr[...].astype(BF16)
                dvc[:, cols] = acc_vc[...].astype(BF16)

                @pl.when(head + 1 < HEADS)
                def _():
                    for copy in head_loads(head + 1):
                        copy.start()

        @pl.when(t == 18)
        def _():
            weight_load(4, 1).wait()
            weight_load(5, 2).wait()
            half = comp // 2
            for i in range(2):
                rows = pl.ds(i * half, half)
                total = times_transposed(dkc[rows, :], weight(1))
                total = total + times_transposed(dvc[rows, :], weight(2))
                pair[rows, :] = total.astype(BF16)
            for d in odds:
                pl.when(needs_comp(seq, seq - d, tok_dev))(lambda d=d: dc_across(d).start())

        @pl.when(t == 19)
        def _():
            for d in chain:
                dc_join(d)

        for i, d in enumerate(reversed(chain)):
            pl.when(t == 19 + i)(lambda d=d: pass_back(d))

        @pl.when(t == 20)
        def _():
            weight_load(3, 0).wait()
            h[...] = times_transposed(q[...], weight(0))
            weight_load(0, 0).start()

        @pl.when(t == 24)
        def _():
            raw_rows(1)[...] = share(raw_devs - 2).astype(BF16)
            pl.when(joins_near)(lambda: da_join(1).start())
            pl.when(gives_beside)(lambda: da_beside().start())

            @pl.when(joins_far)
            def _():
                raw_rows(3)[...] = share(raw_devs - 4).astype(BF16)
                da_join(3).start()

        @pl.when(t == 25)
        def _():
            raw_rows(2)[...] = share(raw_devs - 3).astype(BF16)
            h[...] += share(raw_devs - 1)
            weight_load(1, 1).start()
            weight_load(2, 2).start()

        @pl.when(t == 23)
        def _():
            taken = takes_back(0)

            @pl.when(taken)
            def _():
                dc_arrival(0).wait_recv()
                dc[...] = dc_chain[0]

            @pl.when(jnp.logical_not(taken))
            def _():
                dc[...] = jnp.zeros_like(dc)

        @pl.when(t == 26)
        def _():
            @pl.when(joined)
            def _():
                da_join(2).wait_recv()
                add(raw_rows(2), da_in.at[0])

            pl.when(gives_raw)(lambda: da_back().start())

        @pl.when(t == 28)
        def _():
            for panel in range(3):
                weight_load(panel, panel).wait()
            heads_of = acc_kr.shape[0] // tok_dev
            for k in range(3):
                total = times_transposed(dc[...], weight(k))
                for c in range(HEADS):
                    acc = (acc_kr, acc_vr)[c // heads_of]
                    place = pl.ds(c % heads_of * tok_dev + k, comp_dev, stride=3)
                    acc[place, :] = total[:, c * HEAD_DIM : (c + 1) * HEAD_DIM]
            for c in range(HEADS):
                acc = (acc_kr, acc_vr)[c // heads_of]
                cols = pl.ds(c * HEAD_DIM, HEAD_DIM)
                h[:, cols] += acc[pl.ds(c % heads_of * tok_dev, tok_dev), :]
            for d in odds:
                pl.when(needs_comp(seq, seq - d, tok_dev))(lambda d=d: dc_across(d).wait_send())
            for d in chain:
                pl.when(gives_back(d))(lambda d=d: dc_back(d).wait_send())
            late_load(1).start()

        @pl.when(t == 30)
        def _():
            @pl.when(takes_raw)
            def _():
                da_back().wait_recv()
                h[...] += da_in[2].astype(F32)

            @pl.when(takes_beside)
            def _():
                da_beside().wait_recv()
                h[...] += da_in[1].astype(F32)

            pl.when(joins_near)(lambda: da_join(1).wait_send())
            pl.when(joins_far)(lambda: da_join(3).wait_send())
            pl.when(gives_beside)(lambda: da_beside().wait_send())
            pl.when(gives_raw)(lambda: da_back().wait_send())
            late_load(1).wait()
            first_norm_back()
            norm_copy(0).start()
            late_load(2).start()

        for i in range(2):

            @pl.when(t == 31 + i)
            def _(i=i):
                norm_next(i)
                norm_copy(i + 1).start()

        @pl.when(t == 33)
        def _():
            norm_next(2)
            n_line[at.line] = n_src[3]
            for k in range(1, lines):
                norm_line(k).start()

    def make(t):
        @pl.when(t < 4 * RATIO)
        def _():
            p = t // 2

            @pl.when(t % 2 == 0)
            def _():
                pl.when(p + 1 < 2 * RATIO)(lambda: left_start(p + 1))
                left_load(p, z_hbm).wait()
                pl.when(p == 0)(lambda: early_load(0).wait())
                pl.when(p == RATIO)(lambda: early_load(1).wait())
                turn(opnd.at[token_rows(2 + p % 2), :], 0)

            produce(t, (0, opnd.at[token_rows(p // RATIO), :]))
            pl.when(t == 4 * RATIO - 1)(lambda: late_load(0).start())

        base = 4 * RATIO
        pl.when(t == base)(lambda: turn(o, 0))
        pl.when(t // 2 == base // 2)(lambda: produce(t, (0, dhb)))

        @pl.when(t == base + 2)
        def _():
            late_load(0).wait()
            early_load(6).wait()
            early_load(7).wait()
            turn(opnd.at[token_rows(raw_devs - 1), :], raw - tok_dev)

        pl.when(t // 2 == base // 2 + 1)(lambda: produce(t, (raw - tok_dev, q)))

        @pl.when(t == base + 3)
        def _():
            for i in range(raw_devs - 1):
                turn(opnd.at[token_rows(i), :], i * tok_dev)
            for i in range(comp // tok_dev):
                turn(c_win.at[token_rows(i), :], raw + i * tok_dev)

        pl.when(t // 2 == base // 2 + 2)(lambda: produce(t, (0, dkr), (raw, dkc)))
        pl.when(t // 2 == base // 2 + 3)(lambda: produce(t, (0, dvr), (raw, dvc)))

        @pl.when(t == taps)
        def _():
            for k in range(3):
                turn(a3.at[k], k * comp_dev)

        tap = pl.multiple_of((t - taps) % 3 * comp_dev, comp_dev)
        pl.when(t >= taps)(lambda: produce(t, (tap, dc)))

    at.announce()
    for i in range(len(early)):
        early_load(i).start()
    left_load(0, z_hbm).start()
    for panel, slot in ((6, 0), (4, 1), (5, 2)):
        weight_load(panel, slot).start()
    for copy in head_loads(0):
        copy.start()
    at.enter()

    def step(t, carry):
        pl.when((t >= 1) & (t < chunks + 1))(lambda: start_first(t - 1))
        pl.when((t >= 2) & (t < chunks + 2))(lambda: start_second(t - 2))
        pl.when((t >= 3) & (t < chunks + 3))(lambda: start_lines(t - 3))
        pl.when(t >= BACK_LAG)(lambda: finish(t - BACK_LAG))
        pl.when(t < chunks)(lambda: make(t))
        work(t)
        return carry

    lax.fori_loop(0, chunks + BACK_LAG, step, 0)
    hand(1)
    for i in range(3):
        norm_copy(i).wait_send()
    for k in range(1, lines):
        norm_line_arrival(k).wait_recv()
        norm_line(k).wait_send()
    total = n_line[0]
    for i in range(1, lines):
        total = total + n_line[i]
    norm_out[...] = total
    late_load(2).wait()
    take(0)
    take(1)
    for copy in handed[0] + handed[1]:
        copy.wait_send()


def backward(panel_slot, all_slots, weights, arrays, lse, norm_params, lines):
    panels, rows = weights.shape[0], weights.shape[4]
    wide, pairs, half_rows = D // 4, lines // 2, weights.shape[4] // 2
    a_win, c_win = arrays[0], arrays[1]
    tok_dev = arrays[3].shape[0]
    raw, comp, comp_dev = a_win.shape[0], c_win.shape[0], tok_dev // 3
    raw_devs, blocks = raw // tok_dev, tok_dev // QB
    reach = min(2 * lines - 1, (2 * S + 3 * CM + tok_dev - 1) // tok_dev)
    dma = pltpu.SemaphoreType.DMA
    regular = pltpu.SemaphoreType.REGULAR
    any_spec, vmem = pl.BlockSpec(memory_space=pl.ANY), pl.BlockSpec(memory_space=pltpu.VMEM)
    smem = pl.BlockSpec(memory_space=pltpu.SMEM)

    def buffer(kind, *shape):
        return pltpu.VMEM(shape, kind)

    return pl.pallas_call(
        functools.partial(backward_kernel, panels, lines),
        out_shape=[
            jax.ShapeDtypeStruct((all_slots // 4, rows, D), BF16),
            jax.ShapeDtypeStruct((tok_dev, D), F32),
            jax.ShapeDtypeStruct((4, D), F32),
        ],
        in_specs=[smem] + [any_spec] * (1 + len(arrays)) + [vmem] * 2,
        out_specs=[vmem, any_spec, vmem],
        scratch_shapes=[
            buffer(BF16, HELD, pairs, 2, 2, 2, 2, half_rows, wide),
            buffer(BF16, RING, pairs, 2, 2, 2, half_rows, wide),
            buffer(BF16, RING, 2, pairs, 2, half_rows, wide),
            buffer(BF16, RING, 2, pairs, half_rows, wide),
            buffer(BF16, 2 * panels, lines - 1, half_rows, wide),
            buffer(BF16, panels, rows, wide),
            buffer(BF16, all_slots, rows, wide),
            buffer(BF16, all_slots, rows, wide),
            buffer(BF16, raw, D),
            buffer(BF16, 2 * pairs, 2, 2, half_rows, raw + comp),
            buffer(BF16, comp, D),
            buffer(BF16, 3, comp_dev, D),
            buffer(F32, tok_dev, D),
            buffer(F32, tok_dev, D),
            buffer(F32, tok_dev, D),
            buffer(BF16, max(comp, 2 * tok_dev), D),
            buffer(BF16, tok_dev, D),
            buffer(BF16, raw, HEAD_DIM),
            buffer(BF16, raw, HEAD_DIM),
            buffer(BF16, comp, HEAD_DIM),
            buffer(BF16, comp, HEAD_DIM),
            buffer(F32, raw, HEAD_DIM),
            buffer(F32, raw, HEAD_DIM),
            buffer(F32, comp, HEAD_DIM),
            buffer(F32, comp, HEAD_DIM),
            buffer(F32, blocks, RAW_KEYS, QB),
            buffer(F32, blocks, COMP_KEYS, QB),
            pltpu.SMEM((all_slots,), jnp.int32),
            pltpu.SMEM((all_slots,), F32),
            buffer(BF16, raw, D),
            buffer(BF16, raw, D),
            buffer(BF16, comp, D),
            buffer(BF16, comp, D),
            buffer(BF16, 3, pairs, 2, 2, rows, D),
            buffer(BF16, comp_dev, D),
            buffer(BF16, reach // 2 + 2, comp_dev, D),
            buffer(BF16, reach // 2 + 1, comp_dev, D),
            buffer(BF16, 3, tok_dev, D),
            buffer(F32, 4, 4, D),
            buffer(F32, 3, 4, D),
            buffer(F32, lines, 4, D),
            dma((RING,)), dma((RING,)),
            dma((RING, 2)), dma((RING, 2)),
            dma((RING, 2)), dma((RING, 2)),
            dma((2 * panels, lines)), dma((2 * panels, lines)),
            regular, regular((2,)), regular((2,)),
            dma((2,)), dma((11,)), dma((4,)), dma((3,)),
            dma((reach // 2 + 2,)), dma((reach // 2 + 2,)),
            dma((reach // 2 + 1,)), dma((reach // 2 + 1,)),
            dma((3,)), dma((3,)),
            dma((3,)), dma((3,)),
            dma((lines,)), dma((lines,)),
            dma((2, 3)), dma((2, 3)),
        ],
        compiler_params=pltpu.CompilerParams(
            collective_id=1, has_side_effects=True, vmem_limit_bytes=62 * MIB
        ),
        name="backward",
    )(panel_slot, weights, *arrays, lse, norm_params)


def local(
    tokens, cotangent, master, first_moment, second_moment, norm_params, norm_first, norm_second,
    seg_valid, book_of_group, panel_slot,
):
    lines = lax.axis_size("seq") // 2
    all_slots = master.shape[0] * lax.axis_size("grp")
    results = forward(
        panel_slot, book_of_group, seg_valid, master, tokens, cotangent, norm_params, lines
    )
    weights, saved, log_total, mixed = results[0], results[1:-2], results[-2], results[-1]
    a_win, c_win, q, kr, vr, kc, vc, o, z, df, b, h, db, a3, grad_out = saved
    arrays = (a_win, c_win, a3, q, kr, vr, kc, vc, o, z, df, b, h, db, grad_out, tokens)
    slot_sums, input_grad, norm_grad = backward(
        panel_slot, all_slots, weights, arrays, log_total, norm_params, lines
    )
    slot_grad = slot_sums.astype(F32)
    slot_first, slot_second, slot_weight = adam_update(
        slot_grad, first_moment, second_moment, master, SLOT_RATE
    )
    norm_first_new, norm_second_all, norm_weight = adam_update(
        norm_grad, norm_first, norm_second, norm_params, NORM_RATE
    )
    return (
        mixed, input_grad, slot_grad, slot_first, slot_second, slot_weight, norm_grad,
        norm_first_new, norm_second_all[:2], norm_second_all[2:], norm_weight,
    )


def solution(mesh):
    rows, slots, whole = P(("grp", "seq"), None), P("grp", "seq", None), P()
    return jax.shard_map(
        local,
        mesh=mesh,
        in_specs=(rows, rows, slots, slots, slots) + (whole,) * 6,
        out_specs=(rows, rows, slots, slots, slots, slots) + (whole,) * 5,
        check_vma=False,
    )
```

```python
import functools

import jax
import jax.numpy as jnp
from jax import lax
from jax.experimental import pallas as pl
from jax.experimental.pallas import tpu as pltpu
from jax.sharding import PartitionSpec as P

D = 1024
HEADS = 8
HEAD_DIM = 128
FF = 4096
S = 512
CM = 512
STEP = 10
PANELS = 15
RATIO = FF // D
QB = 128
RAW_KEYS = 2 * S
COMP_KEYS = CM + QB
MIB = 1 << 20

NEG_SCORE = -1e30
NORM_EPS = 1e-05
BETA_ONE = 0.9
BETA_TWO = 0.999
WEIGHT_DECAY = 0.1
ADAM_EPS = 1e-08
NORM_RATE = 1.0
SLOT_RATE = 2.0
BF16 = jnp.bfloat16
F32 = jnp.float32
MESH = pl.DeviceIdType.MESH


def layer_norm(values, gain, shift):
    row_mean = jnp.mean(values, axis=-1, keepdims=True)
    centered = values - row_mean
    variance = jnp.mean(centered * centered, axis=-1, keepdims=True)
    return centered * lax.rsqrt(variance + NORM_EPS) * gain + shift


DEVIATIONS = [D ** (-0.5)] * 3 + [(D // (2 * S)) ** (-0.5)] + [D ** (-0.5)] * RATIO
DEVIATIONS = DEVIATIONS + [FF ** (-0.5)] * RATIO + [(3 * D) ** (-0.5)] * 3


def slot_deviation(panel_slot, slot):
    scale = jnp.float32(0.0)
    for panel in range(PANELS):
        scale = jnp.where(panel_slot[panel] == slot, jnp.float32(DEVIATIONS[panel]), scale)
    return scale


def adam_update(gradient, first_old, second_old, weight_old, step_rate):
    first_new = BETA_ONE * first_old + (1.0 - BETA_ONE) * gradient
    second_new = BETA_TWO * second_old + (1.0 - BETA_TWO) * gradient * gradient
    fix_one = 1.0 - BETA_ONE**STEP
    fix_two = 1.0 - BETA_TWO**STEP
    movement = first_new / fix_one / (jnp.sqrt(second_new / fix_two) + ADAM_EPS)
    return (first_new, second_new, weight_old - step_rate * (movement + WEIGHT_DECAY * weight_old))


def matmul(left, right):
    return jnp.dot(left, right, preferred_element_type=F32)


def times_transposed(left, right):
    return lax.dot_general(left, right, (((1,), (1,)), ((), ())), preferred_element_type=F32)


def contract_rows(left, right):
    return lax.dot_general(left, right, (((0,), (0,)), ((), ())), preferred_element_type=F32)


class Place:
    def __init__(self, lines):
        self.lines = lines
        self.grp = lax.axis_index("grp")
        self.seq = lax.axis_index("seq")
        self.line = self.seq // 2
        self.core = self.seq % 2
        self.row = self.grp // 2
        self.col = self.grp % 2
        self.grp_x = self.row * 2 + 1 - self.col
        self.grp_y = (1 - self.row) * 2 + self.col
        self.x_dev = {"grp": self.grp_x, "seq": self.seq}
        self.y_dev = {"grp": self.grp_y, "seq": self.seq}
        self.far_dev = {"grp": 3 - self.grp, "seq": self.seq}
        self.core_dev = {"grp": self.grp, "seq": self.line * 2 + 1 - self.core}

    def other_line(self, k):
        return lax.rem(self.line + k, self.lines)

    def line_dev(self, k):
        return {"grp": self.grp, "seq": self.other_line(k) * 2 + self.core}

    def seq_dev(self, d):
        count = 2 * self.lines
        return {"grp": self.grp, "seq": lax.rem(self.seq + d + count, count)}

    def announce(self):
        barrier = pltpu.get_barrier_semaphore()
        partners = [self.seq_dev(d) for d in range(1, 2 * self.lines)]
        for device in partners + [self.x_dev, self.y_dev, self.far_dev]:
            pl.semaphore_signal(barrier, inc=1, device_id=device, device_id_type=MESH)

    def enter(self):
        pl.semaphore_wait(pltpu.get_barrier_semaphore(), 2 * self.lines + 2)

    def exchange(self, parts, arrived, send, recv):
        count = parts.shape[0] // 4
        copies = []
        for i, device in enumerate((self.x_dev, self.y_dev, self.far_dev)):
            src = parts.at[pl.ds(device["grp"] * count, count)]
            dst = arrived.at[pl.ds(self.grp * count, count)]
            copies.append(remote(src, dst, send.at[i], recv.at[i], device))
        return copies


def remote(src, dst, send, recv, device):
    return pltpu.make_async_remote_copy(
        src_ref=src,
        dst_ref=dst,
        send_sem=send,
        recv_sem=recv,
        device_id=device,
        device_id_type=MESH,
    )


def memory_start(position):
    return (position // S - 1) * S


def comp_window_first(seq, tok_dev):
    return jnp.maximum(memory_start(seq * tok_dev) - 3 * CM, 0) // tok_dev


def raw_devices(tok_dev):
    return (RAW_KEYS - QB + tok_dev - 1) // tok_dev + 1


def comp_devices(tok_dev, seq_count):
    return min((3 * CM + S) // tok_dev + 1, seq_count)


def needs_raw(reader, owner, tok_dev):
    return (owner >= 0) & ((owner + 1) * tok_dev > memory_start(reader * tok_dev))


def needs_comp(reader, owner, tok_dev):
    last = jnp.maximum(memory_start(reader * tok_dev + tok_dev - 1), 0) // 3
    inside = (owner >= 0) & (owner >= comp_window_first(reader, tok_dev))
    return inside & (owner * (tok_dev // 3) < last)


def chip_needs_comp(reader, owner, tok_dev):
    even = reader // 2 * 2
    return needs_comp(even, owner, tok_dev) | needs_comp(even + 1, owner, tok_dev)


def chain_needs_comp(reader, owner, tok_dev, seq_count, reach):
    needed = chip_needs_comp(reader, owner, tok_dev)
    for ahead in range(2, reach + 1, 2):
        later = reader + ahead
        needed = needed | ((later < seq_count) & chip_needs_comp(later, owner, tok_dev))
    return needed & (owner >= 0) & (reader < seq_count)


def block_window(seq, i, tok_dev, raw_rows, comp_rows):
    position = seq * tok_dev + i * QB
    memory = memory_start(position)
    raw_base = (seq + 1) * tok_dev - raw_rows
    raw_at = jnp.minimum(memory - raw_base, raw_rows - RAW_KEYS)
    comp_end = jnp.maximum(memory, 0) // 3
    comp_low = jnp.maximum(comp_end - CM, 0)
    comp_base = comp_window_first(seq, tok_dev) * (tok_dev // 3)
    comp_at = jnp.minimum((comp_low - comp_base) // QB * QB, comp_rows - COMP_KEYS)
    return (
        position,
        pl.multiple_of(raw_at, QB),
        pl.multiple_of(comp_at, QB),
        raw_base + raw_at,
        comp_base + comp_at,
        memory,
        comp_low,
        comp_end,
    )


def row_sum(values):
    return jnp.sum(values, axis=1, keepdims=True)


def norm_rows(values, params, first):
    mean = row_sum(values) * (1.0 / D)
    centered = values - mean
    variance = row_sum(centered * centered) * (1.0 / D)
    gain, shift = params[first : first + 1, :], params[first + 1 : first + 2, :]
    return centered * lax.rsqrt(variance + NORM_EPS) * gain + shift


GELU_IN = (2.0 / 3.141592653589793) ** 0.5
GELU_CUBE = 0.044715


def gelu_pair(f):
    square = f * f
    t = jnp.tanh(GELU_IN * f * (1.0 + GELU_CUBE * square))
    half = 0.5 * (1.0 + t)
    slope = half + 0.5 * f * (1.0 - t * t) * (GELU_IN * (1.0 + 3.0 * GELU_CUBE * square))
    return f * half, slope


class Attention:
    def __init__(self, seq, i, tok_dev, raw_rows, comp_rows):
        place = block_window(seq, i, tok_dev, raw_rows, comp_rows)
        self.pos, raw_at, comp_at, self.raw_pos, self.comp_pos = place[:5]
        self.memory, self.comp_low, self.comp_end = place[5:]
        self.rows = pl.ds(pl.multiple_of(i * QB, QB), QB)
        self.raw = pl.ds(raw_at, RAW_KEYS)
        self.comp = pl.ds(comp_at, COMP_KEYS)

    def raw_bias(self, shape, key_dim):
        key_pos = self.raw_pos + lax.broadcasted_iota(jnp.int32, shape, key_dim)
        query_pos = self.pos + lax.broadcasted_iota(jnp.int32, shape, 1 - key_dim)
        seen = (key_pos >= jnp.maximum(self.memory, 0)) & (key_pos <= query_pos)
        return jnp.where(seen, 0.0, NEG_SCORE)

    def comp_bias(self, shape, key_dim):
        index = self.comp_pos + lax.broadcasted_iota(jnp.int32, shape, key_dim)
        return jnp.where((index >= self.comp_low) & (index < self.comp_end), 0.0, NEG_SCORE)


SCORE_SCALE = HEAD_DIM ** (-0.5) * 1.4426950408889634


def attend_head(seq, tok_dev, head, q, kr, vr, kc, vc, out, lse, raw_bias, comp_bias):
    cols = pl.ds(pl.multiple_of(head * HEAD_DIM, HEAD_DIM), HEAD_DIM)
    def one(i, carry):
        at = Attention(seq, i, tok_dev, kr.shape[1], kc.shape[1])
        query = q[at.rows, cols]
        raw = times_transposed(query, kr[head, at.raw, :]) * SCORE_SCALE + raw_bias[i]
        comp = times_transposed(query, kc[head, at.comp, :]) * SCORE_SCALE + comp_bias[i]
        top = jnp.maximum(
            jnp.max(raw, axis=1, keepdims=True), jnp.max(comp, axis=1, keepdims=True)
        )
        raw = jnp.exp2(raw - top)
        comp = jnp.exp2(comp - top)
        total = row_sum(raw) + row_sum(comp)
        mixed = matmul(raw.astype(BF16), vr[head, at.raw, :])
        mixed = mixed + matmul(comp.astype(BF16), vc[head, at.comp, :])
        out[at.rows, cols] = mixed / total
        stat = jnp.broadcast_to(top + jnp.log2(total), (QB, QB))
        lse[head, :, at.rows] = stat.T[:8]
        return carry

    lax.fori_loop(0, tok_dev // QB, one, 0)


TAPS = [4 + 2 * RATIO + i for i in range(3)]
ARRIVAL = TAPS + [0, 1, 2, 3]
for _i in range(RATIO):
    ARRIVAL = ARRIVAL + [4 + _i, 4 + RATIO + _i]
AHEAD = 5
LAG = 5
SEMS = 8
KEPT = 4


def forward_kernel(
    panels, lines,
    slot_ref, book_ref, seg_ref, master_ref, tok_ref, cot_ref, norm_ref,
    full_ref, a_out, c_out, q_out, kr_out, vr_out, kc_out, vc_out, o_out, z_out, df_out, b_out,
    h_out, db_out, a3_out, dy_out, lse_ref, mixed_ref,
    wbuf, a_win, a3, c_win, q, kr, vr, kc, vc, o, z, df, b, h, y, db, dy_ref, slots, slots_a, slots_b,
    block, normed, raw_bias, comp_bias,
    own_sem, zs, zr, s1, r1, s2, r2, cs, cr, wsem, a_s, a_r, c_s, c_r, f_s, f_r, es, er, out_sem,
    hidden_sem,
):
    at = Place(lines)
    seq = at.seq
    seq_count = 2 * lines
    chunks = 2 * panels
    tok_dev = tok_ref.shape[0]
    comp_dev = tok_dev // 3
    raw_devs = a_win.shape[0] // tok_dev
    comp_devs = c_win.shape[0] // comp_dev
    reach = min(seq_count - 1, (2 * S + 3 * CM + tok_dev - 1) // tok_dev)
    wide = block.shape[-1]
    half_rows = block.shape[1] // 2

    def cols(g):
        return pl.ds(pl.multiple_of(g * wide, wide), wide)

    def panel_of(u):
        return jnp.where(u < 4, u % 2, u // 2)

    def rows_of(u):
        half = jnp.where(u < 4, u // 2, u % 2)
        return pl.ds(pl.multiple_of(half * half_rows, half_rows), half_rows)

    def line_place(u, line):
        return full_ref.at[panel_of(u), line // 2, line % 2, at.core, rows_of(u), cols(at.grp)]

    def line_copy(u, k):
        src = block.at[panel_of(u), rows_of(u), :]
        return remote(src, line_place(u, at.line), zs.at[u, k], zr.at[u, at.line], at.line_dev(k))

    def line_arrival(u, k):
        src, line = block.at[panel_of(u), rows_of(u), :], at.other_line(k)
        return remote(src, line_place(u, line), zs.at[u, k], zr.at[u, line], at.line_dev(k))

    def part(u, half, g):
        return full_ref.at[panel_of(u), :, half, at.core, rows_of(u), cols(g)]

    def first(u, half, g):
        device, i = (at.x_dev if half == 0 else at.y_dev), u % SEMS
        return remote(part(u, half, g), part(u, half, g), s1.at[i, half], r1.at[i, half], device)

    def second(u, half, j, g):
        device, i = (at.y_dev if half == 0 else at.x_dev), u % SEMS
        ref = part(u, half, g)
        return remote(ref, ref, s2.at[i, half, j], r2.at[i, half, j], device)

    def cross(u, half, core):
        ref, i = full_ref.at[panel_of(u), :, half, core, rows_of(u)], u % SEMS
        return remote(ref, ref, cs.at[i, half], cr.at[i, half], at.core_dev)

    def load(u):
        p = panel_of(u)
        src = full_ref.at[p, :, :, :, rows_of(u)]
        dst = wbuf.at[p % KEPT, :, :, :, rows_of(u)]
        return pltpu.make_async_copy(src, dst, wsem.at[u % SEMS])

    def start_lines(u):
        for k in range(1, lines):
            line_copy(u, k).start()

    def start_first(u):
        for k in range(1, lines):
            line_arrival(u, k).wait_recv()
        for half in (0, 1):
            first(u, half, at.grp).start()

    def start_second(u):
        for half in (0, 1):
            near = at.grp_x if half == 0 else at.grp_y
            first(u, half, near).wait_recv()
            second(u, half, 0, at.grp).start()
            second(u, half, 1, near).start()

    def start_cross(u):
        for half in (0, 1):
            second(u, half, 0, at.grp_y if half == 0 else at.grp_x).wait_recv()
            second(u, half, 1, 3 - at.grp).wait_recv()
            cross(u, half, at.core).start()

    def finish(u):
        for half in (0, 1):
            cross(u, half, 1 - at.core).wait_recv()
            first(u, half, at.grp).wait_send()
            second(u, half, 0, at.grp).wait_send()
            second(u, half, 1, at.grp_x if half == 0 else at.grp_y).wait_send()
            cross(u, half, at.core).wait_send()
        for k in range(1, lines):
            line_copy(u, k).wait_send()
        load(u).start()

    def a_rows(d):
        return a_win.at[pl.ds((raw_devs - 1 - d) * tok_dev, tok_dev), :]

    def a_copy(d, place, i, device):
        return remote(a_rows(d), a_rows(place), a_s.at[i], a_r.at[place - 1], device)

    def a_next():
        return a_copy(0, 2, 0, at.seq_dev(2))

    def a_beside():
        return a_copy(0, 1, 1, at.core_dev)

    def a_on(place):
        return a_copy(2, place, 2, at.core_dev)

    odd = at.core == 1
    even = at.core == 0
    gives_next = (seq + 2 < seq_count) & needs_raw(seq + 2, seq, tok_dev)
    gives_beside = even & needs_raw(seq + 1, seq, tok_dev)
    gives_on_far = even & needs_raw(seq + 1, seq - 2, tok_dev)
    gives_on_near = odd & needs_raw(seq - 1, seq - 2, tok_dev)

    def c_rows(reader, owner):
        place = jnp.clip(owner - comp_window_first(reader, tok_dev), 0, comp_devs - 1)
        return c_win.at[pl.ds(pl.multiple_of(place * comp_dev, comp_dev), comp_dev), :]

    def c_from(d):
        return own_c if d == 0 else c_rows(seq, seq - d)

    def c_next(d):
        dst = c_rows(seq + 2, seq - d)
        return remote(c_from(d), dst, c_s.at[d // 2], c_r.at[d // 2 + 1], at.seq_dev(2))

    def c_arrival(d):
        return remote(own_c, c_rows(seq, seq - d), c_s.at[0], c_r.at[d // 2], at.seq_dev(2))

    def c_across(d):
        other = seq + 1 - 2 * at.core
        dst = c_rows(other, seq - d)
        return remote(c_from(d), dst, f_s.at[d // 2], f_r.at[d // 2], at.core_dev)

    def c_across_arrival(d):
        other = seq + 1 - 2 * at.core
        return remote(own_c, c_rows(seq, other - d), f_s.at[0], f_r.at[d // 2], at.core_dev)

    steps_back = [d for d in range(0, reach + 1, 2)]

    def gives_c(d):
        return chain_needs_comp(seq + 2, seq - d, tok_dev, seq_count, reach - 1)

    def takes_c(d):
        return chain_needs_comp(seq, seq - d, tok_dev, seq_count, reach - 1)

    def gives_c_across(d):
        return needs_comp(seq + 1 - 2 * at.core, seq - d, tok_dev)

    def takes_c_across(d):
        return needs_comp(seq, seq + 1 - 2 * at.core - d, tok_dev)

    def pass_c(d):
        if d > 0:
            pl.when(takes_c(d))(lambda: c_arrival(d).wait_recv())
        pl.when(gives_c(d))(lambda: c_next(d).start())
        pl.when(gives_c_across(d))(lambda: c_across(d).start())

    outs = [
        (a_win, a_out), (c_win, c_out), (q, q_out), (kr, kr_out), (vr, vr_out), (kc, kc_out),
        (vc, vc_out), (o, o_out), (b, b_out), (h, h_out), (db, db_out), (a3, a3_out), (dy_ref, dy_out),
    ]

    def flush(*names):
        for i, (src, dst) in enumerate(outs):
            if any(src is name for name in names):
                pltpu.make_async_copy(src, dst, out_sem.at[i]).start()

    def flush_hidden(pair):
        return [
            pltpu.make_async_copy(src.at[pair], dst.at[pair], hidden_sem.at[i, pair])
            for i, (src, dst) in enumerate(((z, z_out), (df, df_out)))
        ]

    at.announce()
    count = master_ref.shape[0]
    halves = [pl.ds(i * half_rows, half_rows) for i in range(2)]
    arrived = (slots_a, slots_b)
    handed = [
        at.exchange(slots.at[:, halves[i]], arrived[i], es.at[i], er.at[i]) for i in range(2)
    ]

    def hand(i):
        for j in range(count):
            scale = slot_deviation(slot_ref, at.grp * count + j)
            scaled = (master_ref[j, halves[i], :] * scale).astype(BF16)
            for g in range(4):
                slots[g * count + j, halves[i], :] = scaled[:, g * wide : (g + 1) * wide]
        if i == 0:
            at.enter()
        for copy in handed[i]:
            copy.start()
        own = pl.ds(at.grp * count, count)
        arrived[i][own] = slots[own, halves[i], :]

    def take(i):
        for copy in handed[i]:
            copy.wait_recv()
        for p in range(panels):
            block[p, halves[i], :] = arrived[i][slot_ref[ARRIVAL[p]]]
        src = block.at[:, halves[i], :]
        dst = full_ref.at[:, at.line // 2, at.line % 2, at.core, halves[i], cols(at.grp)]
        pltpu.make_async_copy(src, dst, own_sem.at[i]).start()

    hand(0)
    params = norm_ref[...]
    for i in range(tok_dev // QB):
        rows = pl.ds(i * QB, QB)
        mine = norm_rows(tok_ref[rows, :].astype(F32), params, 0)
        a_win[pl.ds((raw_devs - 1) * tok_dev + i * QB, QB), :] = mine.astype(BF16)
        for c in range(HEADS):
            normed[c, rows, :] = mine[:, c * HEAD_DIM : (c + 1) * HEAD_DIM]
    pl.when(gives_next)(lambda: a_next().start())
    pl.when(gives_beside)(lambda: a_beside().start())
    hand(1)
    for d in range(1, raw_devs):
        absent = jnp.logical_not(needs_raw(seq, seq - d, tok_dev))

        @pl.when(absent)
        def _(d=d):
            a_rows(d)[...] = jnp.zeros((tok_dev, D), BF16)

    for k in range(3):
        for c in range(HEADS):
            rows = pl.ds(k, comp_dev, stride=3)
            a3[k, :, pl.ds(c * HEAD_DIM, HEAD_DIM)] = normed[c, rows, :].astype(BF16)
    book = jnp.int32(0)
    for g in range(4):
        book = jnp.where(at.grp == g, book_ref[g], book)
    valid = []
    for i in range(tok_dev // QB):
        rows = pl.ds(i * QB, QB)
        pos = seq * tok_dev + i * QB
        inside = pos % S + lax.broadcasted_iota(jnp.int32, (QB, D), 0)
        valid.append(inside < seg_ref[book, pos // S])
        dy_ref[rows, :] = jnp.where(valid[i], cot_ref[rows, :].astype(F32), 0.0).astype(BF16)
        block_at = Attention(seq, i, tok_dev, kr.shape[1], kc.shape[1])
        raw_bias[i] = block_at.raw_bias((QB, RAW_KEYS), 1)
        comp_bias[i] = block_at.comp_bias((QB, COMP_KEYS), 1)
    for i in range(comp_devs):
        owner = comp_window_first(seq, tok_dev) + i
        taken = needs_comp(seq, owner, tok_dev)
        for d in steps_back[1:]:
            taken = taken | ((owner == seq - d) & takes_c(d))

        @pl.when(jnp.logical_not(taken))
        def _(i=i):
            c_win[pl.ds(i * comp_dev, comp_dev), :] = jnp.zeros((comp_dev, D), BF16)

    take(0)
    start_lines(0)
    start_lines(1)
    take(1)
    for u in range(2, AHEAD):
        start_lines(u)
    for i in range(2):
        src = block.at[:, halves[i], :]
        dst = full_ref.at[:, at.line // 2, at.line % 2, at.core, halves[i], cols(at.grp)]
        pltpu.make_async_copy(src, dst, own_sem.at[i]).wait()

    own_c = b.at[pl.ds(0, comp_dev), :]
    tile = 8 * half_rows

    def weight(slot, col):
        return wbuf[slot, :, :, :, :, col].reshape(D, wide)

    def columns(body):
        def one(j, carry):
            body(pl.ds(pl.multiple_of(j * wide, wide), wide))
            return carry

        lax.fori_loop(0, D // wide, one, 0)

    def tap(k, slot):
        def body(col):
            part_sum = matmul(a3[k], weight(slot, col))
            if k == 0:
                y[pl.ds(0, comp_dev), col] = part_sum
            elif k == 1:
                y[pl.ds(0, comp_dev), col] += part_sum
            else:
                own_c[:, col] = (y[pl.ds(0, comp_dev), col] + part_sum).astype(BF16)

        columns(body)

    def project(dst, src, slot):
        block_rows = min(src.shape[0], tok_dev)

        def body(col):
            for i in range(src.shape[0] // block_rows):
                rows = pl.ds(i * block_rows, block_rows)
                dst[rows, col] = matmul(src[rows, :], weight(slot, col)).astype(BF16)

        columns(body)

    def project_heads(dst, src, slot, low, high):
        block_rows = min(src.shape[0], tok_dev)
        many = wide // HEAD_DIM

        def one(j, carry):
            col = pl.ds(pl.multiple_of(j * wide, wide), wide)
            for i in range(src.shape[0] // block_rows):
                rows = pl.ds(i * block_rows, block_rows)
                made = matmul(src[rows, :], weight(slot, col)).astype(BF16)
                for n in range(many):
                    dst[j * many + n, rows, :] = made[:, n * HEAD_DIM : (n + 1) * HEAD_DIM]
            return carry

        lax.fori_loop(low, high, one, 0)

    def heads(low, high):
        def one(i, carry):
            attend_head(seq, tok_dev, i, q, kr, vr, kc, vc, o, lse_ref, raw_bias, comp_bias)
            return carry

        lax.fori_loop(low, high, one, 0)

    def hidden(pair, low, high):
        up, down = (2 * pair + 7) % KEPT, (2 * pair + 8) % KEPT

        def one(i, carry):
            up_rows = wbuf[up, i].reshape(tile, D)
            down_rows = wbuf[down, i].reshape(tile, D)
            value, slope = gelu_pair(times_transposed(b[...], up_rows))
            units = pl.ds(pl.multiple_of(i * tile, tile), tile)
            z[pair, :, units] = value.astype(BF16)
            df[pair, :, units] = (times_transposed(dy_ref[...], down_rows) * slope).astype(BF16)
            return carry

        lax.fori_loop(low, high, one, 0)

    def gather_hidden(pair):
        up, down = (2 * pair + 7) % KEPT, (2 * pair + 8) % KEPT

        def body(col):
            y[:, col] += matmul(z[pair], weight(down, col))
            db[:, col] += matmul(df[pair], weight(up, col))

        columns(body)

    def work(w):
        slot = w // 2 % KEPT
        for k in range(3):
            pl.when(w == 2 + k)(lambda k=k: tap(k, k))

        @pl.when(w == 1)
        def _():
            for copy in handed[0] + handed[1]:
                copy.wait_send()
            pl.when(needs_raw(seq, seq - 2, tok_dev))(lambda: a_next().wait_recv())
            pl.when(gives_on_far)(lambda: a_on(3).start())
            pl.when(gives_on_near)(lambda: a_on(1).start())

        pl.when(w == 4)(lambda: pass_c(0))

        @pl.when(w == 5)
        def _():
            pl.when(even & needs_raw(seq, seq - 1, tok_dev))(lambda: a_on(1).wait_recv())
            pl.when(odd & needs_raw(seq, seq - 1, tok_dev))(lambda: a_beside().wait_recv())
            pl.when(needs_raw(seq, seq - 3, tok_dev))(lambda: a_on(3).wait_recv())
            pl.when(gives_next)(lambda: a_next().wait_send())
            pl.when(gives_beside)(lambda: a_beside().wait_send())
            pl.when(gives_on_far)(lambda: a_on(3).wait_send())
            pl.when(gives_on_near)(lambda: a_on(1).wait_send())
            flush(a_win, a3, dy_ref)

        @pl.when(w == 6)
        def _():
            project(q, a_win.at[pl.ds((raw_devs - 1) * tok_dev, tok_dev), :], slot)
            flush(q)

        for i, d in enumerate(steps_back[1:]):
            pl.when(w == 6 + 2 * i)(lambda d=d: pass_c(d))

        for i in range(2):
            low = i * (D // wide // 2)
            high = low + D // wide // 2
            pl.when(w == 8 + i)(lambda low=low, high=high: project_heads(kr, a_win, 4 % KEPT, low, high))
            pl.when(w == 10 + i)(lambda low=low, high=high: project_heads(vr, a_win, 5 % KEPT, low, high))

        @pl.when(w == 12)
        def _():
            flush(kr, vr)
            for d in steps_back:
                pl.when(takes_c_across(d))(lambda d=d: c_across_arrival(d).wait_recv())
            flush(c_win)
            project_heads(kc, c_win, 4 % KEPT, 0, D // wide)

        @pl.when(w == 13)
        def _():
            project_heads(vc, c_win, 5 % KEPT, 0, D // wide)
            flush(kc, vc)

        @pl.when((w >= 14) & (w < 18))
        def _():
            low = (w - 14) * (HEADS // 4)
            heads(low, low + HEADS // 4)

        @pl.when(w == 18)
        def _():
            flush(o)
            for d in steps_back:
                pl.when(gives_c(d))(lambda d=d: c_next(d).wait_send())
                pl.when(gives_c_across(d))(lambda d=d: c_across(d).wait_send())

            def body(col):
                sent = matmul(o[...].astype(BF16), weight(6 % KEPT, col))
                h[:, col] = tok_ref[:, col].astype(F32) + sent

            columns(body)
            for i in range(tok_dev // QB):
                rows = pl.ds(i * QB, QB)
                b[rows, :] = norm_rows(h[rows, :], params, 2).astype(BF16)
            y[...] = h[...]
            db[...] = jnp.zeros_like(db)
            flush(b, h)

        pair = jnp.where(w < 21, 0, jnp.where(w < 24, 1, jnp.where(w < 28, 2, 3)))
        lines_half = wbuf.shape[1] // 2
        first_turn = (w == 19) | (w == 21) | (w == 24) | (w == 28)
        second_turn = (w == 20) | (w == 22) | (w == 25) | (w == 29)
        pl.when(first_turn)(lambda: hidden(pair, 0, lines_half))

        @pl.when(second_turn)
        def _():
            hidden(pair, lines_half, 2 * lines_half)
            for copy in flush_hidden(pair):
                copy.start()
            gather_hidden(pair)

    def step(t, carry):
        pl.when(t + AHEAD < chunks)(lambda: start_lines(t + AHEAD))
        pl.when(t < 2)(lambda: start_first(t))
        pl.when((t >= 1) & (t + 1 < chunks))(lambda: start_first(t + 1))
        pl.when((t >= 1) & (t < chunks + 1))(lambda: start_second(t - 1))
        pl.when((t >= 3) & (t < chunks + 3))(lambda: start_cross(t - 3))

        pl.when((t >= LAG) & (t < chunks + LAG))(lambda: load(t - LAG).wait())
        pl.when(t >= LAG + 1)(lambda: work(t - LAG - 1))
        pl.when((t >= 4) & (t < chunks + 4))(lambda: finish(t - 4))
        return carry

    lax.fori_loop(0, chunks + LAG + 1, step, 0)
    flush(db)
    for i in range(tok_dev // QB):
        rows = pl.ds(i * QB, QB)
        mixed_ref[rows, :] = jnp.where(valid[i], y[rows, :], 0.0).astype(BF16)
    for pair in range(RATIO):
        for copy in flush_hidden(pair):
            copy.wait()
    for i, (src, dst) in enumerate(outs):
        pltpu.make_async_copy(src, dst, out_sem.at[i]).wait()


def forward(panel_slot, book_of_group, seg_valid, master, tokens, cotangent, norm_params, lines):
    panels, slot_count, rows = panel_slot.shape[0], master.shape[0], master.shape[1]
    wide = D // 4
    tok_dev = tokens.shape[0]
    raw = raw_devices(tok_dev) * tok_dev
    comp = comp_devices(tok_dev, 2 * lines) * (tok_dev // 3)
    dma = pltpu.SemaphoreType.DMA
    token, wide_token, hidden = ((tok_dev, D), BF16), ((tok_dev, D), F32), ((RATIO, tok_dev, D), BF16)
    raw_rows, comp_rows, thirds = ((raw, D), BF16), ((comp, D), BF16), ((3, tok_dev // 3, D), BF16)
    raw_heads, comp_heads = ((HEADS, raw, HEAD_DIM), BF16), ((HEADS, comp, HEAD_DIM), BF16)
    shapes = [raw_rows, comp_rows, token, raw_heads, raw_heads, comp_heads, comp_heads, wide_token]
    shapes = shapes + [hidden, hidden, token, wide_token, wide_token, thirds, token]
    scratch = [raw_rows, thirds, comp_rows, token, raw_heads, raw_heads, comp_heads, comp_heads]
    scratch = scratch + [wide_token, hidden, hidden, token, wide_token, wide_token, wide_token, token]
    scratch = [pltpu.VMEM(shape, kind) for shape, kind in scratch]
    blocks = tok_dev // QB
    any_spec, vmem = pl.BlockSpec(memory_space=pl.ANY), pl.BlockSpec(memory_space=pltpu.VMEM)
    smem = pl.BlockSpec(memory_space=pltpu.SMEM)
    return pl.pallas_call(
        functools.partial(forward_kernel, panels, lines),
        out_shape=[jax.ShapeDtypeStruct((panels, lines // 2, 2, 2, rows, D), BF16)]
        + [jax.ShapeDtypeStruct(shape, kind) for shape, kind in shapes]
        + [jax.ShapeDtypeStruct((HEADS, 8, tok_dev), F32), jax.ShapeDtypeStruct((tok_dev, D), BF16)],
        in_specs=[smem] * 3 + [vmem] * 4,
        out_specs=[any_spec] * (1 + len(shapes)) + [vmem] * 2,
        scratch_shapes=[pltpu.VMEM((KEPT, lines // 2, 2, 2, rows, D), BF16)]
        + scratch
        + [
            pltpu.VMEM((4 * slot_count, rows, wide), BF16),
            pltpu.VMEM((4 * slot_count, rows // 2, wide), BF16),
            pltpu.VMEM((4 * slot_count, rows // 2, wide), BF16),
            pltpu.VMEM((panels, rows, wide), BF16),
            pltpu.VMEM((HEADS, tok_dev, HEAD_DIM), F32),
            pltpu.VMEM((blocks, QB, RAW_KEYS), F32),
            pltpu.VMEM((blocks, QB, COMP_KEYS), F32),
            dma((2,)),
            dma((2 * panels, lines)), dma((2 * panels, lines)),
            dma((SEMS, 2)), dma((SEMS, 2)),
            dma((SEMS, 2, 2)), dma((SEMS, 2, 2)),
            dma((SEMS, 2)), dma((SEMS, 2)),
            dma((SEMS,)),
            dma((3,)), dma((3,)), dma((5,)), dma((5,)), dma((5,)), dma((5,)),
            dma((2, 3)), dma((2, 3)),
            dma((len(shapes),)),
            dma((2, RATIO)),
        ],
        compiler_params=pltpu.CompilerParams(
            collective_id=0, has_side_effects=True, vmem_limit_bytes=60 * MIB
        ),
        name="forward",
    )(panel_slot, book_of_group, seg_valid, master, tokens, cotangent, norm_params)


RETURN = [4 + RATIO + _i for _i in range(RATIO)] + [4 + _i for _i in range(RATIO)] + [3, 0, 1, 2] + TAPS
RING = 3
HELD = 5
BACK_LAG = 4


def norm_back(grad, values, params, first):
    mean = row_sum(values) * (1.0 / D)
    centered = values - mean
    scale = lax.rsqrt(row_sum(centered * centered) * (1.0 / D) + NORM_EPS)
    unit = centered * scale
    inner = grad * params[first : first + 1, :]
    back = inner - row_sum(inner) * (1.0 / D) - unit * (row_sum(inner * unit) * (1.0 / D))
    gain = jnp.sum(grad * unit, axis=0, keepdims=True)
    return back * scale, gain, jnp.sum(grad, axis=0, keepdims=True)


def attend_block_back(
    seq, tok_dev, i, cols, q, do, o, kr, vr, kc, vc, lse, lse_row, raw_bias, comp_bias,
    acc_kr, acc_vr, acc_kc, acc_vc,
):
    at = Attention(seq, i, tok_dev, kr.shape[0], kc.shape[0])
    query = q[at.rows, cols]
    grad = do[at.rows, cols]
    delta = row_sum(grad.astype(F32) * o[at.rows, cols])
    delta = jnp.broadcast_to(delta, (QB, QB)).T[0:1]
    stat = lse[lse_row, 0:1, at.rows]

    def part(k_ref, v_ref, acc_k, acc_v, keys, bias):
        k = k_ref[keys, :]
        s = times_transposed(k, query) * SCORE_SCALE + bias.astype(F32)
        p = jnp.exp2(s - stat)
        dp = times_transposed(v_ref[keys, :], grad)
        ds = (p * (dp - delta)).astype(BF16)
        acc_v[keys, :] += matmul(p.astype(BF16), grad)
        acc_k[keys, :] += matmul(ds, query)
        return contract_rows(ds, k)

    dq = part(kr, vr, acc_kr, acc_vr, at.raw, raw_bias[i])
    dq = dq + part(kc, vc, acc_kc, acc_vc, at.comp, comp_bias[i])
    q[at.rows, cols] = (dq * HEAD_DIM ** (-0.5)).astype(BF16)


def backward_kernel(
    panels, lines,
    slot_ref,
    full_ref, a_hbm, c_hbm, a3_hbm, q_hbm, kr_hbm, vr_hbm, kc_hbm, vc_hbm, o_hbm, z_hbm, df_hbm,
    b_hbm, h_hbm, db_hbm, dy_hbm, tok_hbm, lse_ref, norm_ref,
    slot_out, in_grad_out, norm_out,
    held, cross_in, first_in, second_in, line_in, out, slots, slots_in,
    opnd, lhs_t, c_win, a3, h, db, o, pair, q, kr, vr, kc, vc, acc_kr, acc_vr, acc_kc, acc_vc,
    raw_bias, comp_bias, place, scale, dkr, dvr, dkc, dvc, wbuf, dc, dc_beside, dc_chain, da_in, n_src, n_in, n_line,
    cs, cr, s1, r1, s2, r2, zs, zr, free_cross, free_first, free_second,
    lsem, osem, hsem, wsem, dbs, dbr, dcs, dcr, das, dar, ns, nr, nzs, nzr, es, er,
):
    at = Place(lines)
    seq = at.seq
    seq_count = 2 * lines
    chunks = 2 * panels
    tok_dev = q.shape[0]
    comp_dev = tok_dev // 3
    raw_devs = dkr.shape[0] // tok_dev
    comp_devs = dkc.shape[0] // comp_dev
    reach = min(seq_count - 1, (2 * S + 3 * CM + tok_dev - 1) // tok_dev)
    wide = out.shape[-1]
    half_rows = out.shape[1] // 2
    pairs = lines // 2
    params = norm_ref[...]
    raw, comp = dkr.shape[0], dkc.shape[0]

    def token_rows(i):
        return pl.ds(pl.multiple_of(i * tok_dev, tok_dev), tok_dev)

    dhb, do = pair.at[token_rows(0), :], pair.at[token_rows(1), :]

    taps = chunks - 6

    def panel_of(u):
        return jnp.where(u < taps, u // 2, panels - 3 + (u - taps) % 3)

    def half_of(u):
        return jnp.where(u < taps, u % 2, (u - taps) // 3)

    def mine(u):
        return held.at[u % HELD, :, :, at.core]

    def cross(u):
        src, i = held.at[u % HELD, :, :, 1 - at.core], u % RING
        return remote(src, cross_in.at[i], cs.at[i], cr.at[i], at.core_dev)

    def first(u, half):
        i = u % RING
        if half == 0:
            src, device = mine(u).at[:, 0, 1 - at.row], at.y_dev
        else:
            src, device = mine(u).at[:, 1, :, 1 - at.col], at.x_dev
        return remote(src, first_in.at[i, half], s1.at[i, half], r1.at[i, half], device)

    def second(u, half):
        i = u % RING
        if half == 0:
            src, device = mine(u).at[:, 0, at.row, 1 - at.col], at.x_dev
        else:
            src, device = mine(u).at[:, 1, 1 - at.row, at.col], at.y_dev
        return remote(src, second_in.at[i, half], s2.at[i, half], r2.at[i, half], device)

    def line_copy(u, k):
        line = at.other_line(k)
        src = mine(u).at[line // 2, line % 2, at.row, at.col]
        i = lines - 1 - k
        return remote(src, line_in.at[u, i], zs.at[u, k], zr.at[u, i], at.line_dev(k))

    def line_arrival(u, k):
        line = at.other_line(k)
        src = mine(u).at[line // 2, line % 2, at.row, at.col]
        return remote(src, line_in.at[u, k - 1], zs.at[u, k], zr.at[u, k - 1], at.line_dev(k))

    def give(semaphore, device):
        pl.semaphore_signal(semaphore, inc=1, device_id=device, device_id_type=MESH)

    def add(dst, src):
        dst[...] = (dst[...].astype(F32) + src[...].astype(F32)).astype(BF16)

    def start_first(u):
        cross(u).wait_recv()
        for half in (0, 1):
            for i in range(pairs):
                for g in range(4):
                    add(
                        mine(u).at[i, half, g // 2, g % 2],
                        cross_in.at[u % RING, i, half, g // 2, g % 2],
                    )
            pl.when(u >= RING)(lambda half=half: pl.semaphore_wait(free_first.at[half], 1))
            first(u, half).start()
        cross(u).wait_send()
        pl.when(u + RING < chunks)(lambda: give(free_cross, at.core_dev))

    def start_second(u):
        for half in (0, 1):
            first(u, half).wait_recv()
            for i in range(pairs):
                for j in (0, 1):
                    row, col = (at.row, j) if half == 0 else (j, at.col)
                    add(mine(u).at[i, half, row, col], first_in.at[u % RING, half, i, j])
            pl.when(u >= RING)(lambda half=half: pl.semaphore_wait(free_second.at[half], 1))
            second(u, half).start()
            first(u, half).wait_send()
            device = at.y_dev if half == 0 else at.x_dev
            pl.when(u + RING < chunks)(
                lambda half=half, device=device: give(free_first.at[half], device)
            )

    def start_lines(u):
        for half in (0, 1):
            second(u, half).wait_recv()
            for i in range(pairs):
                add(mine(u).at[i, half, at.row, at.col], second_in.at[u % RING, half, i])
            second(u, half).wait_send()
            device = at.x_dev if half == 0 else at.y_dev
            pl.when(u + RING < chunks)(
                lambda half=half, device=device: give(free_second.at[half], device)
            )
        for k in range(1, lines):
            line_copy(u, k).start()

    def finish(u):
        total = mine(u)[at.line // 2, at.line % 2, at.row, at.col].astype(F32)
        for k in range(1, lines):
            line_arrival(u, k).wait_recv()
            total = total + line_in[u, k - 1].astype(F32)
        rows = pl.ds(pl.multiple_of(half_of(u) * half_rows, half_rows), half_rows)
        out[panel_of(u), rows, :] = total.astype(BF16)
        for k in range(1, lines):
            line_copy(u, k).wait_send()

    def turn(left, first_row):
        turned = left[...].astype(BF16).T
        count = left.shape[0]
        turned = turned.reshape(2 * pairs, 2, 2, half_rows, count)
        lhs_t[:, :, :, :, pl.ds(first_row, count)] = turned

    def produce(u, *terms):
        def columns(j, carry):
            col = pl.ds(pl.multiple_of(j * wide, wide), wide)
            total = None
            for first_row, right in terms:
                count = right.shape[0]
                left = lhs_t[:, :, half_of(u), :, pl.ds(first_row, count)].reshape(D // 2, count)
                term = matmul(left, right[:, col])
                total = term if total is None else total + term
            total = total.reshape(pairs, 2, 2, half_rows, wide)
            held[u % HELD, :, :, :, j // 2, j % 2] = total.astype(BF16)
            return carry

        lax.fori_loop(0, 4, columns, 0)
        pl.when(u >= RING)(lambda: pl.semaphore_wait(free_cross, 1))
        cross(u).start()

    def left_load(p, src):
        return pltpu.make_async_copy(src.at[p % RATIO], opnd.at[token_rows(2 + p % 2), :], lsem.at[p % 2])

    def left_start(p):
        pl.when(p < RATIO)(lambda: left_load(p, z_hbm).start())
        pl.when(p >= RATIO)(lambda: left_load(p, df_hbm).start())

    early = [
        (dy_hbm, opnd.at[token_rows(0), :]), (b_hbm, opnd.at[token_rows(1), :]), (h_hbm, h),
        (db_hbm, db), (o_hbm, o), (q_hbm, q), (c_hbm, c_win), (a3_hbm, a3),
    ]

    def early_load(i):
        return pltpu.make_async_copy(early[i][0], early[i][1], osem.at[i])

    def late_load(i):
        src, dst = ((a_hbm, opnd), (tok_hbm, dhb), (h, in_grad_out))[i]
        return pltpu.make_async_copy(src, dst, osem.at[len(early) + i])

    def head_loads(i):
        refs = [(kr_hbm, kr), (vr_hbm, vr), (kc_hbm, kc), (vc_hbm, vc)]
        return [
            pltpu.make_async_copy(src.at[i], dst.at[i % 2], hsem.at[i % 2, j])
            for j, (src, dst) in enumerate(refs)
        ]

    def weight_load(panel, slot):
        return pltpu.make_async_copy(full_ref.at[panel], wbuf.at[slot], wsem.at[slot])

    def weight(slot):
        return wbuf[slot].reshape(D, D)

    other = seq + 1 - 2 * at.core

    def comp_rows(owner):
        place = jnp.clip(owner - comp_window_first(seq, tok_dev), 0, comp_devs - 1)
        return pair.at[pl.ds(pl.multiple_of(place * comp_dev, comp_dev), comp_dev), :]

    def dc_across(d):
        i = (d + 1) // 2 - at.core
        return remote(comp_rows(seq - d), dc_beside.at[i], dbs.at[d // 2], dbr.at[i], at.core_dev)

    def dc_join(d):
        i = d // 2

        @pl.when(needs_comp(other, seq - d, tok_dev))
        def _():
            remote(comp_rows(seq - d), dc_beside.at[i], dbs.at[0], dbr.at[i], at.core_dev).wait_recv()
            add(comp_rows(seq - d), dc_beside.at[i])

    def gives_back(d):
        return chain_needs_comp(seq, seq - d, tok_dev, seq_count, reach - 1)

    def takes_back(d):
        return chain_needs_comp(seq + 2, seq - d, tok_dev, seq_count, reach - 1)

    def dc_back(d):
        i = d // 2 - 1
        return remote(comp_rows(seq - d), dc_chain.at[i], dcs.at[i], dcr.at[i], at.seq_dev(-2))

    def dc_arrival(d):
        i = d // 2
        return remote(comp_rows(seq), dc_chain.at[i], dcs.at[0], dcr.at[i], at.seq_dev(-2))

    def pass_back(d):
        if d + 2 <= chain[-1]:

            @pl.when(takes_back(d))
            def _():
                dc_arrival(d).wait_recv()
                add(comp_rows(seq - d), dc_chain.at[d // 2])

        pl.when(gives_back(d))(lambda: dc_back(d).start())

    chain = [d for d in range(2, reach + 1, 2)]
    odds = [d for d in range(1, reach + 1, 2)]

    odd = at.core == 1
    even = at.core == 0

    def raw_rows(d):
        return dkr.at[token_rows(raw_devs - 1 - d), :]

    def da_copy(d, i, place, device):
        return remote(raw_rows(d), da_in.at[place], das.at[i], dar.at[place], device)

    def da_join(d):
        return da_copy(d, 0, 0, at.core_dev)

    def da_beside():
        return da_copy(1, 1, 1, at.core_dev)

    def da_back():
        return da_copy(2, 2, 2, at.seq_dev(-2))

    joins_near = even & needs_raw(seq, seq - 1, tok_dev)
    joins_far = odd & needs_raw(seq, seq - 3, tok_dev)
    joined = needs_raw(other, seq - 2, tok_dev)
    gives_beside = odd & needs_raw(seq, seq - 1, tok_dev)
    takes_beside = even & needs_raw(seq + 1, seq, tok_dev)
    gives_raw = needs_raw(seq, seq - 2, tok_dev)
    takes_raw = (seq + 2 < seq_count) & needs_raw(seq + 2, seq, tok_dev)

    def share(i):
        total = times_transposed(dkr[token_rows(i), :], weight(1))
        return total + times_transposed(dvr[token_rows(i), :], weight(2))

    def norm_copy(i):
        device = (at.core_dev, at.x_dev, at.y_dev)[i]
        return remote(n_src.at[i], n_in.at[i], ns.at[i], nr.at[i], device)

    def norm_next(i):
        norm_copy(i).wait_recv()
        n_src[i + 1] = n_src[i] + n_in[i]

    def norm_line(k):
        return remote(n_src.at[3], n_line.at[at.line], nzs.at[k], nzr.at[at.line], at.line_dev(k))

    def norm_line_arrival(k):
        line = at.other_line(k)
        return remote(n_src.at[3], n_line.at[line], nzs.at[k], nzr.at[line], at.line_dev(k))

    def second_norm_back():
        gains, shifts = [], []
        for i in range(tok_dev // QB):
            rows = pl.ds(i * QB, QB)
            back, gain, shift = norm_back(db[rows, :], h[rows, :], params, 2)
            db[rows, :] = opnd[rows, :].astype(F32) + back
            dhb[rows, :] = db[rows, :].astype(BF16)
            gains.append(gain)
            shifts.append(shift)
        n_src[0, 2:3, :] = sum(gains)
        n_src[0, 3:4, :] = sum(shifts)
        do[...] = times_transposed(dhb[...], weight(0)).astype(BF16)

    def first_norm_back():
        gains, shifts = [], []
        for i in range(tok_dev // QB):
            rows = pl.ds(i * QB, QB)
            back, gain, shift = norm_back(h[rows, :], dhb[rows, :].astype(F32), params, 0)
            h[rows, :] = db[rows, :] + back
            gains.append(gain)
            shifts.append(shift)
        n_src[0, 0:1, :] = sum(gains)
        n_src[0, 1:2, :] = sum(shifts)

    count = slot_out.shape[0]
    halves = [pl.ds(i * half_rows, half_rows) for i in range(2)]
    handed = [
        at.exchange(slots.at[:, halves[i]], slots_in.at[:, halves[i]], es.at[i], er.at[i])
        for i in range(2)
    ]

    def hand(i):
        for j in range(4 * count):
            total = out[place[j], halves[i], :].astype(F32) * scale[j]
            slots[j, halves[i], :] = total.astype(BF16)
        for copy in handed[i]:
            copy.start()
        own = pl.ds(at.grp * count, count)
        slots_in[own, halves[i], :] = slots[own, halves[i], :]

    def take(i):
        for copy in handed[i]:
            copy.wait_recv()
        for g in range(4):
            for j in range(count):
                slot_out[j, halves[i], pl.ds(g * wide, wide)] = slots_in[g * count + j, halves[i], :]

    def work(t):
        pl.when(t == taps + 3 - 1 + BACK_LAG)(lambda: hand(0))

        @pl.when(t == 0)
        def _():
            for i in range(tok_dev // QB):
                block_at = Attention(seq, i, tok_dev, raw, comp)
                raw_bias[i] = block_at.raw_bias((RAW_KEYS, QB), 0).astype(BF16)
                comp_bias[i] = block_at.comp_bias((COMP_KEYS, QB), 0).astype(BF16)
            for j in range(place.shape[0]):
                where = jnp.int32(0)
                for r in range(panels):
                    where = jnp.where(slot_ref[RETURN[r]] == j, r, where)
                place[j] = where
                scale[j] = slot_deviation(slot_ref, j)

        @pl.when(t == 1)
        def _():
            for i in range(2, 6):
                early_load(i).wait()
            weight_load(6, 0).wait()
            second_norm_back()
            weight_load(3, 0).start()

        @pl.when((t >= 2) & (t < 2 + 2 * HEADS))
        def _():
            head = t // 2 - 1
            cols = pl.ds(pl.multiple_of(head * HEAD_DIM, HEAD_DIM), HEAD_DIM)

            def blocks(low, high):
                def one(i, carry):
                    keys = [ref.at[head % 2] for ref in (kr, vr, kc, vc)]
                    attend_block_back(
                        seq, tok_dev, i, cols, q, do, o, *keys, lse_ref, head,
                        raw_bias, comp_bias, acc_kr, acc_vr, acc_kc, acc_vc,
                    )
                    return carry

                lax.fori_loop(low, high, one, 0)

            @pl.when(t % 2 == 0)
            def _():
                for copy in head_loads(head):
                    copy.wait()
                for acc in (acc_kr, acc_vr, acc_kc, acc_vc):
                    acc[...] = jnp.zeros_like(acc)

            count = tok_dev // QB
            split = count // 2
            blocks(t % 2 * split, split + t % 2 * (count - split))

            @pl.when(t % 2 == 1)
            def _():
                score = HEAD_DIM ** (-0.5)
                dkr[:, cols] = (acc_kr[...] * score).astype(BF16)
                dkc[:, cols] = (acc_kc[...] * score).astype(BF16)
                dvr[:, cols] = acc_vr[...].astype(BF16)
                dvc[:, cols] = acc_vc[...].astype(BF16)

                @pl.when(head + 2 < HEADS)
                def _():
                    for copy in head_loads(head + 2):
                        copy.start()

        @pl.when(t == 18)
        def _():
            weight_load(4, 1).wait()
            weight_load(5, 2).wait()
            half = comp // 2
            for i in range(2):
                rows = pl.ds(i * half, half)
                total = times_transposed(dkc[rows, :], weight(1))
                total = total + times_transposed(dvc[rows, :], weight(2))
                pair[rows, :] = total.astype(BF16)
            for d in odds:
                pl.when(needs_comp(seq, seq - d, tok_dev))(lambda d=d: dc_across(d).start())

        @pl.when(t == 19)
        def _():
            for d in chain:
                dc_join(d)

        for i, d in enumerate(reversed(chain)):
            pl.when(t == 19 + i)(lambda d=d: pass_back(d))

        @pl.when(t == 20)
        def _():
            weight_load(3, 0).wait()
            h[...] = times_transposed(q[...], weight(0))
            weight_load(0, 0).start()

        @pl.when(t == 24)
        def _():
            raw_rows(1)[...] = share(raw_devs - 2).astype(BF16)
            pl.when(joins_near)(lambda: da_join(1).start())
            pl.when(gives_beside)(lambda: da_beside().start())

        @pl.when((t == 25) & joins_far)
        def _():
            raw_rows(3)[...] = share(raw_devs - 4).astype(BF16)
            da_join(3).start()

        @pl.when(t == 26)
        def _():
            raw_rows(2)[...] = share(raw_devs - 3).astype(BF16)

        @pl.when(t == 23)
        def _():
            taken = takes_back(0)

            @pl.when(taken)
            def _():
                dc_arrival(0).wait_recv()
                dc[...] = dc_chain[0]

            @pl.when(jnp.logical_not(taken))
            def _():
                dc[...] = jnp.zeros_like(dc)

        @pl.when(t == 27)
        def _():
            @pl.when(joined)
            def _():
                da_join(2).wait_recv()
                add(raw_rows(2), da_in.at[0])

            pl.when(gives_raw)(lambda: da_back().start())
            h[...] += share(raw_devs - 1)
            weight_load(1, 1).start()
            weight_load(2, 2).start()

        @pl.when(t == 29)
        def _():
            for panel in range(3):
                weight_load(panel, panel).wait()
            heads_of = acc_kr.shape[0] // tok_dev
            for k in range(3):
                total = times_transposed(dc[...], weight(k))
                for c in range(HEADS):
                    acc = (acc_kr, acc_vr)[c // heads_of]
                    place = pl.ds(c % heads_of * tok_dev + k, comp_dev, stride=3)
                    acc[place, :] = total[:, c * HEAD_DIM : (c + 1) * HEAD_DIM]
            for c in range(HEADS):
                acc = (acc_kr, acc_vr)[c // heads_of]
                cols = pl.ds(c * HEAD_DIM, HEAD_DIM)
                h[:, cols] += acc[pl.ds(c % heads_of * tok_dev, tok_dev), :]
            for d in odds:
                pl.when(needs_comp(seq, seq - d, tok_dev))(lambda d=d: dc_across(d).wait_send())
            for d in chain:
                pl.when(gives_back(d))(lambda d=d: dc_back(d).wait_send())
            late_load(1).start()

        @pl.when(t == 30)
        def _():
            @pl.when(takes_raw)
            def _():
                da_back().wait_recv()
                h[...] += da_in[2].astype(F32)

            @pl.when(takes_beside)
            def _():
                da_beside().wait_recv()
                h[...] += da_in[1].astype(F32)

            pl.when(joins_near)(lambda: da_join(1).wait_send())
            pl.when(joins_far)(lambda: da_join(3).wait_send())
            pl.when(gives_beside)(lambda: da_beside().wait_send())
            pl.when(gives_raw)(lambda: da_back().wait_send())
            late_load(1).wait()
            first_norm_back()
            norm_copy(0).start()
            late_load(2).start()

        for i in range(2):

            @pl.when(t == 31 + i)
            def _(i=i):
                norm_next(i)
                norm_copy(i + 1).start()

        @pl.when(t == 33)
        def _():
            norm_next(2)
            n_line[at.line] = n_src[3]
            for k in range(1, lines):
                norm_line(k).start()

    def make(t):
        @pl.when(t < 4 * RATIO)
        def _():
            p = t // 2

            @pl.when(t % 2 == 0)
            def _():
                pl.when(p + 1 < 2 * RATIO)(lambda: left_start(p + 1))
                left_load(p, z_hbm).wait()
                pl.when(p == 0)(lambda: early_load(0).wait())
                pl.when(p == RATIO)(lambda: early_load(1).wait())
                turn(opnd.at[token_rows(2 + p % 2), :], 0)

            produce(t, (0, opnd.at[token_rows(p // RATIO), :]))
            pl.when(t == 4 * RATIO - 1)(lambda: late_load(0).start())

        base = 4 * RATIO
        pl.when(t == base)(lambda: turn(o, 0))
        pl.when(t // 2 == base // 2)(lambda: produce(t, (0, dhb)))

        @pl.when(t == base + 2)
        def _():
            late_load(0).wait()
            early_load(6).wait()
            early_load(7).wait()
            for i in (raw_devs - 1, 0, 1):
                turn(opnd.at[token_rows(i), :], i * tok_dev)

        pl.when(t // 2 == base // 2 + 1)(lambda: produce(t, (raw - tok_dev, q)))

        @pl.when(t == base + 3)
        def _():
            for i in range(2, raw_devs - 1):
                turn(opnd.at[token_rows(i), :], i * tok_dev)
            for i in range(comp // tok_dev):
                turn(c_win.at[token_rows(i), :], raw + i * tok_dev)

        pl.when(t // 2 == base // 2 + 2)(lambda: produce(t, (0, dkr), (raw, dkc)))
        pl.when(t // 2 == base // 2 + 3)(lambda: produce(t, (0, dvr), (raw, dvc)))

        @pl.when(t == taps)
        def _():
            for k in range(3):
                turn(a3.at[k], k * comp_dev)

        tap = pl.multiple_of((t - taps) % 3 * comp_dev, comp_dev)
        pl.when(t >= taps)(lambda: produce(t, (tap, dc)))

    at.announce()
    left_load(0, z_hbm).start()
    early_load(0).start()
    weight_load(6, 0).start()
    for i in range(2, 6):
        early_load(i).start()
    for i in range(2):
        for copy in head_loads(i):
            copy.start()
    for i in (1, 6, 7):
        early_load(i).start()
    for panel, slot in ((4, 1), (5, 2)):
        weight_load(panel, slot).start()
    at.enter()

    def step(t, carry):
        pl.when((t >= 1) & (t < chunks + 1))(lambda: start_first(t - 1))
        pl.when((t >= 2) & (t < chunks + 2))(lambda: start_second(t - 2))
        pl.when((t >= 3) & (t < chunks + 3))(lambda: start_lines(t - 3))
        pl.when(t >= BACK_LAG)(lambda: finish(t - BACK_LAG))
        pl.when(t < chunks)(lambda: make(t))
        work(t)
        return carry

    lax.fori_loop(0, chunks + BACK_LAG, step, 0)
    hand(1)
    for i in range(3):
        norm_copy(i).wait_send()
    for k in range(1, lines):
        norm_line_arrival(k).wait_recv()
        norm_line(k).wait_send()
    total = n_line[0]
    for i in range(1, lines):
        total = total + n_line[i]
    norm_out[...] = total
    late_load(2).wait()
    take(0)
    take(1)
    for copy in handed[0] + handed[1]:
        copy.wait_send()


def backward(panel_slot, all_slots, weights, arrays, lse, norm_params, lines):
    panels, rows = weights.shape[0], weights.shape[4]
    wide, pairs, half_rows = D // 4, lines // 2, weights.shape[4] // 2
    a_win, c_win = arrays[0], arrays[1]
    tok_dev = arrays[3].shape[0]
    raw, comp, comp_dev = a_win.shape[0], c_win.shape[0], tok_dev // 3
    raw_devs, blocks = raw // tok_dev, tok_dev // QB
    reach = min(2 * lines - 1, (2 * S + 3 * CM + tok_dev - 1) // tok_dev)
    dma = pltpu.SemaphoreType.DMA
    regular = pltpu.SemaphoreType.REGULAR
    any_spec, vmem = pl.BlockSpec(memory_space=pl.ANY), pl.BlockSpec(memory_space=pltpu.VMEM)
    smem = pl.BlockSpec(memory_space=pltpu.SMEM)

    def buffer(kind, *shape):
        return pltpu.VMEM(shape, kind)

    return pl.pallas_call(
        functools.partial(backward_kernel, panels, lines),
        out_shape=[
            jax.ShapeDtypeStruct((all_slots // 4, rows, D), BF16),
            jax.ShapeDtypeStruct((tok_dev, D), F32),
            jax.ShapeDtypeStruct((4, D), F32),
        ],
        in_specs=[smem] + [any_spec] * (1 + len(arrays)) + [vmem] * 2,
        out_specs=[vmem, any_spec, vmem],
        scratch_shapes=[
            buffer(BF16, HELD, pairs, 2, 2, 2, 2, half_rows, wide),
            buffer(BF16, RING, pairs, 2, 2, 2, half_rows, wide),
            buffer(BF16, RING, 2, pairs, 2, half_rows, wide),
            buffer(BF16, RING, 2, pairs, half_rows, wide),
            buffer(BF16, 2 * panels, lines - 1, half_rows, wide),
            buffer(BF16, panels, rows, wide),
            buffer(BF16, all_slots, rows, wide),
            buffer(BF16, all_slots, rows, wide),
            buffer(BF16, raw, D),
            buffer(BF16, 2 * pairs, 2, 2, half_rows, raw + comp),
            buffer(BF16, comp, D),
            buffer(BF16, 3, comp_dev, D),
            buffer(F32, tok_dev, D),
            buffer(F32, tok_dev, D),
            buffer(F32, tok_dev, D),
            buffer(BF16, max(comp, 2 * tok_dev), D),
            buffer(BF16, tok_dev, D),
            buffer(BF16, 2, raw, HEAD_DIM),
            buffer(BF16, 2, raw, HEAD_DIM),
            buffer(BF16, 2, comp, HEAD_DIM),
            buffer(BF16, 2, comp, HEAD_DIM),
            buffer(F32, raw, HEAD_DIM),
            buffer(F32, raw, HEAD_DIM),
            buffer(F32, comp, HEAD_DIM),
            buffer(F32, comp, HEAD_DIM),
            buffer(BF16, blocks, RAW_KEYS, QB),
            buffer(BF16, blocks, COMP_KEYS, QB),
            pltpu.SMEM((all_slots,), jnp.int32),
            pltpu.SMEM((all_slots,), F32),
            buffer(BF16, raw, D),
            buffer(BF16, raw, D),
            buffer(BF16, comp, D),
            buffer(BF16, comp, D),
            buffer(BF16, 3, pairs, 2, 2, rows, D),
            buffer(BF16, comp_dev, D),
            buffer(BF16, reach // 2 + 2, comp_dev, D),
            buffer(BF16, reach // 2 + 1, comp_dev, D),
            buffer(BF16, 3, tok_dev, D),
            buffer(F32, 4, 4, D),
            buffer(F32, 3, 4, D),
            buffer(F32, lines, 4, D),
            dma((RING,)), dma((RING,)),
            dma((RING, 2)), dma((RING, 2)),
            dma((RING, 2)), dma((RING, 2)),
            dma((2 * panels, lines)), dma((2 * panels, lines)),
            regular, regular((2,)), regular((2,)),
            dma((2,)), dma((11,)), dma((2, 4)), dma((3,)),
            dma((reach // 2 + 2,)), dma((reach // 2 + 2,)),
            dma((reach // 2 + 1,)), dma((reach // 2 + 1,)),
            dma((3,)), dma((3,)),
            dma((3,)), dma((3,)),
            dma((lines,)), dma((lines,)),
            dma((2, 3)), dma((2, 3)),
        ],
        compiler_params=pltpu.CompilerParams(
            collective_id=1, has_side_effects=True, vmem_limit_bytes=63 * MIB
        ),
        name="backward",
    )(panel_slot, weights, *arrays, lse, norm_params)


def local(
    tokens, cotangent, master, first_moment, second_moment, norm_params, norm_first, norm_second,
    seg_valid, book_of_group, panel_slot,
):
    lines = lax.axis_size("seq") // 2
    all_slots = master.shape[0] * lax.axis_size("grp")
    results = forward(
        panel_slot, book_of_group, seg_valid, master, tokens, cotangent, norm_params, lines
    )
    weights, saved, log_total, mixed = results[0], results[1:-2], results[-2], results[-1]
    a_win, c_win, q, kr, vr, kc, vc, o, z, df, b, h, db, a3, grad_out = saved
    arrays = (a_win, c_win, a3, q, kr, vr, kc, vc, o, z, df, b, h, db, grad_out, tokens)
    slot_sums, input_grad, norm_grad = backward(
        panel_slot, all_slots, weights, arrays, log_total, norm_params, lines
    )
    slot_grad = slot_sums.astype(F32)
    slot_first, slot_second, slot_weight = adam_update(
        slot_grad, first_moment, second_moment, master, SLOT_RATE
    )
    norm_first_new, norm_second_all, norm_weight = adam_update(
        norm_grad, norm_first, norm_second, norm_params, NORM_RATE
    )
    return (
        mixed, input_grad, slot_grad, slot_first, slot_second, slot_weight, norm_grad,
        norm_first_new, norm_second_all[:2], norm_second_all[2:], norm_weight,
    )


def solution(mesh):
    rows, slots, whole = P(("grp", "seq"), None), P("grp", "seq", None), P()
    return jax.shard_map(
        local,
        mesh=mesh,
        in_specs=(rows, rows, slots, slots, slots) + (whole,) * 6,
        out_specs=(rows, rows, slots, slots, slots, slots) + (whole,) * 5,
        check_vma=False,
    )
```
